32 devices in a mesh: section: 4 (over x, core), dp: 8 (over z, y).
Axes of the slice: x: 2, y: 2, z: 4, core: 2. Of those that a mesh axis runs over, the one named last changes fastest.
Arguments:
- patches: bfloat16 [32, 352, 768], P('dp'), may hold values from -6 to 6
- cotangent: bfloat16 [32, 352, 768], P('dp'), may hold values from -6 to 6
- mask_flags: int32 [32, 352], P('dp'), may hold values 0 or 1
- segments: int32 [32, 352], P('dp'), may hold values from 0 to 2, as said below
- mask_token: bfloat16 [768], replicated, may hold values from -6 to 6
- norm_gains: bfloat16 [4, 768], P('section'), may hold values from 0.5 to 1.5
- norm_shifts: bfloat16 [4, 768], P('section'), may hold values from -1.75 to 1.75
- w_first: bfloat16 [4, 768, 3072], P('section'), may hold values from -0.21875 to 0.21875
- first_bias: bfloat16 [4, 3072], P('section'), may hold values from -1.25 to 1.25
- down_half: bfloat16 [4, 1536, 768], P('section'), may hold values from -0.109375 to 0.109375
Outputs:
- boundaries: bfloat16 [4, 32, 352, 768], P('section', 'dp')
- boundary_grads: float32 [4, 32, 352, 768], P('section', 'dp')
- token_grad: float32 [768], replicated
- gain_grads: float32 [4, 768], P('section')
- shift_grads: float32 [4, 768], P('section')
- first_grads: float32 [4, 768, 3072], P('section')
- bias_grads: float32 [4, 3072], P('section')
- half_grads: float32 [4, 1536, 768], P('section')
The draws below stay inside these ranges and needn't reach their ends.
Inputs may be any that keep to these rules, and one draw needn't show every extreme that they name: `segments`: each row holds two or three whole images numbered 0, 1, 2 from its start, each of 64 to 256 patches.
All inputs are finite; a program needn't handle non-finite values. No bound on the sum of `mask_flags` on one device may be relied on, other than what follows from the above.
Results may differ from the reference program's by a relative error of at most 0.015.
Values may be sent and summed in bfloat16 or wider, within the bound.
No kernel may reach another device: no remote copies, remote signals or barrier semaphores. Data moves between devices by JAX's collectives and lax.ppermute only.
A program may use at most 192 MiB of HBM per device.

```python
import jax
import jax.numpy as jnp
from jax import lax

D = 768
HEADS = 12
HEAD_SIZE = 64
FF = 3072
SEQ = 352
IMG_LEAST = 64
IMG_MOST = 256
ROWS = 32
N_SECTION = 4


def draw_segments(key, part):
    key = jax.random.fold_in(key, 7)
    key_count, key_first, key_second = jax.random.split(key, 3)
    three_images = jax.random.randint(key_count, (ROWS,), 0, 2)
    first_three = jax.random.randint(key_first, (ROWS,), IMG_LEAST, SEQ - 2 * IMG_LEAST + 1)
    spare_bits = jax.random.randint(key_second, (ROWS,), 0, 1 << 20)
    second_three = first_three + IMG_LEAST + spare_bits % (SEQ - 2 * IMG_LEAST - first_three + 1)
    first_two = SEQ - IMG_MOST + spare_bits % (2 * IMG_MOST - SEQ + 1)
    first_cut = jnp.where(three_images == 1, first_three, first_two)
    second_cut = jnp.where(three_images == 1, second_three, SEQ)
    position = jnp.arange(SEQ)[None, :]
    return (position >= first_cut[:, None]).astype(jnp.int32) + (position >= second_cut[:, None]).astype(jnp.int32)


def place_ends(result, stream_key, low, top_value):
    longest = result.shape.index(max(result.shape))
    spots = []
    for shift in (0, 1):
        where = [jax.random.randint(jax.random.fold_in(stream_key, axis), (), 0, length) for axis, length in enumerate(result.shape)]
        where[longest] = (where[longest] + shift) % result.shape[longest]
        spots.append(tuple(where))
    return result.at[spots[0]].set(low).at[spots[1]].set(top_value)


def block_levels(key, shape, cuts, low, largest):
    level, own = 1.0, jax.random.fold_in(key, 6)
    for dim, blocks in cuts:
        draws = jnp.exp(jax.random.uniform(jax.random.fold_in(own, dim), (blocks,), jnp.float32, low / len(cuts), largest / len(cuts)))
        level = level * jnp.repeat(draws, shape[dim] // blocks).reshape([-1 if axis == dim else 1 for axis in range(len(shape))])
    return level


def normal_values(rng, dims, scale, reach, shards=(), held_as=jnp.bfloat16):
    drawn = jax.random.normal(rng, dims, jnp.float32) * scale
    if len(shards) > 0:
        drawn = block_levels(rng, dims, shards, -0.22, 0.18) * drawn
    return jnp.clip(drawn, min=-reach, max=reach).astype(held_as)


def setup_inputs(seed: int = 0) -> dict:
    key_list = jax.random.split(jax.random.key(seed), 11)
    patches = normal_values(key_list[0], (ROWS, SEQ, D), 1.0, 6.0, ((0, 8),))
    cotangent = normal_values(key_list[1], (ROWS, SEQ, D), 1.0, 6.0, ((0, 8),))
    mask_flags = place_ends((jax.random.randint(key_list[2], (ROWS, SEQ), 0, 5) < 2).astype(jnp.int32), jax.random.fold_in(key_list[2], 1), 0, 1)
    segments = draw_segments(jax.random.fold_in(key_list[10], 71), 0)
    mask_token = normal_values(key_list[4], (D,), 1.0, 6.0)
    norm_gains = jnp.clip(1.0 + 0.1 * jax.random.normal(key_list[5], (N_SECTION, D), jnp.float32), 0.5, 1.5).astype(jnp.bfloat16)
    norm_shifts = normal_values(key_list[6], (N_SECTION, D), 0.3, 1.75, ((0, 4),))
    w_first = normal_values(key_list[7], (N_SECTION, D, FF), D ** -0.5, 0.21875, ((0, 4),))
    first_bias = normal_values(key_list[8], (N_SECTION, FF), 0.2, 1.25, ((0, 4),))
    down_half = normal_values(key_list[9], (N_SECTION, 2 * D, D), FF ** -0.5, 0.109375, ((0, 4),))
    return {"patches": patches, "cotangent": cotangent, "mask_flags": mask_flags, "segments": segments, "mask_token": mask_token, "norm_gains": norm_gains, "norm_shifts": norm_shifts, "w_first": w_first, "first_bias": first_bias, "down_half": down_half}


@jax.custom_vjp
def low(v):
    return lax.optimization_barrier(v.astype(jnp.bfloat16)).astype(jnp.float32)

@jax.custom_vjp
def low_back(v):
    return v

def low_keep(v):
    return (low(v), None)

def low_pass(kept, grad):
    return (grad,)

def back_keep(v):
    return (v, None)

def back_low(kept, grad):
    return (low(grad),)
low.defvjp(low_keep, low_pass)
low_back.defvjp(back_keep, back_low)
EPSILON = 1e-06
NEGATIVE = -1000000000.0
HIGHEST = lax.Precision.HIGHEST

def layer_norm(current, gain_row, shift_row):
    average = lax.optimization_barrier(jnp.mean(current, -1, keepdims=True))
    centred = current - average
    spread = lax.optimization_barrier(jnp.mean(centred * centred, -1, keepdims=True))
    return centred * lax.rsqrt(spread + EPSILON) * gain_row + shift_row

def project(matrix, weight_block):
    return jnp.einsum('rsd,de->rse', matrix, weight_block, precision=HIGHEST)

def attend_item(packed):
    queries, key_rows, values, segment_ids = packed
    scores = jnp.einsum('qhd,khd->hqk', queries, key_rows, precision=HIGHEST) * HEAD_SIZE ** (-0.5)
    same_image = segment_ids[:, None] == segment_ids[None, :]
    scores = low_back(jnp.where(same_image[None], scores, NEGATIVE))
    row_max = lax.optimization_barrier(jnp.max(scores, -1, keepdims=True))
    raised = jnp.exp(scores - row_max)
    weights_soft = raised / lax.optimization_barrier(jnp.sum(raised, -1, keepdims=True))
    return jnp.einsum('hqk,khd->qhd', low(weights_soft), values, precision=HIGHEST)

def attention_block(current, gain_row, shift_row, first_block, bias_row, segments):
    normed = low(layer_norm(current, gain_row, shift_row))
    projected = project(normed, first_block[:, :3 * D])
    queries = low(low_back(projected[..., :D] + bias_row[:D]))
    key_rows = low(low_back(projected[..., D:2 * D]))
    values = low(low_back(projected[..., 2 * D:3 * D] + bias_row[D:2 * D]))
    row_count = current.shape[0]
    head_shape = (row_count, SEQ, HEADS, HEAD_SIZE)
    context = lax.map(jax.checkpoint(attend_item), (queries.reshape(head_shape), key_rows.reshape(head_shape), values.reshape(head_shape), segments))
    context = low(low_back(context.reshape(row_count, SEQ, D)))
    return current + project(context, first_block[:, 3 * D:]) + bias_row[2 * D:3 * D]

def mlp_block(current, gain_row, shift_row, first_block, bias_row, down_block, down_bias):
    normed = low(layer_norm(current, gain_row, shift_row))
    hidden = low_back(project(normed, first_block) + bias_row)
    active = low(jax.nn.gelu(hidden, approximate=False))
    return current + project(active, down_block) + down_bias

def reference(patches, cotangent, mask_flags, segments, mask_token, norm_gains, norm_shifts, w_first, first_bias, down_half):

    def forward(inputs, token, gains_all, shifts_all, first_all, biases_all, halves_all, probes):
        current = jnp.where(mask_flags[..., None] == 1, token, inputs)
        outputs = []
        for number in range(4):
            if number % 2 == 0:
                current = attention_block(current, gains_all[number], shifts_all[number], first_all[number], biases_all[number], segments)
            else:
                down_block = jnp.concatenate([halves_all[number - 1], halves_all[number]], 0)
                current = mlp_block(current, gains_all[number], shifts_all[number], first_all[number], biases_all[number], down_block, biases_all[number - 1, 3 * D:])
            if number < 3:
                current = current + probes[number]
            current = low(low_back(current))
            outputs.append(current)
        return jnp.stack(outputs)
    primals = tuple((argument.astype(jnp.float32) for argument in (patches, mask_token, norm_gains, norm_shifts, w_first, first_bias, down_half)))
    probes = jnp.zeros((3,) + patches.shape, jnp.float32)
    outputs, pullback = jax.vjp(forward, *primals, probes)
    seed_grad = jnp.concatenate([jnp.zeros((3,) + patches.shape, jnp.float32), cotangent.astype(jnp.float32)[None]], 0)
    grads = pullback(seed_grad)
    boundary_grads = jnp.concatenate([grads[0][None], grads[7]], 0)
    return (outputs.astype(jnp.bfloat16), boundary_grads, grads[1], grads[2], grads[3], grads[4], grads[5], grads[6])
```

```python
from functools import partial

import jax
import jax.numpy as jnp
import numpy as np
from jax import lax
from jax.experimental import pallas as pl
from jax.experimental.pallas import tpu as pltpu
from jax.sharding import PartitionSpec as P

HEADS = 12
EPSILON = 1e-06
NEGATIVE = -1000000000.0
GROUP = 256
TILE = 512
VMEM_LIMIT = 60 * 1024 * 1024
BF16 = jnp.bfloat16
F32 = jnp.float32
ANY = pl.BlockSpec(memory_space=pl.ANY)
SMEM = pl.BlockSpec(memory_space=pltpu.SMEM)
VMEM = pl.BlockSpec(memory_space=pltpu.VMEM)


def dot_nn(a, b):
    return jnp.dot(a, b, preferred_element_type=F32)


def dot_nt(a, b):
    return lax.dot_general(a, b, (((1,), (1,)), ((), ())), preferred_element_type=F32)


def dot_tn(a, b):
    return lax.dot_general(a, b, (((0,), (0,)), ((), ())), preferred_element_type=F32)


def fetch(choice, first, second, target, sem):
    @pl.when(choice)
    def _():
        pltpu.make_async_copy(first, target, sem).start()

    @pl.when(jnp.logical_not(choice))
    def _():
        pltpu.make_async_copy(second, target, sem).start()

    return pltpu.make_async_copy(first, target, sem)


def deliver(choice, source, first, second, sem):
    @pl.when(choice)
    def _():
        pltpu.make_async_copy(source, first, sem).start()

    @pl.when(jnp.logical_not(choice))
    def _():
        pltpu.make_async_copy(source, second, sem).start()

    return pltpu.make_async_copy(source, first, sem)


def start_copy(source, target, sem):
    copy = pltpu.make_async_copy(source, target, sem)
    copy.start()
    return copy


def norm_parts(x):
    centred = x - jnp.mean(x, -1, keepdims=True)
    scale = lax.rsqrt(jnp.mean(centred * centred, -1, keepdims=True) + EPSILON)
    return centred * scale, scale


def gelu_pair(hidden):
    z = jnp.abs(hidden) * 0.7071067811865476
    t = 1.0 / (1.0 + 0.3275911 * z)
    poly = ((((1.061405429 * t - 1.453152027) * t + 1.421413741) * t - 0.284496736) * t + 0.254829592) * t
    fall = jnp.exp(-z * z)
    tail = 0.5 * poly * fall
    cdf = jnp.where(hidden >= 0, 1.0 - tail, tail)
    return hidden * cdf, cdf + hidden * fall * 0.3989422804014327


def columns(index, width):
    return pl.ds(pl.multiple_of(index * width, width), width)


def head_mask(rows, head):
    lane = lax.broadcasted_iota(jnp.int32, (rows, GROUP), 1)
    return (lane >= head * 64) & (lane < head * 64 + 64)


def load_weights(core_even, first_own, first_other, half_own, half_other, w_att, w_up, w_down, sems):
    half = half_own.shape[0]
    return (
        fetch(core_even, first_own, first_other, w_att, sems.at[0]),
        fetch(core_even, first_other, first_own, w_up, sems.at[1]),
        fetch(core_even, half_own, half_other, w_down.at[pl.ds(0, half)], sems.at[2]),
        fetch(core_even, half_other, half_own, w_down.at[pl.ds(half, half)], sems.at[3]),
    )


def forward_kernel(
    place, start_row, sent_row, vec_att, vec_mlp, seg_row, seg_col, first_own, first_other, half_own, half_other,
    keep_out, send_out, y_mlp_out, x_out, mid_out, qkv_out, soft_out, ctx_out, act_out, slope_out,
    w_att, w_up, w_down, x, bias, normed, qkv, soft, ctx, mid, act, slope, y_mlp, sems,
):
    core_even = place[0] == 0
    early = place[1] == 0
    rows, width = x.shape
    groups = width // GROUP
    get_x = fetch(early, start_row, sent_row, x, sems.at[4])
    get_att, get_up, get_low, get_high = load_weights(
        core_even, first_own, first_other, half_own, half_other, w_att, w_up, w_down, sems
    )
    bias[...] = jnp.where(seg_col[...] == seg_row[...], 0.0, NEGATIVE)
    get_x.wait()
    put_x = start_copy(x, x_out, sems.at[5])
    hat, _ = norm_parts(x[...].astype(F32))
    normed[...] = (hat * vec_att[0:1] + vec_att[1:2]).astype(BF16)
    get_att.wait()

    def group_step(group, carry):
        low = normed[...]
        cols = columns(group, GROUP)
        k_cols = pl.ds(pl.multiple_of(width + group * GROUP, GROUP), GROUP)
        v_cols = pl.ds(pl.multiple_of(2 * width + group * GROUP, GROUP), GROUP)
        q = ((dot_nn(low, w_att[:, cols]) + vec_att[2:3, cols]).astype(BF16) * 0.125).astype(BF16)
        k = dot_nn(low, w_att[:, k_cols]).astype(BF16)
        v = (dot_nn(low, w_att[:, v_cols]) + vec_att[3:4, cols]).astype(BF16)
        qkv[:, cols] = q
        qkv[:, k_cols] = k
        qkv[:, v_cols] = v
        total = jnp.zeros((rows, GROUP), F32)
        for head in range(GROUP // 64):
            mask = head_mask(rows, head)
            scores = dot_nt(jnp.where(mask, q, 0), k) + bias[...]
            raised = jnp.exp(scores - jnp.max(scores, -1, keepdims=True))
            weight = (raised * (1.0 / jnp.sum(raised, -1, keepdims=True))).astype(BF16)
            soft[group * (GROUP // 64) + head] = weight
            total = total + dot_nn(weight, jnp.where(mask, v, 0))
        ctx[:, cols] = total.astype(BF16)
        return carry

    lax.fori_loop(0, groups, group_step, 0)
    put_qkv = start_copy(qkv, qkv_out, sems.at[6])
    put_soft = start_copy(soft, soft_out, sems.at[7])
    put_ctx = start_copy(ctx, ctx_out, sems.at[8])
    y = x[...].astype(F32) + dot_nn(ctx[...], w_att[:, 3 * width :]) + vec_att[4:5]
    low = y.astype(BF16)
    mid[...] = low
    put_mid = start_copy(mid, mid_out, sems.at[9])
    put_first = deliver(core_even, mid, keep_out, send_out, sems.at[10])
    hat, _ = norm_parts(low.astype(F32))
    normed[...] = (hat * vec_mlp[0:1, :width] + vec_mlp[1:2, :width]).astype(BF16)
    get_up.wait()

    def up_step(tile, carry):
        cols = columns(tile, TILE)
        hidden = dot_nn(normed[...], w_up[:, cols]) + vec_mlp_bias(vec_mlp, tile)
        active, rate = gelu_pair(hidden)
        act[:, cols] = active.astype(BF16)
        slope[:, cols] = rate.astype(BF16)
        return carry

    lax.fori_loop(0, act.shape[1] // TILE, up_step, 0)
    put_act = start_copy(act, act_out, sems.at[11])
    put_slope = start_copy(slope, slope_out, sems.at[12])
    get_low.wait()
    get_high.wait()

    def down_step(group, carry):
        cols = columns(group, GROUP)
        y_mlp[:, cols] = (
            mid[:, cols].astype(F32) + dot_nn(act[...], w_down[:, cols]) + vec_att[5:6, cols]
        ).astype(BF16)
        return carry

    lax.fori_loop(0, groups, down_step, 0)
    put_y = start_copy(y_mlp, y_mlp_out, sems.at[13])
    put_second = deliver(core_even, y_mlp, send_out, keep_out, sems.at[14])
    for put in (put_x, put_qkv, put_soft, put_ctx, put_mid, put_first, put_act, put_slope, put_y, put_second):
        put.wait()


def vec_mlp_bias(vec_mlp, tile):
    return vec_mlp[6:7, columns(tile, TILE)]


def forward_call(place, start_row, sent_row, vec_att, vec_mlp, seg_row, seg_col, weights):
    rows, width = start_row.shape
    hidden = weights[0].shape[1]
    low = lambda *shape: jax.ShapeDtypeStruct(shape, BF16)
    row = low(rows, width)
    outs = [row, row, row, row, row, low(rows, 3 * width), low(HEADS, rows, rows), row, low(rows, hidden), low(rows, hidden)]
    v = pltpu.VMEM
    return pl.pallas_call(
        forward_kernel,
        out_shape=outs,
        in_specs=[SMEM, ANY, ANY, VMEM, VMEM, VMEM, VMEM, ANY, ANY, ANY, ANY],
        out_specs=[ANY] * len(outs),
        scratch_shapes=[
            v((width, hidden), BF16), v((width, hidden), BF16), v((hidden, width), BF16),
            v((rows, width), BF16), v((rows, rows), F32), v((rows, width), BF16),
            v((rows, 3 * width), BF16), v((HEADS, rows, rows), BF16), v((rows, width), BF16), v((rows, width), BF16),
            v((rows, hidden), BF16), v((rows, hidden), BF16), v((rows, width), BF16),
            pltpu.SemaphoreType.DMA((15,)),
        ],
        compiler_params=pltpu.CompilerParams(vmem_limit_bytes=VMEM_LIMIT),
        cost_estimate=pl.CostEstimate(flops=7_000_000_000, bytes_accessed=26_000_000, transcendentals=2_500_000),
        name="row_forward",
    )(place, start_row, sent_row, vec_att, vec_mlp, seg_row, seg_col, *weights)


def backward_kernel(
    place, cot_row, back_row, vec_att, vec_mlp, mask_col, first_own, first_other, half_own, half_other,
    x_a, mid_a, qkv_a, soft_a, ctx_a, slope_a, x_b, mid_b, qkv_b, soft_b, ctx_b, slope_b,
    keep_out, send_out, grad_x_out, small_out, norm_att_out, norm_mlp_out, dqkv_out, dhid_out, gmid_out, grad_y_out,
    w_att, w_up, w_down, grad_y, x, mid, qkv, soft, ctx, slope, normed_att, normed_mlp, dqkv, dhid, gmid, gx, dn, sems,
):
    core_even = place[0] == 0
    early = place[1] == 0
    rows, width = x.shape
    groups = width // GROUP

    @pl.when(place[2] == 0)
    def _():
        small_out[...] = jnp.zeros(small_out.shape, F32)

    @pl.when(place[2] == 1)
    def _():
        get_g = fetch(early, back_row, cot_row, grad_y, sems.at[4])
        get_att, get_up, get_low, get_high = load_weights(
            core_even, first_own, first_other, half_own, half_other, w_att, w_up, w_down, sems
        )
        get_slope = fetch(early, slope_a, slope_b, slope, sems.at[5])
        get_mid = fetch(early, mid_a, mid_b, mid, sems.at[6])
        get_x = fetch(early, x_a, x_b, x, sems.at[7])
        get_qkv = fetch(early, qkv_a, qkv_b, qkv, sems.at[8])
        get_soft = fetch(early, soft_a, soft_b, soft, sems.at[9])
        get_ctx = fetch(early, ctx_a, ctx_b, ctx, sems.at[10])
        small_out[...] = jnp.zeros(small_out.shape, F32)
        get_g.wait()
        put_gy = start_copy(grad_y, grad_y_out, sems.at[11])
        get_low.wait()
        get_high.wait()
        get_slope.wait()
        small_out[5:6, :width] = jnp.sum(grad_y[...].astype(F32), 0, keepdims=True)

        def hid_step(tile, carry):
            cols = columns(tile, TILE)
            grad = dot_nt(grad_y[...], w_down[cols, :]) * slope[:, cols].astype(F32)
            low = grad.astype(BF16)
            dhid[:, cols] = low
            small_out[13:14, cols] = jnp.sum(low.astype(F32), 0, keepdims=True)
            return carry

        lax.fori_loop(0, dhid.shape[1] // TILE, hid_step, 0)
        put_dhid = start_copy(dhid, dhid_out, sems.at[12])
        get_up.wait()

        def up_back(group, carry):
            cols = columns(group, GROUP)
            dn[:, cols] = dot_nt(dhid[...], w_up[cols, :])
            return carry

        lax.fori_loop(0, groups, up_back, 0)
        get_mid.wait()
        hat, scale = norm_parts(mid[...].astype(F32))
        normed_mlp[...] = (hat * vec_mlp[0:1, :width] + vec_mlp[1:2, :width]).astype(BF16)
        put_nm = start_copy(normed_mlp, norm_mlp_out, sems.at[13])
        dnorm = dn[...]
        small_out[6:7, :width] = jnp.sum(dnorm * hat, 0, keepdims=True)
        small_out[7:8, :width] = jnp.sum(dnorm, 0, keepdims=True)
        u = dnorm * vec_mlp[0:1, :width]
        grad = grad_y[...].astype(F32) + scale * (
            u - jnp.mean(u, -1, keepdims=True) - hat * jnp.mean(u * hat, -1, keepdims=True)
        )
        low = grad.astype(BF16)
        gmid[...] = low
        put_gmid = start_copy(gmid, gmid_out, sems.at[14])
        put_first = deliver(core_even, gmid, send_out, keep_out, sems.at[15])
        small_out[4:5, :width] = jnp.sum(low.astype(F32), 0, keepdims=True)
        get_att.wait()
        get_qkv.wait()
        get_soft.wait()
        get_ctx.wait()

        def group_step(group, carry):
            cols = columns(group, GROUP)
            k_cols = pl.ds(pl.multiple_of(width + group * GROUP, GROUP), GROUP)
            v_cols = pl.ds(pl.multiple_of(2 * width + group * GROUP, GROUP), GROUP)
            dctx = dot_nt(gmid[...], w_att[cols, 3 * width :]).astype(BF16)
            q = qkv[:, cols]
            k = qkv[:, k_cols]
            v = qkv[:, v_cols]
            product = dctx.astype(F32) * ctx[:, cols].astype(F32)
            dq = jnp.zeros((rows, GROUP), F32)
            dk = jnp.zeros((rows, GROUP), F32)
            dv = jnp.zeros((rows, GROUP), F32)
            for head in range(GROUP // 64):
                mask = head_mask(rows, head)
                weight = soft[group * (GROUP // 64) + head]
                mine = jnp.where(mask, dctx, 0)
                delta = jnp.sum(jnp.where(mask, product, 0.0), -1, keepdims=True)
                ds = (weight.astype(F32) * (dot_nt(mine, v) - delta)).astype(BF16)
                dq = dq + dot_nn(ds, jnp.where(mask, k, 0))
                dk = dk + dot_tn(ds, jnp.where(mask, q, 0))
                dv = dv + dot_tn(weight, mine)
            dq_low = (dq * 0.125).astype(BF16)
            dv_low = dv.astype(BF16)
            dqkv[:, cols] = dq_low
            dqkv[:, k_cols] = dk.astype(BF16)
            dqkv[:, v_cols] = dv_low
            small_out[2:3, cols] = jnp.sum(dq_low.astype(F32), 0, keepdims=True)
            small_out[3:4, cols] = jnp.sum(dv_low.astype(F32), 0, keepdims=True)
            return carry

        lax.fori_loop(0, groups, group_step, 0)
        put_dqkv = start_copy(dqkv, dqkv_out, sems.at[16])

        def qkv_back(group, carry):
            cols = columns(group, GROUP)
            dn[:, cols] = dot_nt(dqkv[...], w_att[cols, : 3 * width])
            return carry

        lax.fori_loop(0, groups, qkv_back, 0)
        get_x.wait()
        hat, scale = norm_parts(x[...].astype(F32))
        normed_att[...] = (hat * vec_att[0:1] + vec_att[1:2]).astype(BF16)
        put_na = start_copy(normed_att, norm_att_out, sems.at[17])
        dnorm = dn[...]
        small_out[0:1, :width] = jnp.sum(dnorm * hat, 0, keepdims=True)
        small_out[1:2, :width] = jnp.sum(dnorm, 0, keepdims=True)
        u = dnorm * vec_att[0:1]
        grad = gmid[...].astype(F32) + scale * (
            u - jnp.mean(u, -1, keepdims=True) - hat * jnp.mean(u * hat, -1, keepdims=True)
        )
        small_out[12:13, :width] = jnp.sum(jnp.where(mask_col[...] == 1, grad, 0.0), 0, keepdims=True)
        gx[...] = grad.astype(BF16)
        put_gx = start_copy(gx, grad_x_out, sems.at[18])
        put_second = deliver(core_even, gx, keep_out, send_out, sems.at[19])
        for put in (put_gy, put_dhid, put_nm, put_gmid, put_first, put_dqkv, put_na, put_gx, put_second):
            put.wait()


def backward_call(place, cot_row, back_row, vec_att, vec_mlp, mask_col, weights, saved_early, saved_late):
    rows, width = cot_row.shape
    hidden = weights[0].shape[1]
    low = lambda *shape: jax.ShapeDtypeStruct(shape, BF16)
    row = low(rows, width)
    outs = [row, row, row, jax.ShapeDtypeStruct((16, hidden), F32), row, row, low(rows, 3 * width), low(rows, hidden), row, row]
    specs = [ANY] * len(outs)
    specs[3] = VMEM
    v = pltpu.VMEM
    return pl.pallas_call(
        backward_kernel,
        out_shape=outs,
        in_specs=[SMEM, ANY, ANY, VMEM, VMEM, VMEM] + [ANY] * 16,
        out_specs=specs,
        scratch_shapes=[
            v((width, hidden), BF16), v((width, hidden), BF16), v((hidden, width), BF16),
            v((rows, width), BF16), v((rows, width), BF16), v((rows, width), BF16),
            v((rows, 3 * width), BF16), v((HEADS, rows, rows), BF16), v((rows, width), BF16), v((rows, hidden), BF16),
            v((rows, width), BF16), v((rows, width), BF16), v((rows, 3 * width), BF16), v((rows, hidden), BF16),
            v((rows, width), BF16), v((rows, width), BF16), v((rows, width), F32),
            pltpu.SemaphoreType.DMA((20,)),
        ],
        compiler_params=pltpu.CompilerParams(vmem_limit_bytes=VMEM_LIMIT),
        cost_estimate=pl.CostEstimate(flops=8_000_000_000, bytes_accessed=34_000_000, transcendentals=1_000),
        name="row_backward",
    )(place, cot_row, back_row, vec_att, vec_mlp, mask_col, *weights, *saved_early, *saved_late)


def weight_kernel(count, place, *refs):
    per_row = 8
    sources = refs[: 2 * count * per_row]
    own_first, own_half, other_first, other_half = refs[2 * count * per_row : 2 * count * per_row + 4]
    (na, nm, dqkv, dhid, ctx, act, gmid, gy, na_t, nm_t, ctx_t, grad_att, grad_up, grad_low, grad_high, sems) = refs[
        2 * count * per_row + 4 :
    ]
    core_even = place[0] == 0
    early = place[1] == 0
    width = na.shape[1]
    rows = na.shape[0] // count
    hidden = act.shape[1]
    targets = (nm, dhid, act, gy, na, dqkv, ctx, gmid)
    waits = []
    for index, target in enumerate(targets):
        for row in range(count):
            waits.append(
                fetch(
                    early,
                    sources[row * per_row + index],
                    sources[(count + row) * per_row + index],
                    target.at[pl.ds(row * rows, rows)],
                    sems.at[index * count + row],
                )
            )
    for wait in waits[: 2 * count]:
        wait.wait()
    nm_t[...] = nm[...].T

    def up_step(tile, carry):
        cols = columns(tile, TILE)
        grad_up[:, cols] = dot_nn(nm_t[...], dhid[:, cols]).astype(BF16)
        return carry

    lax.fori_loop(0, hidden // TILE, up_step, 0)
    base = 8 * count
    put_up = deliver(core_even, grad_up, other_first, own_first, sems.at[base])
    for wait in waits[2 * count : 4 * count]:
        wait.wait()
    half = hidden // 2

    def down_low(tile, carry):
        cols = columns(tile, GROUP)
        grad_low[cols, :] = dot_nn(act[:, cols].T, gy[...]).astype(BF16)
        return carry

    def down_high(tile, carry):
        cols = pl.ds(pl.multiple_of(half + tile * GROUP, GROUP), GROUP)
        grad_high[columns(tile, GROUP), :] = dot_nn(act[:, cols].T, gy[...]).astype(BF16)
        return carry

    lax.fori_loop(0, half // GROUP, down_low, 0)
    put_low = deliver(core_even, grad_low, own_half, other_half, sems.at[base + 1])
    lax.fori_loop(0, half // GROUP, down_high, 0)
    put_high = deliver(core_even, grad_high, other_half, own_half, sems.at[base + 2])
    for wait in waits[4 * count :]:
        wait.wait()
    na_t[...] = na[...].T
    ctx_t[...] = ctx[...].T

    def in_step(tile, carry):
        cols = columns(tile, width)
        grad_att[:, cols] = dot_nn(na_t[...], dqkv[:, cols]).astype(BF16)
        return carry

    lax.fori_loop(0, 3, in_step, 0)
    grad_att[:, 3 * width :] = dot_nn(ctx_t[...], gmid[...]).astype(BF16)
    put_att = deliver(core_even, grad_att, own_first, other_first, sems.at[base + 3])
    for put in (put_up, put_low, put_high, put_att):
        put.wait()


def weight_call(place, early_rows, late_rows):
    count = len(early_rows)
    rows, width = early_rows[0][0].shape
    hidden = early_rows[0][1].shape[1]
    flat = [array for row in (*early_rows, *late_rows) for array in row]
    low = lambda *shape: jax.ShapeDtypeStruct(shape, BF16)
    outs = [low(width, hidden), low(hidden // 2, width), low(width, hidden), low(hidden // 2, width)]
    v = pltpu.VMEM
    all_rows = count * rows
    return pl.pallas_call(
        partial(weight_kernel, count),
        out_shape=outs,
        in_specs=[SMEM] + [ANY] * len(flat),
        out_specs=[ANY] * 4,
        scratch_shapes=[
            v((all_rows, width), BF16), v((all_rows, width), BF16), v((all_rows, 3 * width), BF16),
            v((all_rows, hidden), BF16), v((all_rows, width), BF16), v((all_rows, hidden), BF16),
            v((all_rows, width), BF16), v((all_rows, width), BF16),
            v((width, all_rows), BF16), v((width, all_rows), BF16), v((width, all_rows), BF16),
            v((width, hidden), BF16), v((width, hidden), BF16), v((hidden // 2, width), BF16), v((hidden // 2, width), BF16),
            pltpu.SemaphoreType.DMA((8 * count + 4,)),
        ],
        compiler_params=pltpu.CompilerParams(vmem_limit_bytes=VMEM_LIMIT),
        cost_estimate=pl.CostEstimate(flops=10_000_000_000, bytes_accessed=30_000_000, transcendentals=0),
        name="weight_gradients",
    )(place, *flat)


def ring_reduce(pieces, extras, axis):
    members = lax.axis_size(axis)
    order = list(range(0, members, 2)) + list(range(members - 1, 0, -2))
    place_of = np.zeros(members, np.int32)
    for position, member in enumerate(order):
        place_of[member] = position
    ahead = [(order[i], order[(i + 1) % members]) for i in range(members)]
    behind = [(b, a) for a, b in ahead]
    position = jnp.asarray(place_of)[lax.axis_index(axis)]

    rings = [(piece, extra, way) for piece, extra in zip(pieces, extras) for way in (0, 1)]

    def chunk(ring, index):
        piece, extra, way = ring
        spot = lax.rem(index + 2 * members, members)
        mine = lax.dynamic_index_in_dim(piece[way], spot, 0, keepdims=False)
        return mine.astype(F32) + lax.dynamic_index_in_dim(extra[way], spot, 0, keepdims=False).astype(F32)

    steps = [1 if ring[2] == 0 else -1 for ring in rings]
    current = [chunk(ring, position).astype(BF16) for ring in rings]
    for number in range(1, members):
        for index, ring in enumerate(rings):
            moved = lax.ppermute(current[index], axis, ahead if ring[2] == 0 else behind)
            current[index] = (moved.astype(F32) + chunk(ring, position - steps[index] * number)).astype(BF16)
    gathered = []
    for index, ring in enumerate(rings):
        blank = jnp.zeros(ring[0].shape[1:], F32)
        gathered.append(
            lax.dynamic_update_index_in_dim(
                blank, current[index].astype(F32), lax.rem(position + steps[index] + 2 * members, members), 0
            )
        )
    for number in range(1, members):
        for index, ring in enumerate(rings):
            current[index] = lax.ppermute(current[index], axis, ahead if ring[2] == 0 else behind)
            spot = lax.rem(position + steps[index] * (1 - number) + 2 * members, members)
            gathered[index] = lax.dynamic_update_index_in_dim(gathered[index], current[index].astype(F32), spot, 0)
    return [jnp.stack(gathered[2 * i : 2 * i + 2]) for i in range(len(pieces))]


def shards(
    patches, cotangent, mask_flags, segments, mask_token, norm_gains, norm_shifts, w_first, first_bias, down_half
):
    section = lax.axis_index("section")
    core = lax.rem(section, 2)
    stage = section // 2
    early = stage == 0
    swap = [(0, 1), (1, 0), (2, 3), (3, 2)]
    forth = [(0, 2), (1, 3)]
    back = [(2, 0), (3, 1)]
    row_count, rows, width = patches.shape
    hidden = w_first.shape[2]
    count = row_count // 2

    first_own, half_own = w_first[0], down_half[0]
    vec_own = jnp.concatenate([norm_gains, norm_shifts, first_bias.reshape(hidden // width, width)], 0)
    vec_other = lax.ppermute(vec_own, "section", swap)
    first_other = lax.ppermute(first_own, "section", swap)
    half_other = lax.ppermute(half_own, "section", swap)
    weights = (first_own, first_other, half_own, half_other)
    vec_att = jnp.where(core == 0, vec_own, vec_other).astype(F32)
    vec_mlp = jnp.where(core == 0, vec_other, vec_own).astype(F32)
    bias_wide = vec_mlp[2:6].reshape(1, hidden)
    vec_mlp = jnp.concatenate([jnp.pad(vec_mlp, ((0, 0), (0, hidden - width))), bias_wide], 0)

    def mine(array):
        return lax.dynamic_slice_in_dim(array, core * count, count, 0)

    my_flags = mine(mask_flags)
    starts = jnp.where(my_flags[..., None] == 1, mask_token, mine(patches))
    my_segments = mine(segments)
    my_cotangent = mine(cotangent)
    place = jnp.stack([core, stage]).astype(jnp.int32)

    def clamp(value):
        return min(max(value, 0), count - 1)

    forwards = []
    sent = starts[0]
    for slot in range(count + 1):
        seg = jnp.where(early, my_segments[clamp(slot)], my_segments[clamp(slot - 1)])
        result = forward_call(
            place, starts[clamp(slot)], sent, vec_att, vec_mlp, seg[None, :], seg[:, None], weights
        )
        forwards.append(result)
        if slot < count:
            sent = lax.ppermute(result[2], "section", forth)

    backs = []
    returned = my_cotangent[0]
    for slot in range(count + 1):
        flags = jnp.where(early, my_flags[clamp(slot - 1)], my_flags[clamp(slot)])
        active = jnp.where(early, slot >= 1, slot < count).astype(jnp.int32)
        saved = [
            [forwards[which][i] for i in (3, 4, 5, 6, 7, 9)] for which in (max(slot - 1, 0), min(slot + 1, count))
        ]
        result = backward_call(
            jnp.concatenate([place, active[None]]), my_cotangent[clamp(slot)], returned, vec_att, vec_mlp,
            flags[:, None], weights, *saved
        )
        backs.append(result)
        if slot < count:
            returned = lax.ppermute(result[2], "section", back)

    def gather_row(forward, backward):
        return (backward[5], backward[7], forward[8], backward[9], backward[4], backward[6], forward[7], backward[8])

    own_first, own_half, to_first, to_half = weight_call(
        place,
        [gather_row(forwards[row], backs[row + 1]) for row in range(count)],
        [gather_row(forwards[row + 1], backs[row]) for row in range(count)],
    )
    from_first = lax.ppermute(to_first, "section", swap)
    from_half = lax.ppermute(to_half, "section", swap)

    members = lax.axis_size("dp")
    first_shape = (2, members, width // (2 * members), hidden)
    half_shape = (2, members, half_own.shape[0] // (2 * members), width)
    grad_first, grad_half = ring_reduce(
        [own_first.reshape(first_shape), own_half.reshape(half_shape)],
        [from_first.reshape(first_shape), from_half.reshape(half_shape)],
        "dp",
    )

    small = sum(jnp.where(early, backs[row + 1][3], backs[row][3]) for row in range(count))
    small = jnp.concatenate([small[:8, :width], small[13].reshape(hidden // width, width), small[12:13, :width]], 0)
    small = jnp.where((jnp.arange(2) == stage)[:, None, None], small[None], 0.0)
    small = lax.psum(small, ("section", "dp"))
    token_grad = small[0, 12]
    here = lax.dynamic_index_in_dim(small, stage, 0, keepdims=False)
    here = lax.dynamic_slice_in_dim(here, 6 * core, 6, 0)

    def assemble(keep, send):
        received = lax.ppermute(send, "section", swap)
        return jnp.where(
            core == 0, jnp.concatenate([keep, received], 0), jnp.concatenate([received, keep], 0)
        )

    keep = jnp.stack([jnp.where(early, forwards[row][0], forwards[row + 1][0]) for row in range(count)])
    send = jnp.stack([jnp.where(early, forwards[row][1], forwards[row + 1][1]) for row in range(count)])
    finals = assemble(keep, send)
    keep = jnp.stack([jnp.where(early, backs[row + 1][0], backs[row][0]) for row in range(count)])
    send = jnp.stack([jnp.where(early, backs[row + 1][1], backs[row][1]) for row in range(count)])
    back_rows = assemble(keep, send).astype(F32)
    back_rows = jnp.where((section == 0) & (mask_flags[..., None] == 1), 0.0, back_rows)
    return (
        finals[None],
        back_rows[None],
        token_grad,
        here[0:1],
        here[1:2],
        grad_first.reshape(1, width, hidden),
        here[2:6].reshape(1, hidden),
        grad_half.reshape(1, half_own.shape[0], width),
    )


def solution(mesh):
    return jax.shard_map(
        shards,
        mesh=mesh,
        in_specs=(
            P("dp", None, None),
            P("dp", None, None),
            P("dp", None),
            P("dp", None),
            P(),
            P("section", None),
            P("section", None),
            P("section", None, None),
            P("section", None),
            P("section", None, None),
        ),
        out_specs=(
            P("section", "dp", None, None),
            P("section", "dp", None, None),
            P(),
            P("section", None),
            P("section", None),
            P("section", None, None),
            P("section", None),
            P("section", None, None),
        ),
        check_vma=False,
    )
```

```python
from functools import partial

import jax
import jax.numpy as jnp
import numpy as np
from jax import lax
from jax.experimental import pallas as pl
from jax.experimental.pallas import tpu as pltpu
from jax.sharding import PartitionSpec as P

HEADS = 12
EPSILON = 1e-06
NEGATIVE = -1000000000.0
GROUP = 256
TILE = 768
VMEM_LIMIT = 60 * 1024 * 1024
BF16 = jnp.bfloat16
F32 = jnp.float32
ANY = pl.BlockSpec(memory_space=pl.ANY)
SMEM = pl.BlockSpec(memory_space=pltpu.SMEM)
VMEM = pl.BlockSpec(memory_space=pltpu.VMEM)


def dot_nn(a, b):
    return jnp.dot(a, b, preferred_element_type=F32)


def dot_nt(a, b):
    return lax.dot_general(a, b, (((1,), (1,)), ((), ())), preferred_element_type=F32)


def dot_tn(a, b):
    return lax.dot_general(a, b, (((0,), (0,)), ((), ())), preferred_element_type=F32)


def fetch(choice, first, second, target, sem):
    @pl.when(choice)
    def _():
        pltpu.make_async_copy(first, target, sem).start()

    @pl.when(jnp.logical_not(choice))
    def _():
        pltpu.make_async_copy(second, target, sem).start()

    return pltpu.make_async_copy(first, target, sem)


def deliver(choice, source, first, second, sem):
    @pl.when(choice)
    def _():
        pltpu.make_async_copy(source, first, sem).start()

    @pl.when(jnp.logical_not(choice))
    def _():
        pltpu.make_async_copy(source, second, sem).start()

    return pltpu.make_async_copy(source, first, sem)


def start_copy(source, target, sem):
    copy = pltpu.make_async_copy(source, target, sem)
    copy.start()
    return copy


def norm_parts(x):
    centred = x - jnp.mean(x, -1, keepdims=True)
    scale = lax.rsqrt(jnp.mean(centred * centred, -1, keepdims=True) + EPSILON)
    return centred * scale, scale


def gelu_pair(hidden):
    z = jnp.abs(hidden) * 0.7071067811865476
    t = 1.0 / (1.0 + 0.3275911 * z)
    poly = ((((1.061405429 * t - 1.453152027) * t + 1.421413741) * t - 0.284496736) * t + 0.254829592) * t
    fall = jnp.exp(-z * z)
    tail = 0.5 * poly * fall
    cdf = jnp.where(hidden >= 0, 1.0 - tail, tail)
    return hidden * cdf, cdf + hidden * fall * 0.3989422804014327


def columns(index, width):
    return pl.ds(pl.multiple_of(index * width, width), width)


def head_mask(rows, head):
    lane = lax.broadcasted_iota(jnp.int32, (rows, GROUP), 1)
    return (lane >= head * 64) & (lane < head * 64 + 64)


def load_weights(core_even, first_own, first_other, half_own, half_other, w_att, w_up, w_down, sems):
    half = half_own.shape[0]
    return (
        fetch(core_even, first_own, first_other, w_att, sems.at[0]),
        fetch(core_even, first_other, first_own, w_up, sems.at[1]),
        fetch(core_even, half_own, half_other, w_down.at[pl.ds(0, half)], sems.at[2]),
        fetch(core_even, half_other, half_own, w_down.at[pl.ds(half, half)], sems.at[3]),
    )


def forward_kernel(
    place, start_row, sent_row, vec_att, vec_mlp, seg_row, seg_col, first_own, first_other, half_own, half_other,
    keep_out, send_out, y_mlp_out, x_out, mid_out, qkv_out, soft_out, ctx_out, act_out, slope_out,
    w_att, w_up, w_down, x, bias, normed, qkv, soft, ctx, mid, act, slope, y_mlp, sems,
):
    core_even = place[0] == 0
    early = place[1] == 0
    rows, width = x.shape
    groups = width // GROUP
    get_x = fetch(early, start_row, sent_row, x, sems.at[4])
    get_att, get_up, get_low, get_high = load_weights(
        core_even, first_own, first_other, half_own, half_other, w_att, w_up, w_down, sems
    )
    bias[...] = jnp.where(seg_col[...] == seg_row[...], 0.0, NEGATIVE)
    get_x.wait()
    put_x = start_copy(x, x_out, sems.at[5])
    hat, _ = norm_parts(x[...].astype(F32))
    normed[...] = (hat * vec_att[0:1] + vec_att[1:2]).astype(BF16)
    get_att.wait()

    def group_step(group, carry):
        low = normed[...]
        cols = columns(group, GROUP)
        k_cols = pl.ds(pl.multiple_of(width + group * GROUP, GROUP), GROUP)
        v_cols = pl.ds(pl.multiple_of(2 * width + group * GROUP, GROUP), GROUP)
        q = ((dot_nn(low, w_att[:, cols]) + vec_att[2:3, cols]).astype(BF16) * 0.125).astype(BF16)
        k = dot_nn(low, w_att[:, k_cols]).astype(BF16)
        v = (dot_nn(low, w_att[:, v_cols]) + vec_att[3:4, cols]).astype(BF16)
        qkv[:, cols] = q
        qkv[:, k_cols] = k
        qkv[:, v_cols] = v
        total = jnp.zeros((rows, GROUP), F32)
        for head in range(GROUP // 64):
            mask = head_mask(rows, head)
            scores = dot_nt(jnp.where(mask, q, 0), k) + bias[...]
            raised = jnp.exp(scores - jnp.max(scores, -1, keepdims=True))
            weight = (raised * (1.0 / jnp.sum(raised, -1, keepdims=True))).astype(BF16)
            soft[group * (GROUP // 64) + head] = weight
            total = total + dot_nn(weight, jnp.where(mask, v, 0))
        ctx[:, cols] = total.astype(BF16)
        return carry

    lax.fori_loop(0, groups, group_step, 0)
    put_qkv = start_copy(qkv, qkv_out, sems.at[6])
    put_soft = start_copy(soft, soft_out, sems.at[7])
    put_ctx = start_copy(ctx, ctx_out, sems.at[8])
    y = x[...].astype(F32) + dot_nn(ctx[...], w_att[:, 3 * width :]) + vec_att[4:5]
    low = y.astype(BF16)
    mid[...] = low
    put_mid = start_copy(mid, mid_out, sems.at[9])
    put_first = deliver(core_even, mid, keep_out, send_out, sems.at[10])
    hat, _ = norm_parts(low.astype(F32))
    normed[...] = (hat * vec_mlp[0:1] + vec_mlp[1:2]).astype(BF16)
    get_up.wait()

    def up_step(tile, carry):
        cols = columns(tile, TILE)
        hidden = dot_nn(normed[...], w_up[:, cols]) + vec_mlp_bias(vec_mlp, tile)
        active, rate = gelu_pair(hidden)
        act[:, cols] = active.astype(BF16)
        slope[:, cols] = rate.astype(BF16)
        return carry

    lax.fori_loop(0, act.shape[1] // TILE, up_step, 0)
    put_act = start_copy(act, act_out, sems.at[11])
    put_slope = start_copy(slope, slope_out, sems.at[12])
    get_low.wait()
    get_high.wait()

    def down_step(group, carry):
        cols = columns(group, GROUP)
        y_mlp[:, cols] = (
            mid[:, cols].astype(F32) + dot_nn(act[...], w_down[:, cols]) + vec_att[5:6, cols]
        ).astype(BF16)
        return carry

    lax.fori_loop(0, groups, down_step, 0)
    put_y = start_copy(y_mlp, y_mlp_out, sems.at[13])
    put_second = deliver(core_even, y_mlp, send_out, keep_out, sems.at[14])
    for put in (put_x, put_qkv, put_soft, put_ctx, put_mid, put_first, put_act, put_slope, put_y, put_second):
        put.wait()


def vec_mlp_bias(vec_mlp, tile):
    return vec_mlp[pl.ds(2 + tile, 1)]


def forward_call(place, start_row, sent_row, vec_att, vec_mlp, seg_row, seg_col, weights):
    rows, width = start_row.shape
    hidden = weights[0].shape[1]
    low = lambda *shape: jax.ShapeDtypeStruct(shape, BF16)
    row = low(rows, width)
    outs = [row, row, row, row, row, low(rows, 3 * width), low(HEADS, rows, rows), row, low(rows, hidden), low(rows, hidden)]
    v = pltpu.VMEM
    return pl.pallas_call(
        forward_kernel,
        out_shape=outs,
        in_specs=[SMEM, ANY, ANY, VMEM, VMEM, VMEM, VMEM, ANY, ANY, ANY, ANY],
        out_specs=[ANY] * len(outs),
        scratch_shapes=[
            v((width, hidden), BF16), v((width, hidden), BF16), v((hidden, width), BF16),
            v((rows, width), BF16), v((rows, rows), F32), v((rows, width), BF16),
            v((rows, 3 * width), BF16), v((HEADS, rows, rows), BF16), v((rows, width), BF16), v((rows, width), BF16),
            v((rows, hidden), BF16), v((rows, hidden), BF16), v((rows, width), BF16),
            pltpu.SemaphoreType.DMA((15,)),
        ],
        compiler_params=pltpu.CompilerParams(vmem_limit_bytes=VMEM_LIMIT),
        cost_estimate=pl.CostEstimate(flops=7_000_000_000, bytes_accessed=26_000_000, transcendentals=2_500_000),
        name="row_forward",
    )(place, start_row, sent_row, vec_att, vec_mlp, seg_row, seg_col, *weights)


def backward_kernel(
    place, cot_row, back_row, vec_att, vec_mlp, mask_col, first_own, first_other, half_own, half_other,
    x_a, mid_a, qkv_a, soft_a, ctx_a, slope_a, x_b, mid_b, qkv_b, soft_b, ctx_b, slope_b,
    keep_out, send_out, grad_x_out, small_out, norm_att_out, norm_mlp_out, dqkv_out, dhid_out, gmid_out, grad_y_out,
    w_att, w_up, w_down, grad_y, x, mid, qkv, soft, ctx, slope, normed_att, normed_mlp, dqkv, dhid, gmid, gx, dn, sems,
):
    core_even = place[0] == 0
    early = place[1] == 0
    rows, width = x.shape
    groups = width // GROUP

    @pl.when(place[2] == 0)
    def _():
        small_out[...] = jnp.zeros(small_out.shape, F32)

    @pl.when(place[2] == 1)
    def _():
        get_g = fetch(early, back_row, cot_row, grad_y, sems.at[4])
        get_att, get_up, get_low, get_high = load_weights(
            core_even, first_own, first_other, half_own, half_other, w_att, w_up, w_down, sems
        )
        get_slope = fetch(early, slope_a, slope_b, slope, sems.at[5])
        get_mid = fetch(early, mid_a, mid_b, mid, sems.at[6])
        get_x = fetch(early, x_a, x_b, x, sems.at[7])
        get_qkv = fetch(early, qkv_a, qkv_b, qkv, sems.at[8])
        get_soft = fetch(early, soft_a, soft_b, soft, sems.at[9])
        get_ctx = fetch(early, ctx_a, ctx_b, ctx, sems.at[10])
        small_out[...] = jnp.zeros(small_out.shape, F32)
        get_g.wait()
        put_gy = start_copy(grad_y, grad_y_out, sems.at[11])
        get_low.wait()
        get_high.wait()
        get_slope.wait()
        small_out[5:6] = jnp.sum(grad_y[...].astype(F32), 0, keepdims=True)

        def hid_step(tile, carry):
            cols = columns(tile, TILE)
            grad = dot_nt(grad_y[...], w_down[cols, :]) * slope[:, cols].astype(F32)
            low = grad.astype(BF16)
            dhid[:, cols] = low
            small_out[pl.ds(10 + tile, 1)] = jnp.sum(low.astype(F32), 0, keepdims=True)
            return carry

        lax.fori_loop(0, dhid.shape[1] // TILE, hid_step, 0)
        put_dhid = start_copy(dhid, dhid_out, sems.at[12])
        get_up.wait()

        def up_back(group, carry):
            cols = columns(group, GROUP)
            dn[:, cols] = dot_nt(dhid[...], w_up[cols, :])
            return carry

        lax.fori_loop(0, groups, up_back, 0)
        get_mid.wait()
        hat, scale = norm_parts(mid[...].astype(F32))
        normed_mlp[...] = (hat * vec_mlp[0:1] + vec_mlp[1:2]).astype(BF16)
        put_nm = start_copy(normed_mlp, norm_mlp_out, sems.at[13])
        dnorm = dn[...]
        small_out[8:9] = jnp.sum(dnorm * hat, 0, keepdims=True)
        small_out[9:10] = jnp.sum(dnorm, 0, keepdims=True)
        u = dnorm * vec_mlp[0:1]
        grad = grad_y[...].astype(F32) + scale * (
            u - jnp.mean(u, -1, keepdims=True) - hat * jnp.mean(u * hat, -1, keepdims=True)
        )
        low = grad.astype(BF16)
        gmid[...] = low
        put_gmid = start_copy(gmid, gmid_out, sems.at[14])
        put_first = deliver(core_even, gmid, send_out, keep_out, sems.at[15])
        small_out[4:5] = jnp.sum(low.astype(F32), 0, keepdims=True)
        get_att.wait()
        get_qkv.wait()
        get_soft.wait()
        get_ctx.wait()

        def group_step(group, carry):
            cols = columns(group, GROUP)
            k_cols = pl.ds(pl.multiple_of(width + group * GROUP, GROUP), GROUP)
            v_cols = pl.ds(pl.multiple_of(2 * width + group * GROUP, GROUP), GROUP)
            dctx = dot_nt(gmid[...], w_att[cols, 3 * width :]).astype(BF16)
            q = qkv[:, cols]
            k = qkv[:, k_cols]
            v = qkv[:, v_cols]
            product = dctx.astype(F32) * ctx[:, cols].astype(F32)
            dq = jnp.zeros((rows, GROUP), F32)
            dk = jnp.zeros((rows, GROUP), F32)
            dv = jnp.zeros((rows, GROUP), F32)
            for head in range(GROUP // 64):
                mask = head_mask(rows, head)
                weight = soft[group * (GROUP // 64) + head]
                mine = jnp.where(mask, dctx, 0)
                delta = jnp.sum(jnp.where(mask, product, 0.0), -1, keepdims=True)
                ds = (weight.astype(F32) * (dot_nt(mine, v) - delta)).astype(BF16)
                dq = dq + dot_nn(ds, jnp.where(mask, k, 0))
                dk = dk + dot_tn(ds, jnp.where(mask, q, 0))
                dv = dv + dot_tn(weight, mine)
            dq_low = (dq * 0.125).astype(BF16)
            dv_low = dv.astype(BF16)
            dqkv[:, cols] = dq_low
            dqkv[:, k_cols] = dk.astype(BF16)
            dqkv[:, v_cols] = dv_low
            small_out[2:3, cols] = jnp.sum(dq_low.astype(F32), 0, keepdims=True)
            small_out[3:4, cols] = jnp.sum(dv_low.astype(F32), 0, keepdims=True)
            return carry

        lax.fori_loop(0, groups, group_step, 0)
        put_dqkv = start_copy(dqkv, dqkv_out, sems.at[16])

        def qkv_back(group, carry):
            cols = columns(group, GROUP)
            dn[:, cols] = dot_nt(dqkv[...], w_att[cols, : 3 * width])
            return carry

        lax.fori_loop(0, groups, qkv_back, 0)
        get_x.wait()
        hat, scale = norm_parts(x[...].astype(F32))
        normed_att[...] = (hat * vec_att[0:1] + vec_att[1:2]).astype(BF16)
        put_na = start_copy(normed_att, norm_att_out, sems.at[17])
        dnorm = dn[...]
        small_out[0:1] = jnp.sum(dnorm * hat, 0, keepdims=True)
        small_out[1:2] = jnp.sum(dnorm, 0, keepdims=True)
        u = dnorm * vec_att[0:1]
        grad = gmid[...].astype(F32) + scale * (
            u - jnp.mean(u, -1, keepdims=True) - hat * jnp.mean(u * hat, -1, keepdims=True)
        )
        token = jnp.sum(jnp.where(mask_col[...] == 1, grad, 0.0), 0, keepdims=True)
        small_out[6:7] = token
        small_out[14:15] = token
        gx[...] = grad.astype(BF16)
        put_gx = start_copy(gx, grad_x_out, sems.at[18])
        put_second = deliver(core_even, gx, keep_out, send_out, sems.at[19])
        for put in (put_gy, put_dhid, put_nm, put_gmid, put_first, put_dqkv, put_na, put_gx, put_second):
            put.wait()


def backward_call(place, cot_row, back_row, vec_att, vec_mlp, mask_col, weights, saved_early, saved_late):
    rows, width = cot_row.shape
    hidden = weights[0].shape[1]
    low = lambda *shape: jax.ShapeDtypeStruct(shape, BF16)
    row = low(rows, width)
    outs = [row, row, row, jax.ShapeDtypeStruct((16, width), F32), row, row, low(rows, 3 * width), low(rows, hidden), row, row]
    specs = [ANY] * len(outs)
    specs[3] = VMEM
    v = pltpu.VMEM
    return pl.pallas_call(
        backward_kernel,
        out_shape=outs,
        in_specs=[SMEM, ANY, ANY, VMEM, VMEM, VMEM] + [ANY] * 16,
        out_specs=specs,
        scratch_shapes=[
            v((width, hidden), BF16), v((width, hidden), BF16), v((hidden, width), BF16),
            v((rows, width), BF16), v((rows, width), BF16), v((rows, width), BF16),
            v((rows, 3 * width), BF16), v((HEADS, rows, rows), BF16), v((rows, width), BF16), v((rows, hidden), BF16),
            v((rows, width), BF16), v((rows, width), BF16), v((rows, 3 * width), BF16), v((rows, hidden), BF16),
            v((rows, width), BF16), v((rows, width), BF16), v((rows, width), F32),
            pltpu.SemaphoreType.DMA((20,)),
        ],
        compiler_params=pltpu.CompilerParams(vmem_limit_bytes=VMEM_LIMIT),
        cost_estimate=pl.CostEstimate(flops=8_000_000_000, bytes_accessed=34_000_000, transcendentals=1_000),
        name="row_backward",
    )(place, cot_row, back_row, vec_att, vec_mlp, mask_col, *weights, *saved_early, *saved_late)


def weight_kernel(count, place, *refs):
    per_row = 8
    sources = refs[: 2 * count * per_row]
    outs = refs[2 * count * per_row : 2 * count * per_row + 8]
    own, other = outs[:4], outs[4:]
    (na, nm, dqkv, dhid, ctx, act, gmid, gy, na_t, nm_t, ctx_t, grad_att, grad_up, grad_down, sems) = refs[
        2 * count * per_row + 8 :
    ]
    core_even = place[0] == 0
    early = place[1] == 0
    width = na.shape[1]
    rows = na.shape[0] // count
    hidden = act.shape[1]
    quarter = hidden // 8
    targets = (nm, dhid, act, gy, na, dqkv, ctx, gmid)
    waits = []
    for index, target in enumerate(targets):
        for row in range(count):
            waits.append(
                fetch(
                    early,
                    sources[row * per_row + index],
                    sources[(count + row) * per_row + index],
                    target.at[pl.ds(row * rows, rows)],
                    sems.at[index * count + row],
                )
            )
    for wait in waits[: 2 * count]:
        wait.wait()
    nm_t[...] = nm[...].T
    base = 8 * count
    puts = []

    def up_step(tile, carry):
        cols = columns(tile, width)
        grad_up[tile] = dot_nn(nm_t[...], dhid[:, cols]).astype(BF16)
        return carry

    lax.fori_loop(0, 4, up_step, 0)
    for part in range(4):
        puts.append(
            deliver(
                core_even,
                grad_up.at[part],
                other[part].at[pl.ds(0, width)],
                own[part].at[pl.ds(0, width)],
                sems.at[base + part],
            )
        )
    for wait in waits[2 * count : 4 * count]:
        wait.wait()

    def down_step(tile, carry):
        cols = columns(tile, quarter)
        grad_down[tile] = dot_nn(act[:, cols].T, gy[...]).astype(BF16)
        return carry

    lax.fori_loop(0, 8, down_step, 0)
    for part in range(4):
        spot = pl.ds(width, quarter)
        puts.append(deliver(core_even, grad_down.at[part], own[part].at[spot], other[part].at[spot], sems.at[base + 4 + part]))
        puts.append(
            deliver(core_even, grad_down.at[4 + part], other[part].at[spot], own[part].at[spot], sems.at[base + 8 + part])
        )
    for wait in waits[4 * count :]:
        wait.wait()
    na_t[...] = na[...].T
    ctx_t[...] = ctx[...].T

    def in_step(tile, carry):
        cols = columns(tile, width)
        grad_att[tile] = dot_nn(na_t[...], dqkv[:, cols]).astype(BF16)
        return carry

    lax.fori_loop(0, 3, in_step, 0)
    grad_att[3] = dot_nn(ctx_t[...], gmid[...]).astype(BF16)
    for part in range(4):
        spot = pl.ds(0, width)
        puts.append(deliver(core_even, grad_att.at[part], own[part].at[spot], other[part].at[spot], sems.at[base + 12 + part]))
    for put in puts:
        put.wait()


def weight_call(place, early_rows, late_rows):
    count = len(early_rows)
    rows, width = early_rows[0][0].shape
    hidden = early_rows[0][1].shape[1]
    flat = [array for row in (*early_rows, *late_rows) for array in row]
    low = lambda *shape: jax.ShapeDtypeStruct(shape, BF16)
    outs = [low(width + hidden // 8, width)] * 8
    v = pltpu.VMEM
    all_rows = count * rows
    result = pl.pallas_call(
        partial(weight_kernel, count),
        out_shape=outs,
        in_specs=[SMEM] + [ANY] * len(flat),
        out_specs=[ANY] * 8,
        scratch_shapes=[
            v((all_rows, width), BF16), v((all_rows, width), BF16), v((all_rows, 3 * width), BF16),
            v((all_rows, hidden), BF16), v((all_rows, width), BF16), v((all_rows, hidden), BF16),
            v((all_rows, width), BF16), v((all_rows, width), BF16),
            v((width, all_rows), BF16), v((width, all_rows), BF16), v((width, all_rows), BF16),
            v((4, width, width), BF16), v((4, width, width), BF16), v((8, hidden // 8, width), BF16),
            pltpu.SemaphoreType.DMA((8 * count + 16,)),
        ],
        compiler_params=pltpu.CompilerParams(vmem_limit_bytes=VMEM_LIMIT),
        cost_estimate=pl.CostEstimate(flops=10_000_000_000, bytes_accessed=30_000_000, transcendentals=0),
        name="weight_gradients",
    )(place, *flat)
    return result[:4], result[4:]


def doubling_sum(value, axis):
    members = lax.axis_size(axis)
    if members & (members - 1):
        return lax.psum(value, axis)
    distance = 1
    while distance < members:
        value = value + lax.ppermute(value, axis, [(i, i ^ distance) for i in range(members)])
        distance *= 2
    return value


def ring_reduce(own, extra, axis):
    members = lax.axis_size(axis)
    order = list(range(0, members, 2)) + list(range(members - 1, 0, -2))
    place_of = np.zeros(members, np.int32)
    for position, member in enumerate(order):
        place_of[member] = position
    ahead = [(order[i], order[(i + 1) % members]) for i in range(members)]
    behind = [(b, a) for a, b in ahead]
    position = jnp.asarray(place_of)[lax.axis_index(axis)]
    parts = len(own)
    width = own[0].shape[1]
    tall, short = width // members, (own[0].shape[0] - width) // members

    def spot(index):
        return lax.rem(index + 2 * members, members)

    def piece(array, index):
        return jnp.concatenate(
            [
                lax.dynamic_slice_in_dim(array, index * tall, tall, 0),
                lax.dynamic_slice_in_dim(array, width + index * short, short, 0),
            ],
            0,
        ).astype(F32)

    def chunk(part, index):
        return piece(own[part], index) + piece(extra[part], index)

    def shift(part, value):
        return lax.ppermute(value, axis, ahead if part % 2 == 0 else behind)

    steps = [1 - 2 * (part % 2) for part in range(parts)]
    current = [chunk(part, position).astype(BF16) for part in range(parts)]

    def reduce_step(number, current):
        moved = [shift(part, current[part]) for part in range(parts)]
        return [
            (moved[part].astype(F32) + chunk(part, spot(position - steps[part] * number))).astype(BF16)
            for part in range(parts)
        ]

    def place_chunks(number, current, matrix, half):
        for part in range(parts):
            index = spot(position + steps[part] * (1 - number))
            wide = current[part].astype(F32)
            matrix = lax.dynamic_update_slice(matrix, wide[:tall], (index * tall, part * width))
            half = lax.dynamic_update_slice(half, wide[tall:], ((part * members + index) * short, 0))
        return matrix, half

    def gather_step(number, carry):
        current, matrix, half = carry
        current = [shift(part, current[part]) for part in range(parts)]
        return (current, *place_chunks(number, current, matrix, half))

    def repeat(step, carry):
        if members > 8:
            return lax.fori_loop(1, members, step, carry)
        for number in range(1, members):
            carry = step(number, carry)
        return carry

    current = repeat(reduce_step, current)
    matrix = jnp.zeros((width, parts * width), F32)
    half = jnp.zeros((parts * short * members, width), F32)
    _, matrix, half = repeat(gather_step, (current, *place_chunks(0, current, matrix, half)))
    return matrix, half


def shards(
    patches, cotangent, mask_flags, segments, mask_token, norm_gains, norm_shifts, w_first, first_bias, down_half
):
    section = lax.axis_index("section")
    core = lax.rem(section, 2)
    stage = section // 2
    early = stage == 0
    swap = [(0, 1), (1, 0), (2, 3), (3, 2)]
    forth = [(0, 2), (1, 3)]
    back = [(2, 0), (3, 1)]
    row_count, rows, width = patches.shape
    hidden = w_first.shape[2]
    count = row_count // 2

    first_own, half_own = w_first[0], down_half[0]
    vec_own = jnp.concatenate([norm_gains, norm_shifts, first_bias.reshape(hidden // width, width)], 0)
    vec_other = lax.ppermute(vec_own, "section", swap)
    first_other = lax.ppermute(first_own, "section", swap)
    half_other = lax.ppermute(half_own, "section", swap)
    weights = (first_own, first_other, half_own, half_other)
    vec_att = jnp.where(core == 0, vec_own, vec_other).astype(F32)
    vec_mlp = jnp.where(core == 0, vec_other, vec_own).astype(F32)

    def mine(array):
        return lax.dynamic_slice_in_dim(array, core * count, count, 0)

    my_flags = mine(mask_flags)
    starts = jnp.where(my_flags[..., None] == 1, mask_token, mine(patches))
    my_segments = mine(segments)
    my_cotangent = mine(cotangent)
    place = jnp.stack([core, stage]).astype(jnp.int32)

    def clamp(value):
        return min(max(value, 0), count - 1)

    forwards = []
    sent = starts[0]
    for slot in range(count + 1):
        seg = jnp.where(early, my_segments[clamp(slot)], my_segments[clamp(slot - 1)])
        result = forward_call(
            place, starts[clamp(slot)], sent, vec_att, vec_mlp, seg[None, :], seg[:, None], weights
        )
        forwards.append(result)
        if slot < count:
            sent = lax.ppermute(result[2], "section", forth)

    backs = []
    returned = my_cotangent[0]
    for slot in range(count + 1):
        flags = jnp.where(early, my_flags[clamp(slot - 1)], my_flags[clamp(slot)])
        active = jnp.where(early, slot >= 1, slot < count).astype(jnp.int32)
        saved = [
            [forwards[which][i] for i in (3, 4, 5, 6, 7, 9)] for which in (max(slot - 1, 0), min(slot + 1, count))
        ]
        result = backward_call(
            jnp.concatenate([place, active[None]]), my_cotangent[clamp(slot)], returned, vec_att, vec_mlp,
            flags[:, None], weights, *saved
        )
        backs.append(result)
        if slot < count:
            returned = lax.ppermute(result[2], "section", back)

    def gather_row(forward, backward):
        return (backward[5], backward[7], forward[8], backward[9], backward[4], backward[6], forward[7], backward[8])

    small = sum(jnp.where(early, backs[row + 1][3], backs[row][3]) for row in range(count))
    small = lax.dynamic_slice_in_dim(small, 8 * core, 8, 0) + lax.ppermute(
        lax.dynamic_slice_in_dim(small, 8 * (1 - core), 8, 0), "section", swap
    )
    small = doubling_sum(small, "dp")
    token_grad = jnp.where(early, small[6], lax.ppermute(small[6], "section", forth))

    own, other = weight_call(
        place,
        [gather_row(forwards[row], backs[row + 1]) for row in range(count)],
        [gather_row(forwards[row + 1], backs[row]) for row in range(count)],
    )
    grad_first, grad_half = ring_reduce(own, [lax.ppermute(array, "section", swap) for array in other], "dp")

    def assemble(keep, send):
        received = lax.ppermute(send, "section", swap)
        return jnp.where(
            core == 0, jnp.concatenate([keep, received], 0), jnp.concatenate([received, keep], 0)
        )

    keep = jnp.stack([jnp.where(early, forwards[row][0], forwards[row + 1][0]) for row in range(count)])
    send = jnp.stack([jnp.where(early, forwards[row][1], forwards[row + 1][1]) for row in range(count)])
    finals = assemble(keep, send)
    keep = jnp.stack([jnp.where(early, backs[row + 1][0], backs[row][0]) for row in range(count)])
    send = jnp.stack([jnp.where(early, backs[row + 1][1], backs[row][1]) for row in range(count)])
    back_rows = assemble(keep, send).astype(F32)
    back_rows = jnp.where((section == 0) & (mask_flags[..., None] == 1), 0.0, back_rows)
    return (
        finals[None],
        back_rows[None],
        token_grad,
        small[0:1],
        small[1:2],
        grad_first[None],
        small[2:6].reshape(1, hidden),
        grad_half[None],
    )


def solution(mesh):
    return jax.shard_map(
        shards,
        mesh=mesh,
        in_specs=(
            P("dp", None, None),
            P("dp", None, None),
            P("dp", None),
            P("dp", None),
            P(),
            P("section", None),
            P("section", None),
            P("section", None, None),
            P("section", None),
            P("section", None, None),
        ),
        out_specs=(
            P("section", "dp", None, None),
            P("section", "dp", None, None),
            P(),
            P("section", None),
            P("section", None),
            P("section", None, None),
            P("section", None),
            P("section", None, None),
        ),
        check_vma=False,
    )
```

```python
from functools import partial

import jax
import jax.numpy as jnp
import numpy as np
from jax import lax
from jax.experimental import pallas as pl
from jax.experimental.pallas import tpu as pltpu
from jax.sharding import PartitionSpec as P

HEADS = 12
EPSILON = 1e-06
NEGATIVE = -1000000000.0
GROUP = 256
TILE = 768
VMEM_LIMIT = 60 * 1024 * 1024
BF16 = jnp.bfloat16
F32 = jnp.float32
ANY = pl.BlockSpec(memory_space=pl.ANY)
SMEM = pl.BlockSpec(memory_space=pltpu.SMEM)
VMEM = pl.BlockSpec(memory_space=pltpu.VMEM)


def dot_nn(a, b):
    return jnp.dot(a, b, preferred_element_type=F32)


def dot_nt(a, b):
    return lax.dot_general(a, b, (((1,), (1,)), ((), ())), preferred_element_type=F32)


def dot_tn(a, b):
    return lax.dot_general(a, b, (((0,), (0,)), ((), ())), preferred_element_type=F32)


def fetch(choice, first, second, target, sem):
    @pl.when(choice)
    def _():
        pltpu.make_async_copy(first, target, sem).start()

    @pl.when(jnp.logical_not(choice))
    def _():
        pltpu.make_async_copy(second, target, sem).start()

    return pltpu.make_async_copy(first, target, sem)


def deliver(choice, source, first, second, sem):
    @pl.when(choice)
    def _():
        pltpu.make_async_copy(source, first, sem).start()

    @pl.when(jnp.logical_not(choice))
    def _():
        pltpu.make_async_copy(source, second, sem).start()

    return pltpu.make_async_copy(source, first, sem)


def start_copy(source, target, sem):
    copy = pltpu.make_async_copy(source, target, sem)
    copy.start()
    return copy


def settle(place, *copies):
    @pl.when(place[0] >= 0)
    def _():
        for copy in copies:
            copy.wait()


def norm_parts(x):
    centred = x - jnp.mean(x, -1, keepdims=True)
    scale = lax.rsqrt(jnp.mean(centred * centred, -1, keepdims=True) + EPSILON)
    return centred * scale, scale


def gelu_pair(hidden):
    base = 1.0 + 0.23164189 * jnp.abs(hidden)
    t = pl.reciprocal(base, approx=True)
    t = t * (2.0 - base * t)
    poly = ((((0.5307027145 * t - 0.7265760135) * t + 0.7107068705) * t - 0.142248368) * t + 0.127414796) * t
    fall = jnp.exp2(hidden * hidden * -0.7213475204444817)
    tail = poly * fall
    cdf = jnp.where(hidden >= 0, 1.0 - tail, tail)
    return hidden * cdf, cdf + hidden * fall * 0.3989422804014327


def columns(index, width):
    return pl.ds(pl.multiple_of(index * width, width), width)


def head_mask(rows, head):
    lane = lax.broadcasted_iota(jnp.int32, (rows, GROUP), 1)
    return (lane >= head * 64) & (lane < head * 64 + 64)


def load_down(core_even, half_own, half_other, w_down, sems):
    half = half_own.shape[0]
    low = fetch(core_even, half_own, half_other, w_down.at[pl.ds(0, half)], sems.at[2])
    high = fetch(core_even, half_other, half_own, w_down.at[pl.ds(half, half)], sems.at[3])
    return low, high


def vectors(core_even, refs):
    own, other = refs[:3], refs[3:]
    att = [jnp.where(core_even, a[...].astype(F32), b[...].astype(F32)) for a, b in zip(own, other)]
    mlp = [jnp.where(core_even, b[...].astype(F32), a[...].astype(F32)) for a, b in zip(own, other)]
    return att, mlp


def upright(row, width):
    return jnp.broadcast_to(row.astype(F32), (width, row.shape[1])).T[:, :1]


def row_number(place, slot, count, backward):
    late = place[1]
    number = slot - (1 - late) if backward else slot - late
    return place[0] * count + jnp.clip(number, 0, count - 1)


def forward_kernel(
    slot, count, place, patches, sent_row, flags, segments, token, *refs
):
    vecs = refs[:6]
    (first_own, first_other, half_own, half_other,
     keep_out, send_out, y_mlp_out, x_out, mid_out, qkv_out, soft_out, ctx_out, act_keep_out, act_send_out, slope_out,
     w_att, w_up, w_down, x, bias, normed, qkv, soft, ctx, mid, act, slope, y_mlp, sems) = refs[6:]
    core_even = place[0] == 0
    early = place[1] == 0
    rows, width = x.shape
    groups = width // GROUP
    row = row_number(place, slot, count, False)
    get_x = fetch(early, patches.at[row], sent_row, x, sems.at[4])
    get_att = fetch(core_even, first_own, first_other, w_att, sems.at[0])
    (att_gain, att_shift, att_bias), (mlp_gain, mlp_shift, mlp_bias) = vectors(core_even, vecs)
    seg = segments[pl.ds(row, 1)]
    bias[...] = jnp.where(upright(seg, 128) == seg.astype(F32), 0.0, NEGATIVE)
    settle(place, get_x)

    @pl.when(early)
    def _():
        flag = upright(flags[pl.ds(row, 1)], 128)
        x[...] = jnp.where(flag == 1.0, token[...].astype(F32), x[...].astype(F32)).astype(BF16)

    puts = [start_copy(x, x_out, sems.at[5])]
    hat, _ = norm_parts(x[...].astype(F32))
    normed[...] = (hat * att_gain + att_shift).astype(BF16)
    settle(place, get_att)
    get_up = fetch(core_even, first_other, first_own, w_up, sems.at[1])
    get_low, get_high = load_down(core_even, half_own, half_other, w_down, sems)
    projected = dot_nn(normed[...], w_att[:, : 3 * width])
    q_low = (projected[:, :width] + att_bias[:, :width]).astype(BF16)
    qkv[:, :width] = (q_low * 0.125).astype(BF16)
    qkv[:, width : 2 * width] = projected[:, width : 2 * width].astype(BF16)
    qkv[:, 2 * width :] = (projected[:, 2 * width :] + att_bias[:, width : 2 * width]).astype(BF16)
    puts.append(start_copy(qkv, qkv_out, sems.at[6]))
    heads = GROUP // 64
    for group in range(groups):
        cols = pl.ds(group * GROUP, GROUP)
        q = qkv[:, cols]
        k = qkv[:, pl.ds(width + group * GROUP, GROUP)]
        v = qkv[:, pl.ds(2 * width + group * GROUP, GROUP)]
        masks = [head_mask(rows, head) for head in range(heads)]
        scores = dot_nt(jnp.concatenate([jnp.where(mask, q, 0) for mask in masks], 0), k)
        total = jnp.zeros((rows, GROUP), F32)
        for head in range(heads):
            mine = scores[head * rows : (head + 1) * rows] + bias[...]
            raised = jnp.exp(mine - jnp.max(mine, -1, keepdims=True))
            weight = (raised * (1.0 / jnp.sum(raised, -1, keepdims=True))).astype(BF16)
            soft[group * heads + head] = weight
            total = total + dot_nn(weight, jnp.where(masks[head], v, 0))
        ctx[:, cols] = total.astype(BF16)
        span = pl.ds(group * heads, heads)
        puts.append(start_copy(soft.at[span], soft_out.at[span], sems.at[17 + group]))
    puts.append(start_copy(ctx, ctx_out, sems.at[8]))
    y = x[...].astype(F32) + dot_nn(ctx[...], w_att[:, 3 * width :]) + att_bias[:, 2 * width : 3 * width]
    low = y.astype(BF16)
    mid[...] = low
    puts.append(start_copy(mid, mid_out, sems.at[9]))
    puts.append(deliver(core_even, mid, keep_out, send_out, sems.at[10]))
    hat, _ = norm_parts(low.astype(F32))
    normed[...] = (hat * mlp_gain + mlp_shift).astype(BF16)
    settle(place, get_up)
    half = act.shape[1] // 2
    for side in range(2):
        cols = pl.ds(side * half, half)
        hidden = dot_nn(normed[...], w_up[:, cols]) + mlp_bias[:, side * half : (side + 1) * half]
        active, rate = gelu_pair(hidden)
        act[:, cols] = active.astype(BF16)
        slope[:, cols] = rate.astype(BF16)
        targets = (act_send_out, act_keep_out) if side else (act_keep_out, act_send_out)
        puts.append(deliver(core_even, act.at[:, cols], *targets, sems.at[11 + side]))
        puts.append(start_copy(slope.at[:, cols], slope_out.at[:, cols], sems.at[13 + side]))
    settle(place, get_low, get_high)
    y = mid[...].astype(F32) + dot_nn(act[...], w_down[...]) + att_bias[:, 3 * width :]
    y_mlp[...] = y.astype(BF16)
    puts.append(start_copy(y_mlp, y_mlp_out, sems.at[15]))
    puts.append(deliver(core_even, y_mlp, send_out, keep_out, sems.at[16]))
    for put in puts:
        put.wait()


def forward_call(slot, place, patches, sent_row, flags, segments, token, vecs, weights):
    rows, width = sent_row.shape
    hidden = weights[0].shape[1]
    low = lambda *shape: jax.ShapeDtypeStruct(shape, BF16)
    row = low(rows, width)
    outs = [row, row, row, row, row, low(rows, 3 * width), low(HEADS, rows, rows), row]
    outs += [low(rows, hidden // 2), low(rows, hidden // 2), low(rows, hidden)]
    v = pltpu.VMEM
    return pl.pallas_call(
        partial(forward_kernel, slot, patches.shape[0] // 2),
        out_shape=outs,
        in_specs=[SMEM, ANY, ANY] + [VMEM] * 9 + [ANY] * 4,
        out_specs=[ANY] * len(outs),
        scratch_shapes=[
            v((width, hidden), BF16), v((width, hidden), BF16), v((hidden, width), BF16),
            v((rows, width), BF16), v((rows, rows), F32), v((rows, width), BF16),
            v((rows, 3 * width), BF16), v((HEADS, rows, rows), BF16), v((rows, width), BF16), v((rows, width), BF16),
            v((rows, hidden), BF16), v((rows, hidden), BF16), v((rows, width), BF16),
            pltpu.SemaphoreType.DMA((20,)),
        ],
        compiler_params=pltpu.CompilerParams(vmem_limit_bytes=VMEM_LIMIT),
        cost_estimate=pl.CostEstimate(flops=7_000_000_000, bytes_accessed=26_000_000, transcendentals=2_500_000),
        name="row_forward",
    )(place, patches, sent_row, flags, segments, token, *vecs, *weights)


def backward_kernel(slot, count, place, cotangent, back_row, flags, *refs):
    vecs = refs[:6]
    (first_own, first_other, half_own, half_other,
     x_a, mid_a, qkv_a, soft_a, ctx_a, slope_a, x_b, mid_b, qkv_b, soft_b, ctx_b, slope_b,
     keep_out, send_out, grad_x_out, small_out, pack_keep, pack_send,
     w_att, w_up, w_down, grad_y, x, mid, qkv, soft, ctx, slope, normed_att, normed_mlp, dqkv, dhid, gmid, gx,
     dctx_all, ds_all, soft_all, small_low, sems) = refs[6:]
    core_even = place[0] == 0
    early = place[1] == 0
    rows, width = x.shape
    groups = width // GROUP
    row = row_number(place, slot, count, True)
    busy = jnp.logical_and(early, slot >= 1) | jnp.logical_and(jnp.logical_not(early), slot < count)
    small_out[...] = jnp.zeros(small_out.shape, F32)

    @pl.when(busy)
    def _():
        get_g = fetch(early, back_row, cotangent.at[row], grad_y, sems.at[4])
        get_low, get_high = load_down(core_even, half_own, half_other, w_down, sems)
        get_slope = fetch(early, slope_a, slope_b, slope, sems.at[5])
        get_up = fetch(core_even, first_other, first_own, w_up, sems.at[1])
        (att_gain, att_shift, _), (mlp_gain, mlp_shift, _) = vectors(core_even, vecs)
        settle(place, get_g)

        def pack(source, start, to_even, sem):
            spot = (pl.ds(0, rows), pl.ds(start, source.shape[1]))
            if to_even:
                return deliver(core_even, source, pack_keep.at[spot], pack_send.at[spot], sem)
            return deliver(core_even, source, pack_send.at[spot], pack_keep.at[spot], sem)

        hidden = dhid.shape[1]
        last = 2 * width + hidden
        puts = [
            start_copy(grad_y, pack_keep.at[pl.ds(0, rows), pl.ds(last, width)], sems.at[11]),
            start_copy(grad_y, pack_send.at[pl.ds(0, rows), pl.ds(last, width)], sems.at[20]),
        ]
        small_out[5:6] = jnp.sum(grad_y[...].astype(F32), 0, keepdims=True)
        settle(place, get_low, get_high, get_slope)
        get_mid = fetch(early, mid_a, mid_b, mid, sems.at[6])
        get_att = fetch(core_even, first_own, first_other, w_att, sems.at[0])
        get_soft = fetch(early, soft_a, soft_b, soft, sems.at[9])
        get_qkv = fetch(early, qkv_a, qkv_b, qkv, sems.at[8])
        get_ctx = fetch(early, ctx_a, ctx_b, ctx, sems.at[10])
        get_x = fetch(early, x_a, x_b, x, sems.at[7])
        half = hidden // 2
        for side in range(2):
            cols = pl.ds(side * half, half)
            low = (dot_nt(grad_y[...], w_down[cols, :]) * slope[:, cols].astype(F32)).astype(BF16)
            dhid[:, cols] = low
            sums = jnp.sum(low.astype(F32), 0, keepdims=True)
            for part in range(half // width):
                number = 10 + side * (half // width) + part
                small_out[number : number + 1] = sums[:, part * width : (part + 1) * width]
        puts.append(pack(dhid, 2 * width, False, sems.at[12]))
        settle(place, get_up, get_mid)
        dnorm = dot_nt(dhid[...], w_up[...])
        hat, scale = norm_parts(mid[...].astype(F32))
        normed_mlp[...] = (hat * mlp_gain + mlp_shift).astype(BF16)
        puts.append(pack(normed_mlp, 0, False, sems.at[13]))
        puts.append(pack(normed_mlp, width, False, sems.at[21]))
        small_out[8:9] = jnp.sum(dnorm * hat, 0, keepdims=True)
        small_out[9:10] = jnp.sum(dnorm, 0, keepdims=True)
        u = dnorm * mlp_gain
        grad = grad_y[...].astype(F32) + scale * (
            u - jnp.mean(u, -1, keepdims=True) - hat * jnp.mean(u * hat, -1, keepdims=True)
        )
        low = grad.astype(BF16)
        gmid[...] = low
        puts.append(pack(gmid, 2 * width + 3 * width, True, sems.at[14]))
        puts.append(deliver(core_even, gmid, send_out, keep_out, sems.at[15]))
        small_out[4:5] = jnp.sum(low.astype(F32), 0, keepdims=True)
        settle(place, get_att, get_qkv, get_soft, get_ctx)
        puts.append(pack(ctx, width, True, sems.at[22]))
        dctx_all[...] = dot_nt(gmid[...], w_att[:, 3 * width :]).astype(BF16)
        heads = GROUP // 64

        def group_step(group, carry):
            cols = columns(group, GROUP)
            k_cols = pl.ds(pl.multiple_of(width + group * GROUP, GROUP), GROUP)
            v_cols = pl.ds(pl.multiple_of(2 * width + group * GROUP, GROUP), GROUP)
            dctx = dctx_all[:, cols]
            q = qkv[:, cols]
            k = qkv[:, k_cols]
            v = qkv[:, v_cols]
            product = dctx.astype(F32) * ctx[:, cols].astype(F32)
            masks = [head_mask(rows, head) for head in range(heads)]
            mine = jnp.concatenate([jnp.where(mask, dctx, 0) for mask in masks], 0)
            dp = dot_nt(mine, v)
            dq = jnp.zeros((rows, GROUP), F32)
            for head in range(heads):
                span = pl.ds(head * rows, rows)
                weight = soft[group * heads + head]
                delta = jnp.sum(jnp.where(masks[head], product, 0.0), -1, keepdims=True)
                ds = (weight.astype(F32) * (dp[head * rows : (head + 1) * rows] - delta)).astype(BF16)
                ds_all[span] = ds
                soft_all[span] = weight
                dq = dq + dot_nn(ds, jnp.where(masks[head], k, 0))
            dk = dot_tn(ds_all[...], jnp.concatenate([jnp.where(mask, q, 0) for mask in masks], 0))
            dv = dot_tn(soft_all[...], mine)
            dq_low = (dq * 0.125).astype(BF16)
            dv_low = dv.astype(BF16)
            dqkv[:, cols] = dq_low
            dqkv[:, k_cols] = dk.astype(BF16)
            dqkv[:, v_cols] = dv_low
            small_out[2:3, cols] = jnp.sum(dq_low.astype(F32), 0, keepdims=True)
            small_out[3:4, cols] = jnp.sum(dv_low.astype(F32), 0, keepdims=True)
            return carry

        lax.fori_loop(0, groups, group_step, 0)
        puts.append(pack(dqkv, 2 * width, True, sems.at[16]))
        settle(place, get_x)
        dnorm = dot_nt(dqkv[...], w_att[:, : 3 * width])
        hat, scale = norm_parts(x[...].astype(F32))
        normed_att[...] = (hat * att_gain + att_shift).astype(BF16)
        puts.append(pack(normed_att, 0, True, sems.at[17]))
        small_out[0:1] = jnp.sum(dnorm * hat, 0, keepdims=True)
        small_out[1:2] = jnp.sum(dnorm, 0, keepdims=True)
        u = dnorm * att_gain
        grad = gmid[...].astype(F32) + scale * (
            u - jnp.mean(u, -1, keepdims=True) - hat * jnp.mean(u * hat, -1, keepdims=True)
        )
        gx[...] = grad.astype(BF16)
        puts.append(start_copy(gx, grad_x_out, sems.at[18]))
        puts.append(deliver(core_even, gx, keep_out, send_out, sems.at[19]))
        token = jnp.sum(jnp.where(upright(flags[pl.ds(row, 1)], 128) == 1.0, grad, 0.0), 0, keepdims=True)
        small_out[6:7] = token
        small_out[14:15] = token
        theirs = jnp.where(core_even, small_out[8:16], small_out[0:8])
        high = theirs.astype(BF16)
        small_low[...] = jnp.concatenate([high, (theirs - high.astype(F32)).astype(BF16)], 0)
        puts.append(start_copy(small_low, pack_send.at[pl.ds(rows, 16), pl.ds(0, width)], sems.at[23]))
        for put in puts:
            put.wait()


def backward_call(slot, place, cotangent, back_row, flags, vecs, weights, saved_early, saved_late):
    rows, width = back_row.shape
    hidden = weights[0].shape[1]
    low = lambda *shape: jax.ShapeDtypeStruct(shape, BF16)
    row = low(rows, width)
    pack = low(rows + 16, 3 * width + hidden)
    outs = [row, row, row, jax.ShapeDtypeStruct((16, width), F32), pack, pack]
    specs = [ANY] * len(outs)
    specs[3] = VMEM
    v = pltpu.VMEM
    return pl.pallas_call(
        partial(backward_kernel, slot, cotangent.shape[0] // 2),
        out_shape=outs,
        in_specs=[SMEM, ANY, ANY] + [VMEM] * 7 + [ANY] * 16,
        out_specs=specs,
        scratch_shapes=[
            v((width, hidden), BF16), v((width, hidden), BF16), v((hidden, width), BF16),
            v((rows, width), BF16), v((rows, width), BF16), v((rows, width), BF16),
            v((rows, 3 * width), BF16), v((HEADS, rows, rows), BF16), v((rows, width), BF16), v((rows, hidden), BF16),
            v((rows, width), BF16), v((rows, width), BF16), v((rows, 3 * width), BF16), v((rows, hidden), BF16),
            v((rows, width), BF16), v((rows, width), BF16), v((rows, width), BF16),
            v((GROUP // 64 * rows, rows), BF16), v((GROUP // 64 * rows, rows), BF16),
            v((16, width), BF16), pltpu.SemaphoreType.DMA((24,)),
        ],
        compiler_params=pltpu.CompilerParams(vmem_limit_bytes=VMEM_LIMIT),
        cost_estimate=pl.CostEstimate(flops=8_000_000_000, bytes_accessed=34_000_000, transcendentals=1_000),
        name="row_backward",
    )(place, cotangent, back_row, flags, *vecs, *weights, *saved_early, *saved_late)


def weight_kernel(first_row, last_row, tall_rows, short_rows, place, token, *refs):
    sources, refs = refs[:10], refs[10:]
    if not first_row:
        before, refs = refs[:3], refs[3:]
    made = len(refs) - 13
    outs, refs = refs[:made], refs[made:]
    (left, right, act, grad_y, turned, part_t, grad_first, grad_half, mine, theirs, summed, small_low, sems) = refs
    early = place[1] == 0
    rows = left.shape[0] // 2
    hidden = right.shape[1]
    width = grad_y.shape[1]
    quarter = grad_half.shape[1]
    tall = pl.ds(pl.multiple_of(place[2] * place[3], 16), width)
    short = pl.ds(pl.multiple_of(place[2] * place[4], 16), quarter)
    core_even = place[0] == 0
    get_mine = fetch(early, sources[4], sources[9], mine, sems.at[10])
    spot = (pl.ds(rows, 16), pl.ds(0, width))
    get_theirs = fetch(early, sources[1].at[spot], sources[6].at[spot], theirs, sems.at[11])
    if not first_row:
        old_small = start_copy(before[2], summed, sems.at[12])
    waits = []
    for index, (first, second) in enumerate(zip(sources[2:4], sources[7:9])):
        waits.append(fetch(early, first, second, act.at[pl.ds(index * rows, rows)], sems.at[index]))
    start = 0
    pieces = []
    for number, target in enumerate((left, right, grad_y)):
        span = pl.ds(start, target.shape[1])
        start += target.shape[1]
        pieces.append([(first.at[pl.ds(0, rows), span], second.at[pl.ds(0, rows), span], target.at[pl.ds(index * rows, rows)], sems.at[2 + 2 * number + index])
                       for index, (first, second) in enumerate(zip(sources[:2], sources[5:7]))])
    waits += [fetch(early, *piece) for piece in pieces[2]]
    if not first_row:
        old_half = start_copy(before[1], grad_half, sems.at[8])
    waits_left = [fetch(early, *piece) for piece in pieces[0]]
    waits_right = [fetch(early, *piece) for piece in pieces[1]]
    if not first_row:
        old_first = start_copy(before[0], grad_first, sems.at[9])
    puts = []
    settle(place, get_mine, get_theirs, *([] if first_row else [old_small]))
    ours = jnp.where(core_even, mine[0:8], mine[8:16]) + theirs[0:8].astype(F32) + theirs[8:16].astype(F32)
    summed[...] = ours if first_row else ours + summed[...]
    if last_row:
        lines = lax.broadcasted_iota(jnp.int32, summed.shape, 0)
        summed[...] = jnp.where((lines == 6) & jnp.logical_not(early), token[...], summed[...])
        small_low[...] = jnp.concatenate([summed[...], jnp.zeros(summed.shape, F32)], 0).astype(BF16)
        if tall_rows:
            for index in range(width // tall_rows):
                target = outs[3 + index].at[pl.ds(tall_rows + short_rows, 16)]
                puts.append(start_copy(small_low, target, sems.at[14 + index]))
    puts.append(start_copy(summed, outs[2], sems.at[13]))

    def total(target, index, value):
        if not first_row:
            value = value + target[index].astype(F32)
        target[index] = value.astype(BF16)

    for wait in waits:
        wait.wait()
    if not first_row:
        old_half.wait()

    def half_step(part, carry):
        flipped = act[:, columns(part, quarter)].T
        part_t[pl.ds(0, quarter)] = flipped
        part_t[pl.ds(quarter, quarter)] = flipped
        total(grad_half, part, dot_nn(part_t[short], grad_y[...]))
        return carry

    lax.fori_loop(0, 4, half_step, 0)
    chunks = width // tall_rows if tall_rows else 0

    def ship(source, part, start, sem):
        if not chunks:
            return [start_copy(source.at[part], outs[3 + part].at[pl.ds(start, source.shape[1])], sems.at[sem + part])]
        size = source.shape[1] // chunks
        return [
            start_copy(
                source.at[part, pl.ds(index * size, size)],
                outs[3 + part * chunks + index].at[pl.ds(start // chunks, size)],
                sems.at[sem + part * chunks + index],
            )
            for index in range(chunks)
        ]

    if last_row:
        for part in range(4):
            puts += ship(grad_half, part, width, 14 + chunks)
    if not last_row:
        puts.append(start_copy(grad_half, outs[1], sems.at[14]))
    for wait in waits_left:
        wait.wait()

    for wait in waits_right:
        wait.wait()
    if not first_row:
        old_first.wait()

    def first_step(part, carry):
        @pl.when((part == 0) | (part == 3))
        def _():
            flipped = left[:, columns(part // 3, width)].T
            turned[pl.ds(0, width)] = flipped
            turned[pl.ds(width, width)] = flipped

        total(grad_first, part, dot_nn(turned[tall], right[:, columns(part, width)]))
        return carry

    lax.fori_loop(0, 4, first_step, 0)
    if last_row:
        for part in range(4):
            puts += ship(grad_first, part, 0, 14 + chunks + 4 * max(chunks, 1))
    if not last_row:
        puts.append(start_copy(grad_first, outs[0], sems.at[15]))
    for put in puts:
        put.wait()


def weight_call(place, token, early_row, late_row, before, last_row, members):
    rows, half = early_row[2].shape
    hidden = 2 * half
    width = (early_row[0].shape[1] - hidden) // 3
    quarter = half // 4
    low = lambda *shape: jax.ShapeDtypeStruct(shape, BF16)
    tall, short = aligned_chunk(width, quarter, members)
    sums = jax.ShapeDtypeStruct((8, width), F32)
    outs = [low(4, width, width), low(4, quarter, width), sums]
    if last_row:
        outs = [
            jax.ShapeDtypeStruct((members, width // members, hidden), F32),
            jax.ShapeDtypeStruct((4, members, quarter // members, width), F32),
            sums,
        ]
        outs += [low(tall + short + 16, width)] * members + [low(tall + short, width)] * (3 * members) if tall else [low(width + quarter, width)] * 4
    v = pltpu.VMEM
    return pl.pallas_call(
        partial(weight_kernel, before is None, last_row, tall, short),
        out_shape=outs,
        in_specs=[SMEM, VMEM] + [ANY] * (10 if before is None else 13),
        out_specs=[ANY] * len(outs),
        scratch_shapes=[
            v((2 * rows, 2 * width), BF16), v((2 * rows, hidden), BF16), v((2 * rows, half), BF16),
            v((2 * rows, width), BF16), v((2 * width, 2 * rows), BF16), v((2 * quarter, 2 * rows), BF16),
            v((4, width, width), BF16), v((4, quarter, width), BF16),
            v((16, width), F32), v((16, width), BF16), v((8, width), F32), v((16, width), BF16),
            pltpu.SemaphoreType.DMA((24 + 9 * members,)),
        ],
        compiler_params=pltpu.CompilerParams(vmem_limit_bytes=VMEM_LIMIT),
        cost_estimate=pl.CostEstimate(flops=8_000_000_000, bytes_accessed=24_000_000, transcendentals=0),
        name="weight_gradients",
    )(place, token, *early_row, *late_row, *(before or ()))


def aligned_chunk(width, quarter, members):
    tall, short = width // members, quarter // members
    return (tall, short) if tall % 16 == 0 and short % 16 == 0 else (0, 0)


def ring_order(members):
    return list(range(0, members, 2)) + list(range(members - 1, 0, -2))


def ring_reduce(own, matrix, half, position, axis, pending):
    members = lax.axis_size(axis)
    order = ring_order(members)
    ahead = [(order[i], order[(i + 1) % members]) for i in range(members)]
    behind = [(b, a) for a, b in ahead]
    parts = len(own)
    tall, width = matrix.shape[1], half.shape[3]
    short = half.shape[2]
    steps = [1 - 2 * (part % 2) for part in range(parts)]

    def piece(array, index):
        cut = lambda start, size: lax.dynamic_slice_in_dim(array, start, size, 0)
        if isinstance(index, int):
            cut = lambda start, size: lax.slice_in_dim(array, start, start + size, axis=0)
        return jnp.concatenate([cut(index * tall, tall), cut(width + index * short, short)], 0).astype(F32)

    def chunk(part, number):
        index = (members - steps[part] * number) % members
        return own[part][index].astype(F32) if isinstance(own[part], (list, tuple)) else piece(own[part], index)

    def shift(part, value):
        return lax.ppermute(value, axis, ahead if part % 2 == 0 else behind)

    def reduce_step(number, current):
        moved = [shift(part, current[part]) for part in range(parts)]
        return [(moved[part].astype(F32) + chunk(part, number)).astype(BF16) for part in range(parts)]

    def place_chunks(number, current, matrix, half):
        for part in range(parts):
            index = lax.rem(position + jnp.uint32(members) + jnp.uint32(steps[part] % members) * (
                jnp.uint32(members + 1) - jnp.uint32(number)), jnp.uint32(members))
            wide = current[part].astype(F32)
            zero, block = jnp.uint32(0), jnp.uint32(part)
            matrix = lax.dynamic_update_slice(matrix, wide[None, :tall], (index, zero, jnp.uint32(part * width)))
            half = lax.dynamic_update_slice(half, wide[None, None, tall:], (block, index, zero, zero))
        return matrix, half

    def gather_step(number, carry):
        current, matrix, half = carry
        current = [shift(part, current[part]) for part in range(parts)]
        return (current, *place_chunks(number, current, matrix, half))

    current = [chunk(part, 0).astype(BF16) for part in range(parts)]
    extra = current[0]
    if members > 8:
        current = lax.fori_loop(1, members, reduce_step, current)
        carry = lax.fori_loop(1, members, gather_step, (current, *place_chunks(0, current, matrix, half)))
    else:
        for number in range(1, members):
            current = reduce_step(number, current)
        extra = current[0][tall + short :]
        current[0] = current[0][: tall + short]
        carry = (current, *place_chunks(0, current, matrix, half))
        for number in range(1, members):
            carry = gather_step(number, carry)
            if number in (1, 3):
                which = number // 2
                pending[which] = lax.optimization_barrier((pending[which], carry[0][0]))[0]
    return carry[1].reshape(tall * members, parts * width), carry[2].reshape(parts * short * members, width), extra, pending


def turn_rows(array, width, position, members):
    top = jnp.roll(array[:width], -position * (width // members), 0)
    return jnp.concatenate([top, jnp.roll(array[width:], -position * ((array.shape[0] - width) // members), 0)], 0)


def shards(
    patches, cotangent, mask_flags, segments, mask_token, norm_gains, norm_shifts, w_first, first_bias, down_half
):
    section = lax.axis_index("section")
    core = section & 1
    stage = section >> 1
    early = stage == 0
    swap = [(0, 1), (1, 0), (2, 3), (3, 2)]
    forth = [(0, 2), (1, 3)]
    back = [(2, 0), (3, 1)]
    row_count, rows, width = patches.shape
    count = row_count // 2
    members = lax.axis_size("dp")
    place_of = np.zeros(members, np.int32)
    for spot, member in enumerate(ring_order(members)):
        place_of[member] = spot
    position = jnp.asarray(place_of)[lax.axis_index("dp").astype(jnp.uint32)]

    first_own, half_own = w_first[0], down_half[0]
    hidden = first_own.shape[1]
    quarter = hidden // 8
    tall, short = width // members, quarter // members
    aligned = aligned_chunk(width, quarter, members)[0] > 0
    first_other = lax.ppermute(first_own, "section", swap)
    half_other = lax.ppermute(half_own, "section", swap)
    own_vecs = (norm_gains, norm_shifts, first_bias)
    vecs = own_vecs + tuple(lax.ppermute(array, "section", swap) for array in own_vecs)
    weights = (first_own, first_other, half_own, half_other)
    turns = position if aligned else 0 * position
    place = jnp.stack([core, stage, turns, jnp.int32(16 * (tall // 16)), jnp.int32(16 * (short // 16))]).astype(jnp.int32)
    token = mask_token[None]

    forwards, acts, packs = [], [], []
    sent = patches[0]
    for slot in range(count + 1):
        result = forward_call(slot, place, patches, sent, mask_flags, segments, token, vecs, weights)
        forwards.append(result)
        if slot < count:
            sent = lax.ppermute(result[2], "section", forth)
        acts.append(lax.ppermute(result[9], "section", swap))

    def assemble(pairs):
        chosen = [jnp.where(early, a, b) for a, b in pairs]
        keep, send = jnp.stack(chosen[0::2]), jnp.stack(chosen[1::2])
        received = lax.ppermute(send, "section", swap)
        return jnp.where(
            core == 0, jnp.concatenate([keep, received], 0), jnp.concatenate([received, keep], 0)
        )

    backs = []
    returned = patches[0]
    grads = None
    for slot in range(count + 1):
        saved = [
            [forwards[which][i] for i in (3, 4, 5, 6, 7, 10)] for which in (max(slot - 1, 0), min(slot + 1, count))
        ]
        backs.append(backward_call(slot, place, cotangent, returned, mask_flags, vecs, weights, *saved))
        if slot < count:
            returned = lax.ppermute(backs[slot][2], "section", back)
        packs.append(lax.ppermute(backs[slot][5], "section", swap))
        if slot > 0:
            row = slot - 1
            chosen = [
                (backs[b][4], packs[b], forwards[f][8], acts[f], backs[b][3]) for f, b in ((row, row + 1), (row + 1, row))
            ]
            total = sum(backs[b][3][6:7] for b in range(1, slot + 1))
            if row == count - 1:
                cross = [(0, 3), (1, 2)]
                total = lax.ppermute(total, "section", forth) + lax.ppermute(total, "section", cross)
            grads = weight_call(place, total, *chosen, grads, row == count - 1, members)
            if row < count - 1:
                returned, grads = lax.optimization_barrier((returned, grads))

    blank, small = grads[:2], grads[2]
    if aligned:
        own = [grads[3 + part * members : 3 + (part + 1) * members] for part in range(4)]
    else:
        own = [turn_rows(array, width, position, members) for array in grads[3:]]
        small = lax.psum(small, "dp")

    pending = [
        [(forwards[row][i], forwards[row + 1][i]) for row in range(count) for i in (0, 1)],
        [(backs[row + 1][i], backs[row][i]) for row in range(count) for i in (0, 1)],
    ]
    grad_first, grad_half, extra, pending = ring_reduce(own, *blank, position.astype(jnp.uint32), "dp", pending)
    if aligned:
        small = extra[:8].astype(F32)
    token_grad = small[6]

    finals = assemble(pending[0])
    back_rows = assemble(pending[1]).astype(F32)
    back_rows = jnp.where((section == 0) & (mask_flags[..., None] == 1), 0.0, back_rows)
    return (
        finals[None],
        back_rows[None],
        token_grad,
        small[0:1],
        small[1:2],
        grad_first[None],
        small[2:6].reshape(1, hidden),
        grad_half[None],
    )


def solution(mesh):
    return jax.shard_map(
        shards,
        mesh=mesh,
        in_specs=(
            P("dp", None, None),
            P("dp", None, None),
            P("dp", None),
            P("dp", None),
            P(),
            P("section", None),
            P("section", None),
            P("section", None, None),
            P("section", None),
            P("section", None, None),
        ),
        out_specs=(
            P("section", "dp", None, None),
            P("section", "dp", None, None),
            P(),
            P("section", None),
            P("section", None),
            P("section", None, None),
            P("section", None),
            P("section", None, None),
        ),
        check_vma=False,
    )
```

```python
from functools import partial

import jax
import jax.numpy as jnp
import numpy as np
from jax import lax
from jax.experimental import pallas as pl
from jax.experimental.pallas import tpu as pltpu
from jax.sharding import PartitionSpec as P

HEADS = 12
EPSILON = 1e-06
NEGATIVE = -1000000000.0
GROUP = 256
TILE = 768
MIB = 1024 * 1024
VMEM_LIMIT = 49 * MIB
BF16 = jnp.bfloat16
F32 = jnp.float32
ANY = pl.BlockSpec(memory_space=pl.ANY)
SMEM = pl.BlockSpec(memory_space=pltpu.SMEM)
VMEM = pl.BlockSpec(memory_space=pltpu.VMEM)


def dot_nn(a, b):
    return jnp.dot(a, b, preferred_element_type=F32)


def dot_nt(a, b):
    return lax.dot_general(a, b, (((1,), (1,)), ((), ())), preferred_element_type=F32)


def dot_tn(a, b):
    return lax.dot_general(a, b, (((0,), (0,)), ((), ())), preferred_element_type=F32)


def fetch(choice, first, second, target, sem):
    @pl.when(choice)
    def _():
        pltpu.make_async_copy(first, target, sem).start()

    @pl.when(jnp.logical_not(choice))
    def _():
        pltpu.make_async_copy(second, target, sem).start()

    return pltpu.make_async_copy(first, target, sem)


def deliver(choice, source, first, second, sem):
    @pl.when(choice)
    def _():
        pltpu.make_async_copy(source, first, sem).start()

    @pl.when(jnp.logical_not(choice))
    def _():
        pltpu.make_async_copy(source, second, sem).start()

    return pltpu.make_async_copy(source, first, sem)


def start_copy(source, target, sem):
    copy = pltpu.make_async_copy(source, target, sem)
    copy.start()
    return copy


def settle(place, *copies):
    @pl.when(place[0] >= 0)
    def _():
        for copy in copies:
            copy.wait()


def norm_parts(x):
    centred = x - jnp.mean(x, -1, keepdims=True)
    scale = lax.rsqrt(jnp.mean(centred * centred, -1, keepdims=True) + EPSILON)
    return centred * scale, scale


def gelu_pair(hidden):
    base = 1.0 + 0.23164189 * jnp.abs(hidden)
    t = pl.reciprocal(base, approx=True)
    t = t * (2.0 - base * t)
    poly = ((((0.5307027145 * t - 0.7265760135) * t + 0.7107068705) * t - 0.142248368) * t + 0.127414796) * t
    fall = jnp.exp2(hidden * hidden * -0.7213475204444817)
    tail = poly * fall
    cdf = jnp.where(hidden >= 0, 1.0 - tail, tail)
    return hidden * cdf, cdf + hidden * fall * 0.3989422804014327


def columns(index, width):
    return pl.ds(pl.multiple_of(index * width, width), width)


def head_mask(rows, head):
    lane = lax.broadcasted_iota(jnp.int32, (rows, GROUP), 1)
    return (lane >= head * 64) & (lane < head * 64 + 64)


def load_down(core_even, half_own, half_other, w_down, sems):
    half = half_own.shape[0]
    low = fetch(core_even, half_own, half_other, w_down.at[pl.ds(0, half)], sems.at[2])
    high = fetch(core_even, half_other, half_own, w_down.at[pl.ds(half, half)], sems.at[3])
    return low, high


def vectors(core_even, refs):
    own, other = refs[:3], refs[3:]
    att = [jnp.where(core_even, a[...].astype(F32), b[...].astype(F32)) for a, b in zip(own, other)]
    mlp = [jnp.where(core_even, b[...].astype(F32), a[...].astype(F32)) for a, b in zip(own, other)]
    return att, mlp


def upright(row, width):
    return jnp.broadcast_to(row.astype(F32), (width, row.shape[1])).T[:, :1]


def in_hbm(arrays):
    return [pltpu.with_memory_space_constraint(array, pltpu.HBM) for array in arrays]


def row_number(place, slot, count, backward):
    late = place[1]
    number = slot - (1 - late) if backward else slot - late
    return place[0] * count + jnp.clip(number, 0, count - 1)


def forward_kernel(
    slot, count, held, place, patches, sent_row, flags, segments, token, *refs
):
    vecs, refs = refs[:6], refs[6:]
    if held:
        (w_att, w_up, w_down), refs = refs[:3], refs[3:]
    else:
        (first_own, first_other, half_own, half_other), refs = refs[:4], refs[4:]
    (keep_out, send_out, y_mlp_out, x_out, mid_out, qkv_out, soft_out, ctx_out, act_keep_out, act_send_out,
     slope_out, x, bias, normed, qkv, soft, ctx, mid, act, slope, y_mlp, sems) = refs[:22]
    if not held:
        w_att, w_up, w_down = refs[22:]
    core_even = place[0] == 0
    early = place[1] == 0
    rows, width = x.shape
    groups = width // GROUP
    row = row_number(place, slot, count, False)
    get_x = fetch(early, patches.at[row], sent_row, x, sems.at[4])
    if not held:
        get_att = fetch(core_even, first_own, first_other, w_att, sems.at[0])
    (att_gain, att_shift, att_bias), (mlp_gain, mlp_shift, mlp_bias) = vectors(core_even, vecs)
    seg = segments[pl.ds(row, 1)]
    bias[...] = jnp.where(upright(seg, 128) == seg.astype(F32), 0.0, NEGATIVE)
    settle(place, get_x)

    @pl.when(early)
    def _():
        flag = upright(flags[pl.ds(row, 1)], 128)
        x[...] = jnp.where(flag == 1.0, token[...].astype(F32), x[...].astype(F32)).astype(BF16)

    puts = [start_copy(x, x_out, sems.at[5])]
    hat, _ = norm_parts(x[...].astype(F32))
    normed[...] = (hat * att_gain + att_shift).astype(BF16)
    if not held:
        settle(place, get_att)
        get_up = fetch(core_even, first_other, first_own, w_up, sems.at[1])
        get_low, get_high = load_down(core_even, half_own, half_other, w_down, sems)
    projected = dot_nn(normed[...], w_att[:, : 3 * width])
    q_low = (projected[:, :width] + att_bias[:, :width]).astype(BF16)
    qkv[:, :width] = (q_low * 0.125).astype(BF16)
    qkv[:, width : 2 * width] = projected[:, width : 2 * width].astype(BF16)
    qkv[:, 2 * width :] = (projected[:, 2 * width :] + att_bias[:, width : 2 * width]).astype(BF16)
    puts.append(start_copy(qkv, qkv_out, sems.at[6]))
    heads = GROUP // 64
    for group in range(groups):
        cols = pl.ds(group * GROUP, GROUP)
        q = qkv[:, cols]
        k = qkv[:, pl.ds(width + group * GROUP, GROUP)]
        v = qkv[:, pl.ds(2 * width + group * GROUP, GROUP)]
        masks = [head_mask(rows, head) for head in range(heads)]
        scores = dot_nt(jnp.concatenate([jnp.where(mask, q, 0) for mask in masks], 0), k)
        total = jnp.zeros((rows, GROUP), F32)
        for head in range(heads):
            mine = scores[head * rows : (head + 1) * rows] + bias[...]
            raised = jnp.exp(mine - jnp.max(mine, -1, keepdims=True))
            weight = (raised * (1.0 / jnp.sum(raised, -1, keepdims=True))).astype(BF16)
            soft[group * heads + head] = weight
            total = total + dot_nn(weight, jnp.where(masks[head], v, 0))
        ctx[:, cols] = total.astype(BF16)
        span = pl.ds(group * heads, heads)
        puts.append(start_copy(soft.at[span], soft_out.at[span], sems.at[17 + group]))
    puts.append(start_copy(ctx, ctx_out, sems.at[8]))
    y = x[...].astype(F32) + dot_nn(ctx[...], w_att[:, 3 * width :]) + att_bias[:, 2 * width : 3 * width]
    low = y.astype(BF16)
    mid[...] = low
    puts.append(start_copy(mid, mid_out, sems.at[9]))
    puts.append(deliver(core_even, mid, keep_out, send_out, sems.at[10]))
    hat, _ = norm_parts(low.astype(F32))
    normed[...] = (hat * mlp_gain + mlp_shift).astype(BF16)
    if not held:
        settle(place, get_up)
    half = act.shape[1] // 2
    for side in range(2):
        cols = pl.ds(side * half, half)
        hidden = dot_nn(normed[...], w_up[:, cols]) + mlp_bias[:, side * half : (side + 1) * half]
        active, rate = gelu_pair(hidden)
        act[:, cols] = active.astype(BF16)
        slope[:, cols] = rate.astype(BF16)
        targets = (act_send_out, act_keep_out) if side else (act_keep_out, act_send_out)
        puts.append(deliver(core_even, act.at[:, cols], *targets, sems.at[11 + side]))
        puts.append(start_copy(slope.at[:, cols], slope_out.at[:, cols], sems.at[13 + side]))
    if not held:
        settle(place, get_low, get_high)
    y = mid[...].astype(F32) + dot_nn(act[...], w_down[...]) + att_bias[:, 3 * width :]
    y_mlp[...] = y.astype(BF16)
    puts.append(start_copy(y_mlp, y_mlp_out, sems.at[15]))
    puts.append(deliver(core_even, y_mlp, send_out, keep_out, sems.at[16]))
    for put in puts:
        put.wait()


def hold_kernel(place, first_own, first_other, half_own, half_other, w_att, w_up, w_down, sems):
    core_even = place[0] == 0
    copies = [
        fetch(core_even, first_own, first_other, w_att, sems.at[0]),
        fetch(core_even, first_other, first_own, w_up, sems.at[1]),
        *load_down(core_even, half_own, half_other, w_down, sems),
    ]
    for copy in copies:
        copy.wait()


def hold_call(place, weights):
    width, hidden = weights[0].shape
    v = pltpu.VMEM
    return pl.pallas_call(
        hold_kernel,
        out_shape=[v((width, hidden), BF16), v((width, hidden), BF16), v((hidden, width), BF16)],
        in_specs=[SMEM] + [ANY] * 4,
        out_specs=[VMEM] * 3,
        scratch_shapes=[pltpu.SemaphoreType.DMA((4,))],
        compiler_params=pltpu.CompilerParams(vmem_limit_bytes=VMEM_LIMIT),
        cost_estimate=pl.CostEstimate(flops=0, bytes_accessed=14_000_000, transcendentals=0),
        name="hold_weights",
    )(place, *weights)


def forward_call(slot, place, patches, sent_row, flags, segments, token, vecs, weights):
    rows, width = sent_row.shape
    held = len(weights) == 3
    if held:
        weights = [pltpu.with_memory_space_constraint(array, pltpu.VMEM) for array in weights]
    hidden = weights[0].shape[1]
    low = lambda *shape: jax.ShapeDtypeStruct(shape, BF16)
    row = low(rows, width)
    outs = [row, row, row, row, row, low(rows, 3 * width), low(HEADS, rows, rows), row]
    outs += [low(rows, hidden // 2), low(rows, hidden // 2), low(rows, hidden)]
    v = pltpu.VMEM
    return pl.pallas_call(
        partial(forward_kernel, slot, patches.shape[0] // 2, held),
        out_shape=outs,
        in_specs=[SMEM, ANY, ANY] + [VMEM] * 9 + ([VMEM] * 3 if held else [ANY] * 4),
        out_specs=[ANY] * len(outs),
        scratch_shapes=[
            v((rows, width), BF16), v((rows, rows), F32), v((rows, width), BF16),
            v((rows, 3 * width), BF16), v((HEADS, rows, rows), BF16), v((rows, width), BF16), v((rows, width), BF16),
            v((rows, hidden), BF16), v((rows, hidden), BF16), v((rows, width), BF16),
            pltpu.SemaphoreType.DMA((20,)),
        ]
        + ([] if held else [v((width, hidden), BF16), v((width, hidden), BF16), v((hidden, width), BF16)]),
        compiler_params=pltpu.CompilerParams(vmem_limit_bytes=VMEM_LIMIT if held else 60 * MIB),
        cost_estimate=pl.CostEstimate(flops=7_000_000_000, bytes_accessed=26_000_000, transcendentals=2_500_000),
        name="row_forward",
    )(place, patches, sent_row, flags, segments, token, *vecs, *weights)


def backward_kernel(slot, count, place, cotangent, back_row, flags, *refs):
    vecs = refs[:6]
    (w_att, w_up, w_down,
     x_a, mid_a, qkv_a, soft_a, ctx_a, slope_a, x_b, mid_b, qkv_b, soft_b, ctx_b, slope_b,
     keep_out, send_out, grad_x_out, small_out, pack_keep, pack_send,
     grad_y, x, mid, qkv, soft, ctx, slope, normed_att, normed_mlp, dqkv, dhid, gmid, gx,
     dctx_all, ds_all, soft_all, small_low, sems) = refs[6:]
    core_even = place[0] == 0
    early = place[1] == 0
    rows, width = x.shape
    groups = width // GROUP
    row = row_number(place, slot, count, True)
    busy = jnp.logical_and(early, slot >= 1) | jnp.logical_and(jnp.logical_not(early), slot < count)
    small_out[...] = jnp.zeros(small_out.shape, F32)

    @pl.when(busy)
    def _():
        get_g = fetch(early, back_row, cotangent.at[row], grad_y, sems.at[4])
        get_slope = fetch(early, slope_a, slope_b, slope, sems.at[5])
        (att_gain, att_shift, _), (mlp_gain, mlp_shift, _) = vectors(core_even, vecs)
        settle(place, get_g)

        def pack(source, start, to_even, sem):
            spot = (pl.ds(0, rows), pl.ds(start, source.shape[1]))
            if to_even:
                return deliver(core_even, source, pack_keep.at[spot], pack_send.at[spot], sem)
            return deliver(core_even, source, pack_send.at[spot], pack_keep.at[spot], sem)

        hidden = dhid.shape[1]
        last = 2 * width + hidden
        puts = [
            start_copy(grad_y, pack_keep.at[pl.ds(0, rows), pl.ds(last, width)], sems.at[11]),
            start_copy(grad_y, pack_send.at[pl.ds(0, rows), pl.ds(last, width)], sems.at[20]),
        ]
        small_out[5:6] = jnp.sum(grad_y[...].astype(F32), 0, keepdims=True)
        settle(place, get_slope)
        get_mid = fetch(early, mid_a, mid_b, mid, sems.at[6])
        get_soft = fetch(early, soft_a, soft_b, soft, sems.at[9])
        get_qkv = fetch(early, qkv_a, qkv_b, qkv, sems.at[8])
        get_ctx = fetch(early, ctx_a, ctx_b, ctx, sems.at[10])
        get_x = fetch(early, x_a, x_b, x, sems.at[7])
        half = hidden // 2
        for side in range(2):
            cols = pl.ds(side * half, half)
            low = (dot_nt(grad_y[...], w_down[cols, :]) * slope[:, cols].astype(F32)).astype(BF16)
            dhid[:, cols] = low
            sums = jnp.sum(low.astype(F32), 0, keepdims=True)
            for part in range(half // width):
                number = 10 + side * (half // width) + part
                small_out[number : number + 1] = sums[:, part * width : (part + 1) * width]
        puts.append(pack(dhid, 2 * width, False, sems.at[12]))
        settle(place, get_mid)
        dnorm = dot_nt(dhid[...], w_up[...])
        hat, scale = norm_parts(mid[...].astype(F32))
        normed_mlp[...] = (hat * mlp_gain + mlp_shift).astype(BF16)
        puts.append(pack(normed_mlp, 0, False, sems.at[13]))
        puts.append(pack(normed_mlp, width, False, sems.at[21]))
        small_out[8:9] = jnp.sum(dnorm * hat, 0, keepdims=True)
        small_out[9:10] = jnp.sum(dnorm, 0, keepdims=True)
        u = dnorm * mlp_gain
        grad = grad_y[...].astype(F32) + scale * (
            u - jnp.mean(u, -1, keepdims=True) - hat * jnp.mean(u * hat, -1, keepdims=True)
        )
        low = grad.astype(BF16)
        gmid[...] = low
        puts.append(pack(gmid, 2 * width + 3 * width, True, sems.at[14]))
        puts.append(deliver(core_even, gmid, send_out, keep_out, sems.at[15]))
        small_out[4:5] = jnp.sum(low.astype(F32), 0, keepdims=True)
        settle(place, get_qkv, get_soft, get_ctx)
        puts.append(pack(ctx, width, True, sems.at[22]))
        dctx_all[...] = dot_nt(gmid[...], w_att[:, 3 * width :]).astype(BF16)
        heads = GROUP // 64

        def group_step(group, carry):
            cols = columns(group, GROUP)
            k_cols = pl.ds(pl.multiple_of(width + group * GROUP, GROUP), GROUP)
            v_cols = pl.ds(pl.multiple_of(2 * width + group * GROUP, GROUP), GROUP)
            dctx = dctx_all[:, cols]
            q = qkv[:, cols]
            k = qkv[:, k_cols]
            v = qkv[:, v_cols]
            product = dctx.astype(F32) * ctx[:, cols].astype(F32)
            masks = [head_mask(rows, head) for head in range(heads)]
            mine = jnp.concatenate([jnp.where(mask, dctx, 0) for mask in masks], 0)
            dp = dot_nt(mine, v)
            dq = jnp.zeros((rows, GROUP), F32)
            for head in range(heads):
                span = pl.ds(head * rows, rows)
                weight = soft[group * heads + head]
                delta = jnp.sum(jnp.where(masks[head], product, 0.0), -1, keepdims=True)
                ds = (weight.astype(F32) * (dp[head * rows : (head + 1) * rows] - delta)).astype(BF16)
                ds_all[span] = ds
                soft_all[span] = weight
                dq = dq + dot_nn(ds, jnp.where(masks[head], k, 0))
            dk = dot_tn(ds_all[...], jnp.concatenate([jnp.where(mask, q, 0) for mask in masks], 0))
            dv = dot_tn(soft_all[...], mine)
            dq_low = (dq * 0.125).astype(BF16)
            dv_low = dv.astype(BF16)
            dqkv[:, cols] = dq_low
            dqkv[:, k_cols] = dk.astype(BF16)
            dqkv[:, v_cols] = dv_low
            small_out[2:3, cols] = jnp.sum(dq_low.astype(F32), 0, keepdims=True)
            small_out[3:4, cols] = jnp.sum(dv_low.astype(F32), 0, keepdims=True)
            return carry

        lax.fori_loop(0, groups, group_step, 0)
        puts.append(pack(dqkv, 2 * width, True, sems.at[16]))
        settle(place, get_x)
        dnorm = dot_nt(dqkv[...], w_att[:, : 3 * width])
        hat, scale = norm_parts(x[...].astype(F32))
        normed_att[...] = (hat * att_gain + att_shift).astype(BF16)
        puts.append(pack(normed_att, 0, True, sems.at[17]))
        small_out[0:1] = jnp.sum(dnorm * hat, 0, keepdims=True)
        small_out[1:2] = jnp.sum(dnorm, 0, keepdims=True)
        u = dnorm * att_gain
        grad = gmid[...].astype(F32) + scale * (
            u - jnp.mean(u, -1, keepdims=True) - hat * jnp.mean(u * hat, -1, keepdims=True)
        )
        gx[...] = grad.astype(BF16)
        puts.append(start_copy(gx, grad_x_out, sems.at[18]))
        puts.append(deliver(core_even, gx, keep_out, send_out, sems.at[19]))
        token = jnp.sum(jnp.where(upright(flags[pl.ds(row, 1)], 128) == 1.0, grad, 0.0), 0, keepdims=True)
        small_out[6:7] = token
        small_out[14:15] = token
        theirs = jnp.where(core_even, small_out[8:16], small_out[0:8])
        high = theirs.astype(BF16)
        small_low[...] = jnp.concatenate([high, (theirs - high.astype(F32)).astype(BF16)], 0)
        puts.append(start_copy(small_low, pack_send.at[pl.ds(rows, 16), pl.ds(0, width)], sems.at[23]))
        for put in puts:
            put.wait()


def backward_call(slot, place, cotangent, back_row, flags, vecs, weights, saved_early, saved_late):
    rows, width = back_row.shape
    hidden = weights[0].shape[1]
    low = lambda *shape: jax.ShapeDtypeStruct(shape, BF16)
    row = low(rows, width)
    pack = low(rows + 16, 3 * width + hidden)
    weights = [pltpu.with_memory_space_constraint(array, pltpu.VMEM) for array in weights]
    outs = [row, row, row, jax.ShapeDtypeStruct((16, width), F32), pack, pack]
    specs = [ANY] * len(outs)
    specs[3] = VMEM
    v = pltpu.VMEM
    return pl.pallas_call(
        partial(backward_kernel, slot, cotangent.shape[0] // 2),
        out_shape=outs,
        in_specs=[SMEM, ANY, ANY] + [VMEM] * 10 + [ANY] * 12,
        out_specs=specs,
        scratch_shapes=[
            v((rows, width), BF16), v((rows, width), BF16), v((rows, width), BF16),
            v((rows, 3 * width), BF16), v((HEADS, rows, rows), BF16), v((rows, width), BF16), v((rows, hidden), BF16),
            v((rows, width), BF16), v((rows, width), BF16), v((rows, 3 * width), BF16), v((rows, hidden), BF16),
            v((rows, width), BF16), v((rows, width), BF16), v((rows, width), BF16),
            v((GROUP // 64 * rows, rows), BF16), v((GROUP // 64 * rows, rows), BF16),
            v((16, width), BF16), pltpu.SemaphoreType.DMA((24,)),
        ],
        compiler_params=pltpu.CompilerParams(vmem_limit_bytes=VMEM_LIMIT),
        cost_estimate=pl.CostEstimate(flops=8_000_000_000, bytes_accessed=34_000_000, transcendentals=1_000),
        name="row_backward",
    )(place, cotangent, back_row, flags, *vecs, *weights, *in_hbm(saved_early), *in_hbm(saved_late))


def weight_kernel(first_row, last_row, tall_rows, short_rows, place, token, *refs):
    sources, refs = refs[:10], refs[10:]
    if not first_row:
        before, refs = refs[:3], refs[3:]
    made = len(refs) - 13
    outs, refs = refs[:made], refs[made:]
    (left, right, act, grad_y, turned, part_t, grad_first, grad_half, mine, theirs, summed, small_low, sems) = refs
    early = place[1] == 0
    rows = left.shape[0] // 2
    hidden = right.shape[1]
    width = grad_y.shape[1]
    quarter = grad_half.shape[1]
    tall = pl.ds(pl.multiple_of(place[2] * place[3], 16), width)
    short = pl.ds(pl.multiple_of(place[2] * place[4], 16), quarter)
    core_even = place[0] == 0
    get_mine = fetch(early, sources[4], sources[9], mine, sems.at[10])
    spot = (pl.ds(rows, 16), pl.ds(0, width))
    get_theirs = fetch(early, sources[1].at[spot], sources[6].at[spot], theirs, sems.at[11])
    if not first_row:
        old_small = start_copy(before[2], summed, sems.at[12])
    waits = []
    for index, (first, second) in enumerate(zip(sources[2:4], sources[7:9])):
        waits.append(fetch(early, first, second, act.at[pl.ds(index * rows, rows)], sems.at[index]))
    start = 0
    pieces = []
    for number, target in enumerate((left, right, grad_y)):
        span = pl.ds(start, target.shape[1])
        start += target.shape[1]
        pieces.append([(first.at[pl.ds(0, rows), span], second.at[pl.ds(0, rows), span], target.at[pl.ds(index * rows, rows)], sems.at[2 + 2 * number + index])
                       for index, (first, second) in enumerate(zip(sources[:2], sources[5:7]))])
    waits += [fetch(early, *piece) for piece in pieces[2]]
    if not first_row:
        old_half = start_copy(before[1], grad_half, sems.at[8])
    waits_left = [fetch(early, *piece) for piece in pieces[0]]
    waits_right = [fetch(early, *piece) for piece in pieces[1]]
    if not first_row:
        old_first = start_copy(before[0], grad_first, sems.at[9])
    puts = []
    settle(place, get_mine, get_theirs, *([] if first_row else [old_small]))
    ours = jnp.where(core_even, mine[0:8], mine[8:16]) + theirs[0:8].astype(F32) + theirs[8:16].astype(F32)
    summed[...] = ours if first_row else ours + summed[...]
    if last_row:
        lines = lax.broadcasted_iota(jnp.int32, summed.shape, 0)
        summed[...] = jnp.where((lines == 6) & jnp.logical_not(early), token[...], summed[...])
        small_low[...] = jnp.concatenate([summed[...], jnp.zeros(summed.shape, F32)], 0).astype(BF16)
        if tall_rows:
            for index in range(width // tall_rows):
                target = outs[3 + index].at[pl.ds(tall_rows + short_rows, 16)]
                puts.append(start_copy(small_low, target, sems.at[14 + index]))
    puts.append(start_copy(summed, outs[2], sems.at[13]))

    def total(target, index, value):
        if not first_row:
            value = value + target[index].astype(F32)
        target[index] = value.astype(BF16)

    settle(place, *waits, *([] if first_row else [old_half]))

    def half_step(part, carry):
        flipped = act[:, columns(part, quarter)].T
        part_t[part, pl.ds(0, quarter)] = flipped
        part_t[part, pl.ds(quarter, quarter)] = flipped
        return carry

    lax.fori_loop(0, 4, half_step, 0)
    value = dot_nn(jnp.concatenate([part_t[part, short] for part in range(4)], 0), grad_y[...])
    for part in range(4):
        total(grad_half, part, value[part * quarter : (part + 1) * quarter])
    chunks = width // tall_rows if tall_rows else 0

    def ship(source, part, start, sem):
        if not chunks:
            return [start_copy(source.at[part], outs[3 + part].at[pl.ds(start, source.shape[1])], sems.at[sem + part])]
        size = source.shape[1] // chunks
        return [
            start_copy(
                source.at[part, pl.ds(index * size, size)],
                outs[3 + part * chunks + index].at[pl.ds(start // chunks, size)],
                sems.at[sem + part * chunks + index],
            )
            for index in range(chunks)
        ]

    if last_row:
        for part in range(4):
            puts += ship(grad_half, part, width, 14 + chunks)
    if not last_row:
        puts.append(start_copy(grad_half, outs[1], sems.at[14]))
    settle(place, *waits_left)

    settle(place, *waits_right, *([] if first_row else [old_first]))

    def turn_step(side, carry):
        flipped = left[:, columns(side, width)].T
        turned[side, pl.ds(0, width)] = flipped
        turned[side, pl.ds(width, width)] = flipped
        return carry

    lax.fori_loop(0, 2, turn_step, 0)
    value = dot_nn(turned[0, tall], right[:, : 3 * width])
    for part in range(3):
        total(grad_first, part, value[:, part * width : (part + 1) * width])
    total(grad_first, 3, dot_nn(turned[1, tall], right[:, 3 * width :]))
    if last_row:
        for part in range(4):
            puts += ship(grad_first, part, 0, 14 + chunks + 4 * max(chunks, 1))
    if not last_row:
        puts.append(start_copy(grad_first, outs[0], sems.at[15]))
    for put in puts:
        put.wait()


def weight_call(place, token, early_row, late_row, before, last_row, members):
    rows, half = early_row[2].shape
    hidden = 2 * half
    width = (early_row[0].shape[1] - hidden) // 3
    quarter = half // 4
    low = lambda *shape: jax.ShapeDtypeStruct(shape, BF16)
    tall, short = aligned_chunk(width, quarter, members)
    sums = jax.ShapeDtypeStruct((8, width), F32)
    outs = [low(4, width, width), low(4, quarter, width), sums]
    if last_row:
        outs = [
            pltpu.HBM((members, width // members, hidden), F32),
            pltpu.HBM((4, members, quarter // members, width), F32),
            sums,
        ]
        outs += [low(tall + short + 16, width)] * members + [low(tall + short, width)] * (3 * members) if tall else [low(width + quarter, width)] * 4
    v = pltpu.VMEM
    return pl.pallas_call(
        partial(weight_kernel, before is None, last_row, tall, short),
        out_shape=outs,
        in_specs=[SMEM, VMEM] + [ANY] * (10 if before is None else 13),
        out_specs=[ANY] * len(outs),
        scratch_shapes=[
            v((2 * rows, 2 * width), BF16), v((2 * rows, hidden), BF16), v((2 * rows, half), BF16),
            v((2 * rows, width), BF16), v((2, 2 * width, 2 * rows), BF16), v((4, 2 * quarter, 2 * rows), BF16),
            v((4, width, width), BF16), v((4, quarter, width), BF16),
            v((16, width), F32), v((16, width), BF16), v((8, width), F32), v((16, width), BF16),
            pltpu.SemaphoreType.DMA((24 + 9 * members,)),
        ],
        compiler_params=pltpu.CompilerParams(vmem_limit_bytes=(60 if last_row else 42) * MIB),
        cost_estimate=pl.CostEstimate(flops=8_000_000_000, bytes_accessed=24_000_000, transcendentals=0),
        name="weight_gradients",
    )(place, token, *in_hbm(early_row), *in_hbm(late_row), *in_hbm(before or ()))


def aligned_chunk(width, quarter, members):
    tall, short = width // members, quarter // members
    return (tall, short) if tall % 16 == 0 and short % 16 == 0 else (0, 0)


def ring_order(members):
    return list(range(0, members, 2)) + list(range(members - 1, 0, -2))


def ring_reduce(own, matrix, half, position, axis, pending):
    members = lax.axis_size(axis)
    order = ring_order(members)
    ahead = [(order[i], order[(i + 1) % members]) for i in range(members)]
    behind = [(b, a) for a, b in ahead]
    parts = len(own)
    tall, width = matrix.shape[1], half.shape[3]
    short = half.shape[2]
    steps = [1 - 2 * (part % 2) for part in range(parts)]

    def piece(array, index):
        cut = lambda start, size: lax.dynamic_slice_in_dim(array, start, size, 0)
        if isinstance(index, int):
            cut = lambda start, size: lax.slice_in_dim(array, start, start + size, axis=0)
        return jnp.concatenate([cut(index * tall, tall), cut(width + index * short, short)], 0).astype(F32)

    def chunk(part, number):
        index = (members - steps[part] * number) % members
        return own[part][index].astype(F32) if isinstance(own[part], (list, tuple)) else piece(own[part], index)

    def shift(part, value):
        return lax.ppermute(value, axis, ahead if part % 2 == 0 else behind)

    def reduce_step(number, current):
        moved = [shift(part, current[part]) for part in range(parts)]
        return [(moved[part].astype(F32) + chunk(part, number)).astype(BF16) for part in range(parts)]

    def place_chunks(number, current, matrix, half):
        for part in range(parts):
            index = lax.rem(position + jnp.uint32(members) + jnp.uint32(steps[part] % members) * (
                jnp.uint32(members + 1) - jnp.uint32(number)), jnp.uint32(members))
            wide = current[part].astype(F32)
            zero, block = jnp.uint32(0), jnp.uint32(part)
            matrix = lax.dynamic_update_slice(matrix, wide[None, :tall], (index, zero, jnp.uint32(part * width)))
            half = lax.dynamic_update_slice(half, wide[None, None, tall:], (block, index, zero, zero))
        return matrix, half

    def gather_step(number, carry):
        current, matrix, half = carry
        current = [shift(part, current[part]) for part in range(parts)]
        return (current, *place_chunks(number, current, matrix, half))

    current = [chunk(part, 0).astype(BF16) for part in range(parts)]
    extra = current[0]
    if members > 8:
        current = lax.fori_loop(1, members, reduce_step, current)
        carry = lax.fori_loop(1, members, gather_step, (current, *place_chunks(0, current, matrix, half)))
    else:
        for number in range(1, members):
            current = reduce_step(number, current)
        extra = current[0][tall + short :]
        current[0] = current[0][: tall + short]
        carry = (current, *place_chunks(0, current, matrix, half))
        for number in range(1, members):
            carry = gather_step(number, carry)
            if number in (1, 3):
                which = number // 2
                pending[which] = lax.optimization_barrier((pending[which], carry[0][0]))[0]
    return carry[1].reshape(tall * members, parts * width), carry[2].reshape(parts * short * members, width), extra, pending


def turn_rows(array, width, position, members):
    top = jnp.roll(array[:width], -position * (width // members), 0)
    return jnp.concatenate([top, jnp.roll(array[width:], -position * ((array.shape[0] - width) // members), 0)], 0)


def shards(
    patches, cotangent, mask_flags, segments, mask_token, norm_gains, norm_shifts, w_first, first_bias, down_half
):
    section = lax.axis_index("section")
    core = section & 1
    stage = section >> 1
    early = stage == 0
    swap = [(0, 1), (1, 0), (2, 3), (3, 2)]
    forth = [(0, 2), (1, 3)]
    back = [(2, 0), (3, 1)]
    row_count, rows, width = patches.shape
    count = row_count // 2
    members = lax.axis_size("dp")
    place_of = np.zeros(members, np.int32)
    for spot, member in enumerate(ring_order(members)):
        place_of[member] = spot
    position = jnp.asarray(place_of)[lax.axis_index("dp").astype(jnp.uint32)]

    first_own, half_own = w_first[0], down_half[0]
    hidden = first_own.shape[1]
    quarter = hidden // 8
    tall, short = width // members, quarter // members
    aligned = aligned_chunk(width, quarter, members)[0] > 0
    first_other = lax.ppermute(first_own, "section", swap)
    half_other = lax.ppermute(half_own, "section", swap)
    own_vecs = (norm_gains, norm_shifts, first_bias)
    vecs = own_vecs + tuple(lax.ppermute(array, "section", swap) for array in own_vecs)
    weights = (first_own, first_other, half_own, half_other)
    turns = position if aligned else 0 * position
    place = jnp.stack([core, stage, turns, jnp.int32(16 * (tall // 16)), jnp.int32(16 * (short // 16))]).astype(jnp.int32)
    token = mask_token[None]

    forwards, acts, packs = [], [], []
    sent = patches[0]
    for slot in range(count + 1):
        result = forward_call(slot, place, patches, sent, mask_flags, segments, token, vecs, weights)
        forwards.append(result)
        if slot < count:
            sent = lax.ppermute(result[2], "section", forth)
        acts.append(lax.ppermute(result[9], "section", swap))
        if slot == 0:
            weights = hold_call(place, lax.optimization_barrier((weights, result[2]))[0])

    def assemble(pairs):
        chosen = [jnp.where(early, a, b) for a, b in pairs]
        keep, send = jnp.stack(chosen[0::2]), jnp.stack(chosen[1::2])
        received = lax.ppermute(send, "section", swap)
        return jnp.where(
            core == 0, jnp.concatenate([keep, received], 0), jnp.concatenate([received, keep], 0)
        )

    backs = []
    returned = patches[0]
    grads = None
    for slot in range(count + 1):
        saved = [
            [forwards[which][i] for i in (3, 4, 5, 6, 7, 10)] for which in (max(slot - 1, 0), min(slot + 1, count))
        ]
        backs.append(backward_call(slot, place, cotangent, returned, mask_flags, vecs, weights, *saved))
        if slot < count:
            returned = lax.ppermute(backs[slot][2], "section", back)
            if slot == 0:
                returned, acts[:2] = lax.optimization_barrier((returned, acts[:2]))
        packs.append(lax.ppermute(backs[slot][5], "section", swap))
        if slot > 0:
            row = slot - 1
            chosen = [
                (backs[b][4], packs[b], forwards[f][8], acts[f], backs[b][3]) for f, b in ((row, row + 1), (row + 1, row))
            ]
            total = sum(backs[b][3][6:7] for b in range(1, slot + 1))
            if row == count - 1:
                cross = [(0, 3), (1, 2)]
                total = lax.ppermute(total, "section", forth) + lax.ppermute(total, "section", cross)
            grads = weight_call(place, total, *chosen, grads, row == count - 1, members)
            if row < count - 1:
                returned, grads, acts = lax.optimization_barrier((returned, grads, acts))

    blank, small = grads[:2], grads[2]
    if aligned:
        own = [grads[3 + part * members : 3 + (part + 1) * members] for part in range(4)]
    else:
        own = [turn_rows(array, width, position, members) for array in grads[3:]]
        small = lax.psum(small, "dp")

    pending = [
        [(forwards[row][i], forwards[row + 1][i]) for row in range(count) for i in (0, 1)],
        [(backs[row + 1][i], backs[row][i]) for row in range(count) for i in (0, 1)],
    ]
    grad_first, grad_half, extra, pending = ring_reduce(own, *blank, position.astype(jnp.uint32), "dp", pending)
    if aligned:
        small = extra[:8].astype(F32)
    token_grad = small[6]

    finals = assemble(pending[0])
    back_rows = assemble(pending[1]).astype(F32)
    back_rows = jnp.where((section == 0) & (mask_flags[..., None] == 1), 0.0, back_rows)
    return (
        finals[None],
        back_rows[None],
        token_grad,
        small[0:1],
        small[1:2],
        grad_first[None],
        small[2:6].reshape(1, hidden),
        grad_half[None],
    )


def solution(mesh):
    return jax.shard_map(
        shards,
        mesh=mesh,
        in_specs=(
            P("dp", None, None),
            P("dp", None, None),
            P("dp", None),
            P("dp", None),
            P(),
            P("section", None),
            P("section", None),
            P("section", None, None),
            P("section", None),
            P("section", None, None),
        ),
        out_specs=(
            P("section", "dp", None, None),
            P("section", "dp", None, None),
            P(),
            P("section", None),
            P("section", None),
            P("section", None, None),
            P("section", None),
            P("section", None, None),
        ),
        check_vma=False,
    )
```

```python
from functools import partial

import jax
import jax.numpy as jnp
import numpy as np
from jax import lax
from jax.experimental import pallas as pl
from jax.experimental.pallas import tpu as pltpu
from jax.sharding import PartitionSpec as P

HEADS = 12
EPSILON = 1e-06
NEGATIVE = -1000000000.0
GROUP = 256
TILE = 768
MIB = 1024 * 1024
VMEM_LIMIT = 49 * MIB
BF16 = jnp.bfloat16
F32 = jnp.float32
ANY = pl.BlockSpec(memory_space=pl.ANY)
SMEM = pl.BlockSpec(memory_space=pltpu.SMEM)
VMEM = pl.BlockSpec(memory_space=pltpu.VMEM)


def dot_nn(a, b):
    return jnp.dot(a, b, preferred_element_type=F32)


def dot_nt(a, b):
    return lax.dot_general(a, b, (((1,), (1,)), ((), ())), preferred_element_type=F32)


def dot_tn(a, b):
    return lax.dot_general(a, b, (((0,), (0,)), ((), ())), preferred_element_type=F32)


def fetch(choice, first, second, target, sem):
    @pl.when(choice)
    def _():
        pltpu.make_async_copy(first, target, sem).start()

    @pl.when(jnp.logical_not(choice))
    def _():
        pltpu.make_async_copy(second, target, sem).start()

    return pltpu.make_async_copy(first, target, sem)


def deliver(choice, source, first, second, sem):
    @pl.when(choice)
    def _():
        pltpu.make_async_copy(source, first, sem).start()

    @pl.when(jnp.logical_not(choice))
    def _():
        pltpu.make_async_copy(source, second, sem).start()

    return pltpu.make_async_copy(source, first, sem)


def start_copy(source, target, sem):
    copy = pltpu.make_async_copy(source, target, sem)
    copy.start()
    return copy


def settle(place, *copies):
    @pl.when(place[0] >= 0)
    def _():
        for copy in copies:
            copy.wait()


def norm_parts(x):
    centred = x - jnp.mean(x, -1, keepdims=True)
    scale = lax.rsqrt(jnp.mean(centred * centred, -1, keepdims=True) + EPSILON)
    return centred * scale, scale


def gelu_pair(hidden):
    base = 1.0 + 0.23164189 * jnp.abs(hidden)
    t = pl.reciprocal(base, approx=True)
    t = t * (2.0 - base * t)
    poly = ((((0.5307027145 * t - 0.7265760135) * t + 0.7107068705) * t - 0.142248368) * t + 0.127414796) * t
    fall = jnp.exp2(hidden * hidden * -0.7213475204444817)
    tail = poly * fall
    cdf = jnp.where(hidden >= 0, 1.0 - tail, tail)
    return hidden * cdf, cdf + hidden * fall * 0.3989422804014327


def columns(index, width):
    return pl.ds(pl.multiple_of(index * width, width), width)


def head_mask(rows, head):
    lane = lax.broadcasted_iota(jnp.int32, (rows, GROUP), 1)
    return (lane >= head * 64) & (lane < head * 64 + 64)


def load_down(core_even, half_own, half_other, w_down, sems):
    half = half_own.shape[0]
    low = fetch(core_even, half_own, half_other, w_down.at[pl.ds(0, half)], sems.at[2])
    high = fetch(core_even, half_other, half_own, w_down.at[pl.ds(half, half)], sems.at[3])
    return low, high


def vectors(core_even, refs):
    own, other = refs[:3], refs[3:]
    att = [jnp.where(core_even, a[...].astype(F32), b[...].astype(F32)) for a, b in zip(own, other)]
    mlp = [jnp.where(core_even, b[...].astype(F32), a[...].astype(F32)) for a, b in zip(own, other)]
    return att, mlp


def upright(row, width):
    return jnp.broadcast_to(row.astype(F32), (width, row.shape[1])).T[:, :1]


def in_hbm(arrays):
    return [pltpu.with_memory_space_constraint(array, pltpu.HBM) for array in arrays]


def row_number(place, slot, count, backward):
    late = place[1]
    number = slot - (1 - late) if backward else slot - late
    return place[0] * count + jnp.clip(number, 0, count - 1)


def forward_kernel(
    slot, count, held, place, patches, sent_row, flags, segments, token, *refs
):
    vecs, refs = refs[:6], refs[6:]
    if held:
        (w_att, w_up, w_down), refs = refs[:3], refs[3:]
    else:
        (first_own, first_other, half_own, half_other), refs = refs[:4], refs[4:]
    (keep_out, send_out, y_mlp_out, x_out, mid_out, qkv_out, soft_out, ctx_out, act_keep_out, act_send_out,
     slope_out, x, bias, normed, qkv, soft, ctx, mid, act, slope, y_mlp, sems) = refs[:22]
    if not held:
        w_att, w_up, w_down = refs[22:]
    core_even = place[0] == 0
    early = place[1] == 0
    rows, width = x.shape
    groups = width // GROUP
    row = row_number(place, slot, count, False)
    get_x = fetch(early, patches.at[row], sent_row, x, sems.at[4])
    if not held:
        get_att = fetch(core_even, first_own, first_other, w_att, sems.at[0])
    (att_gain, att_shift, att_bias), (mlp_gain, mlp_shift, mlp_bias) = vectors(core_even, vecs)
    seg = segments[pl.ds(row, 1)]
    bias[...] = jnp.where(upright(seg, 128) == seg.astype(F32), 0.0, NEGATIVE)
    settle(place, get_x)

    @pl.when(early)
    def _():
        flag = upright(flags[pl.ds(row, 1)], 128)
        x[...] = jnp.where(flag == 1.0, token[...].astype(F32), x[...].astype(F32)).astype(BF16)

    puts = [start_copy(x, x_out, sems.at[5])]
    hat, _ = norm_parts(x[...].astype(F32))
    normed[...] = (hat * att_gain + att_shift).astype(BF16)
    if not held:
        settle(place, get_att)
        get_up = fetch(core_even, first_other, first_own, w_up, sems.at[1])
        get_low, get_high = load_down(core_even, half_own, half_other, w_down, sems)
    projected = dot_nn(normed[...], w_att[:, : 3 * width])
    q_low = (projected[:, :width] + att_bias[:, :width]).astype(BF16)
    qkv[:, :width] = (q_low * 0.125).astype(BF16)
    qkv[:, width : 2 * width] = projected[:, width : 2 * width].astype(BF16)
    qkv[:, 2 * width :] = (projected[:, 2 * width :] + att_bias[:, width : 2 * width]).astype(BF16)
    puts.append(start_copy(qkv, qkv_out, sems.at[6]))
    heads = GROUP // 64
    for group in range(groups):
        cols = pl.ds(group * GROUP, GROUP)
        q = qkv[:, cols]
        k = qkv[:, pl.ds(width + group * GROUP, GROUP)]
        v = qkv[:, pl.ds(2 * width + group * GROUP, GROUP)]
        masks = [head_mask(rows, head) for head in range(heads)]
        scores = dot_nt(jnp.concatenate([jnp.where(mask, q, 0) for mask in masks], 0), k)
        total = jnp.zeros((rows, GROUP), F32)
        for head in range(heads):
            mine = scores[head * rows : (head + 1) * rows] + bias[...]
            raised = jnp.exp(mine - jnp.max(mine, -1, keepdims=True))
            weight = (raised * (1.0 / jnp.sum(raised, -1, keepdims=True))).astype(BF16)
            soft[group * heads + head] = weight
            total = total + dot_nn(weight, jnp.where(masks[head], v, 0))
        ctx[:, cols] = total.astype(BF16)
        span = pl.ds(group * heads, heads)
        puts.append(start_copy(soft.at[span], soft_out.at[span], sems.at[17 + group]))
    puts.append(start_copy(ctx, ctx_out, sems.at[8]))
    y = x[...].astype(F32) + dot_nn(ctx[...], w_att[:, 3 * width :]) + att_bias[:, 2 * width : 3 * width]
    low = y.astype(BF16)
    mid[...] = low
    puts.append(start_copy(mid, mid_out, sems.at[9]))
    puts.append(deliver(core_even, mid, keep_out, send_out, sems.at[10]))
    hat, _ = norm_parts(low.astype(F32))
    normed[...] = (hat * mlp_gain + mlp_shift).astype(BF16)
    if not held:
        settle(place, get_up)
    half = act.shape[1] // 2
    for side in range(2):
        cols = pl.ds(side * half, half)
        hidden = dot_nn(normed[...], w_up[:, cols]) + mlp_bias[:, side * half : (side + 1) * half]
        active, rate = gelu_pair(hidden)
        act[:, cols] = active.astype(BF16)
        slope[:, cols] = rate.astype(BF16)
        targets = (act_send_out, act_keep_out) if side else (act_keep_out, act_send_out)
        puts.append(deliver(core_even, act.at[:, cols], *targets, sems.at[11 + side]))
        puts.append(start_copy(slope.at[:, cols], slope_out.at[:, cols], sems.at[13 + side]))
    if not held:
        settle(place, get_low, get_high)
    y = mid[...].astype(F32) + dot_nn(act[...], w_down[...]) + att_bias[:, 3 * width :]
    y_mlp[...] = y.astype(BF16)
    puts.append(start_copy(y_mlp, y_mlp_out, sems.at[15]))
    puts.append(deliver(core_even, y_mlp, send_out, keep_out, sems.at[16]))
    for put in puts:
        put.wait()


def hold_kernel(place, first_own, first_other, half_own, half_other, w_att, w_up, w_down, sems):
    core_even = place[0] == 0
    copies = [
        fetch(core_even, first_own, first_other, w_att, sems.at[0]),
        fetch(core_even, first_other, first_own, w_up, sems.at[1]),
        *load_down(core_even, half_own, half_other, w_down, sems),
    ]
    for copy in copies:
        copy.wait()


def hold_call(place, weights):
    width, hidden = weights[0].shape
    v = pltpu.VMEM
    return pl.pallas_call(
        hold_kernel,
        out_shape=[v((width, hidden), BF16), v((width, hidden), BF16), v((hidden, width), BF16)],
        in_specs=[SMEM] + [ANY] * 4,
        out_specs=[VMEM] * 3,
        scratch_shapes=[pltpu.SemaphoreType.DMA((4,))],
        compiler_params=pltpu.CompilerParams(vmem_limit_bytes=VMEM_LIMIT),
        cost_estimate=pl.CostEstimate(flops=0, bytes_accessed=14_000_000, transcendentals=0),
        name="hold_weights",
    )(place, *weights)


def forward_call(slot, place, patches, sent_row, flags, segments, token, vecs, weights):
    rows, width = sent_row.shape
    held = len(weights) == 3
    if held:
        weights = [pltpu.with_memory_space_constraint(array, pltpu.VMEM) for array in weights]
    hidden = weights[0].shape[1]
    low = lambda *shape: jax.ShapeDtypeStruct(shape, BF16)
    row = low(rows, width)
    outs = [row, row, row, row, row, low(rows, 3 * width), low(HEADS, rows, rows), row]
    outs += [low(rows, hidden // 2), low(rows, hidden // 2), low(rows, hidden)]
    v = pltpu.VMEM
    return pl.pallas_call(
        partial(forward_kernel, slot, patches.shape[0] // 2, held),
        out_shape=outs,
        in_specs=[SMEM, ANY, ANY] + [VMEM] * 9 + ([VMEM] * 3 if held else [ANY] * 4),
        out_specs=[ANY] * len(outs),
        scratch_shapes=[
            v((rows, width), BF16), v((rows, rows), F32), v((rows, width), BF16),
            v((rows, 3 * width), BF16), v((HEADS, rows, rows), BF16), v((rows, width), BF16), v((rows, width), BF16),
            v((rows, hidden), BF16), v((rows, hidden), BF16), v((rows, width), BF16),
            pltpu.SemaphoreType.DMA((20,)),
        ]
        + ([] if held else [v((width, hidden), BF16), v((width, hidden), BF16), v((hidden, width), BF16)]),
        compiler_params=pltpu.CompilerParams(vmem_limit_bytes=VMEM_LIMIT if held else 60 * MIB),
        cost_estimate=pl.CostEstimate(flops=7_000_000_000, bytes_accessed=26_000_000, transcendentals=2_500_000),
        name="row_forward",
    )(place, patches, sent_row, flags, segments, token, *vecs, *weights)


def backward_kernel(slot, count, place, cotangent, back_row, flags, *refs):
    vecs = refs[:6]
    (w_att, w_up, w_down,
     x_a, mid_a, qkv_a, soft_a, ctx_a, slope_a, x_b, mid_b, qkv_b, soft_b, ctx_b, slope_b,
     keep_out, send_out, grad_x_out, small_out, pack_keep, pack_send,
     grad_y, x, mid, qkv, soft, ctx, slope, normed_att, normed_mlp, dqkv, dhid, gmid, gx,
     dctx_all, ds_all, soft_all, small_low, sems) = refs[6:]
    core_even = place[0] == 0
    early = place[1] == 0
    rows, width = x.shape
    groups = width // GROUP
    row = row_number(place, slot, count, True)
    busy = jnp.logical_and(early, slot >= 1) | jnp.logical_and(jnp.logical_not(early), slot < count)
    small_out[...] = jnp.zeros(small_out.shape, F32)

    @pl.when(busy)
    def _():
        get_g = fetch(early, back_row, cotangent.at[row], grad_y, sems.at[4])
        get_slope = fetch(early, slope_a, slope_b, slope, sems.at[5])
        (att_gain, att_shift, _), (mlp_gain, mlp_shift, _) = vectors(core_even, vecs)
        settle(place, get_g)

        def pack(source, start, to_even, sem):
            spot = (pl.ds(0, rows), pl.ds(start, source.shape[1]))
            if to_even:
                return deliver(core_even, source, pack_keep.at[spot], pack_send.at[spot], sem)
            return deliver(core_even, source, pack_send.at[spot], pack_keep.at[spot], sem)

        hidden = dhid.shape[1]
        last = 2 * width + hidden
        puts = [
            start_copy(grad_y, pack_keep.at[pl.ds(0, rows), pl.ds(last, width)], sems.at[11]),
            start_copy(grad_y, pack_send.at[pl.ds(0, rows), pl.ds(last, width)], sems.at[20]),
        ]
        small_out[5:6] = jnp.sum(grad_y[...].astype(F32), 0, keepdims=True)
        settle(place, get_slope)
        get_mid = fetch(early, mid_a, mid_b, mid, sems.at[6])
        get_soft = fetch(early, soft_a, soft_b, soft, sems.at[9])
        get_qkv = fetch(early, qkv_a, qkv_b, qkv, sems.at[8])
        get_ctx = fetch(early, ctx_a, ctx_b, ctx, sems.at[10])
        get_x = fetch(early, x_a, x_b, x, sems.at[7])
        half = hidden // 2
        for side in range(2):
            cols = pl.ds(side * half, half)
            low = (dot_nt(grad_y[...], w_down[cols, :]) * slope[:, cols].astype(F32)).astype(BF16)
            dhid[:, cols] = low
            sums = jnp.sum(low.astype(F32), 0, keepdims=True)
            for part in range(half // width):
                number = 10 + side * (half // width) + part
                small_out[number : number + 1] = sums[:, part * width : (part + 1) * width]
        puts.append(pack(dhid, 2 * width, False, sems.at[12]))
        settle(place, get_mid)
        dnorm = dot_nt(dhid[...], w_up[...])
        hat, scale = norm_parts(mid[...].astype(F32))
        normed_mlp[...] = (hat * mlp_gain + mlp_shift).astype(BF16)
        puts.append(pack(normed_mlp, 0, False, sems.at[13]))
        puts.append(pack(normed_mlp, width, False, sems.at[21]))
        small_out[8:9] = jnp.sum(dnorm * hat, 0, keepdims=True)
        small_out[9:10] = jnp.sum(dnorm, 0, keepdims=True)
        u = dnorm * mlp_gain
        grad = grad_y[...].astype(F32) + scale * (
            u - jnp.mean(u, -1, keepdims=True) - hat * jnp.mean(u * hat, -1, keepdims=True)
        )
        low = grad.astype(BF16)
        gmid[...] = low
        puts.append(pack(gmid, 2 * width + 3 * width, True, sems.at[14]))
        puts.append(deliver(core_even, gmid, send_out, keep_out, sems.at[15]))
        small_out[4:5] = jnp.sum(low.astype(F32), 0, keepdims=True)
        settle(place, get_qkv, get_soft, get_ctx)
        puts.append(pack(ctx, width, True, sems.at[22]))
        dctx_all[...] = dot_nt(gmid[...], w_att[:, 3 * width :]).astype(BF16)
        heads = GROUP // 64

        def group_step(group, carry):
            cols = columns(group, GROUP)
            k_cols = pl.ds(pl.multiple_of(width + group * GROUP, GROUP), GROUP)
            v_cols = pl.ds(pl.multiple_of(2 * width + group * GROUP, GROUP), GROUP)
            dctx = dctx_all[:, cols]
            q = qkv[:, cols]
            k = qkv[:, k_cols]
            v = qkv[:, v_cols]
            product = dctx.astype(F32) * ctx[:, cols].astype(F32)
            masks = [head_mask(rows, head) for head in range(heads)]
            mine = jnp.concatenate([jnp.where(mask, dctx, 0) for mask in masks], 0)
            dp = dot_nt(mine, v)
            dq = jnp.zeros((rows, GROUP), F32)
            for head in range(heads):
                span = pl.ds(head * rows, rows)
                weight = soft[group * heads + head]
                delta = jnp.sum(jnp.where(masks[head], product, 0.0), -1, keepdims=True)
                ds = (weight.astype(F32) * (dp[head * rows : (head + 1) * rows] - delta)).astype(BF16)
                ds_all[span] = ds
                soft_all[span] = weight
                dq = dq + dot_nn(ds, jnp.where(masks[head], k, 0))
            dk = dot_tn(ds_all[...], jnp.concatenate([jnp.where(mask, q, 0) for mask in masks], 0))
            dv = dot_tn(soft_all[...], mine)
            dq_low = (dq * 0.125).astype(BF16)
            dv_low = dv.astype(BF16)
            dqkv[:, cols] = dq_low
            dqkv[:, k_cols] = dk.astype(BF16)
            dqkv[:, v_cols] = dv_low
            small_out[2:3, cols] = jnp.sum(dq_low.astype(F32), 0, keepdims=True)
            small_out[3:4, cols] = jnp.sum(dv_low.astype(F32), 0, keepdims=True)
            return carry

        lax.fori_loop(0, groups, group_step, 0)
        puts.append(pack(dqkv, 2 * width, True, sems.at[16]))
        settle(place, get_x)
        dnorm = dot_nt(dqkv[...], w_att[:, : 3 * width])
        hat, scale = norm_parts(x[...].astype(F32))
        normed_att[...] = (hat * att_gain + att_shift).astype(BF16)
        puts.append(pack(normed_att, 0, True, sems.at[17]))
        small_out[0:1] = jnp.sum(dnorm * hat, 0, keepdims=True)
        small_out[1:2] = jnp.sum(dnorm, 0, keepdims=True)
        u = dnorm * att_gain
        grad = gmid[...].astype(F32) + scale * (
            u - jnp.mean(u, -1, keepdims=True) - hat * jnp.mean(u * hat, -1, keepdims=True)
        )
        gx[...] = grad.astype(BF16)
        puts.append(start_copy(gx, grad_x_out, sems.at[18]))
        puts.append(deliver(core_even, gx, keep_out, send_out, sems.at[19]))
        token = jnp.sum(jnp.where(upright(flags[pl.ds(row, 1)], 128) == 1.0, grad, 0.0), 0, keepdims=True)
        small_out[6:7] = token
        small_out[14:15] = token
        theirs = jnp.where(core_even, small_out[8:16], small_out[0:8])
        high = theirs.astype(BF16)
        small_low[...] = jnp.concatenate([high, (theirs - high.astype(F32)).astype(BF16)], 0)
        puts.append(start_copy(small_low, pack_send.at[pl.ds(rows, 16), pl.ds(0, width)], sems.at[23]))
        for put in puts:
            put.wait()


def backward_call(slot, place, cotangent, back_row, flags, vecs, weights, saved_early, saved_late):
    rows, width = back_row.shape
    hidden = weights[0].shape[1]
    low = lambda *shape: jax.ShapeDtypeStruct(shape, BF16)
    row = low(rows, width)
    pack = low(rows + 16, 3 * width + hidden)
    weights = [pltpu.with_memory_space_constraint(array, pltpu.VMEM) for array in weights]
    outs = [row, row, row, jax.ShapeDtypeStruct((16, width), F32), pack, pack]
    specs = [ANY] * len(outs)
    specs[3] = VMEM
    v = pltpu.VMEM
    return pl.pallas_call(
        partial(backward_kernel, slot, cotangent.shape[0] // 2),
        out_shape=outs,
        in_specs=[SMEM, ANY, ANY] + [VMEM] * 10 + [ANY] * 12,
        out_specs=specs,
        scratch_shapes=[
            v((rows, width), BF16), v((rows, width), BF16), v((rows, width), BF16),
            v((rows, 3 * width), BF16), v((HEADS, rows, rows), BF16), v((rows, width), BF16), v((rows, hidden), BF16),
            v((rows, width), BF16), v((rows, width), BF16), v((rows, 3 * width), BF16), v((rows, hidden), BF16),
            v((rows, width), BF16), v((rows, width), BF16), v((rows, width), BF16),
            v((GROUP // 64 * rows, rows), BF16), v((GROUP // 64 * rows, rows), BF16),
            v((16, width), BF16), pltpu.SemaphoreType.DMA((24,)),
        ],
        compiler_params=pltpu.CompilerParams(vmem_limit_bytes=VMEM_LIMIT),
        cost_estimate=pl.CostEstimate(flops=8_000_000_000, bytes_accessed=34_000_000, transcendentals=1_000),
        name="row_backward",
    )(place, cotangent, back_row, flags, *vecs, *weights, *in_hbm(saved_early), *in_hbm(saved_late))


def weight_kernel(first_row, last_row, tall_rows, short_rows, place, token, *refs):
    sources, refs = refs[:10], refs[10:]
    if not first_row:
        before, refs = refs[:3], refs[3:]
    made = len(refs) - 13
    outs, refs = refs[:made], refs[made:]
    (left, right, act, grad_y, turned, part_t, grad_first, grad_half, mine, theirs, summed, small_low, sems) = refs
    early = place[1] == 0
    rows = left.shape[0] // 2
    hidden = right.shape[1]
    width = grad_y.shape[1]
    quarter = grad_half.shape[1]
    tall = pl.ds(pl.multiple_of(place[2] * place[3], 16), width)
    short = pl.ds(pl.multiple_of(place[2] * place[4], 16), quarter)
    core_even = place[0] == 0
    get_mine = fetch(early, sources[4], sources[9], mine, sems.at[10])
    spot = (pl.ds(rows, 16), pl.ds(0, width))
    get_theirs = fetch(early, sources[1].at[spot], sources[6].at[spot], theirs, sems.at[11])
    if not first_row:
        old_small = start_copy(before[2], summed, sems.at[12])
    waits = []
    for index, (first, second) in enumerate(zip(sources[2:4], sources[7:9])):
        waits.append(fetch(early, first, second, act.at[pl.ds(index * rows, rows)], sems.at[index]))
    start = 0
    pieces = []
    for number, target in enumerate((left, right, grad_y)):
        span = pl.ds(start, target.shape[1])
        start += target.shape[1]
        pieces.append([(first.at[pl.ds(0, rows), span], second.at[pl.ds(0, rows), span], target.at[pl.ds(index * rows, rows)], sems.at[2 + 2 * number + index])
                       for index, (first, second) in enumerate(zip(sources[:2], sources[5:7]))])
    waits += [fetch(early, *piece) for piece in pieces[2]]
    if not first_row:
        old_half = start_copy(before[1], grad_half, sems.at[8])
    waits_left = [fetch(early, *piece) for piece in pieces[0]]
    waits_right = [fetch(early, *piece) for piece in pieces[1]]
    if not first_row:
        old_first = start_copy(before[0], grad_first, sems.at[9])
    puts = []
    settle(place, get_mine, get_theirs, *([] if first_row else [old_small]))
    ours = jnp.where(core_even, mine[0:8], mine[8:16]) + theirs[0:8].astype(F32) + theirs[8:16].astype(F32)
    summed[...] = ours if first_row else ours + summed[...]
    if last_row:
        lines = lax.broadcasted_iota(jnp.int32, summed.shape, 0)
        summed[...] = jnp.where((lines == 6) & jnp.logical_not(early), token[...], summed[...])
        small_low[...] = jnp.concatenate([summed[...], jnp.zeros(summed.shape, F32)], 0).astype(BF16)
        if tall_rows:
            for index in range(width // tall_rows):
                target = outs[3 + index].at[pl.ds(tall_rows + short_rows, 16)]
                puts.append(start_copy(small_low, target, sems.at[14 + index]))
    puts.append(start_copy(summed, outs[2], sems.at[13]))

    def total(target, index, value):
        if not first_row:
            value = value + target[index].astype(F32)
        target[index] = value.astype(BF16)

    settle(place, *waits, *([] if first_row else [old_half]))

    def half_step(part, carry):
        flipped = act[:, columns(part, quarter)].T
        part_t[part, pl.ds(0, quarter)] = flipped
        part_t[part, pl.ds(quarter, quarter)] = flipped
        return carry

    lax.fori_loop(0, 4, half_step, 0)
    value = dot_nn(jnp.concatenate([part_t[part, short] for part in range(4)], 0), grad_y[...])
    for part in range(4):
        total(grad_half, part, value[part * quarter : (part + 1) * quarter])
    chunks = width // tall_rows if tall_rows else 0

    def ship(source, part, start, sem):
        if not chunks:
            return [start_copy(source.at[part], outs[3 + part].at[pl.ds(start, source.shape[1])], sems.at[sem + part])]
        size = source.shape[1] // chunks
        return [
            start_copy(
                source.at[part, pl.ds(index * size, size)],
                outs[3 + part * chunks + index].at[pl.ds(start // chunks, size)],
                sems.at[sem + part * chunks + index],
            )
            for index in range(chunks)
        ]

    if last_row:
        for part in range(4):
            puts += ship(grad_half, part, width, 14 + chunks)
    if not last_row:
        puts.append(start_copy(grad_half, outs[1], sems.at[14]))
    settle(place, *waits_left)

    settle(place, *waits_right, *([] if first_row else [old_first]))

    def turn_step(side, carry):
        flipped = left[:, columns(side, width)].T
        turned[side, pl.ds(0, width)] = flipped
        turned[side, pl.ds(width, width)] = flipped
        return carry

    lax.fori_loop(0, 2, turn_step, 0)
    value = dot_nn(turned[0, tall], right[:, : 3 * width])
    for part in range(3):
        total(grad_first, part, value[:, part * width : (part + 1) * width])
    total(grad_first, 3, dot_nn(turned[1, tall], right[:, 3 * width :]))
    if last_row:
        for part in range(4):
            puts += ship(grad_first, part, 0, 14 + chunks + 4 * max(chunks, 1))
    if not last_row:
        puts.append(start_copy(grad_first, outs[0], sems.at[15]))
    for put in puts:
        put.wait()


def weight_call(place, token, early_row, late_row, before, last_row, members):
    rows, half = early_row[2].shape
    hidden = 2 * half
    width = (early_row[0].shape[1] - hidden) // 3
    quarter = half // 4
    low = lambda *shape: jax.ShapeDtypeStruct(shape, BF16)
    tall, short = aligned_chunk(width, quarter, members)
    sums = jax.ShapeDtypeStruct((8, width), F32)
    outs = [pltpu.HBM((4, width, width), BF16), pltpu.HBM((4, quarter, width), BF16), sums]
    if last_row:
        outs = [
            pltpu.HBM((members, width // members, hidden), F32),
            pltpu.HBM((4, members, quarter // members, width), F32),
            sums,
        ]
        outs += [low(tall + short + 16, width)] * members + [low(tall + short, width)] * (3 * members) if tall else [low(width + quarter, width)] * 4
    v = pltpu.VMEM
    return pl.pallas_call(
        partial(weight_kernel, before is None, last_row, tall, short),
        out_shape=outs,
        in_specs=[SMEM, VMEM] + [ANY] * (10 if before is None else 13),
        out_specs=[ANY] * len(outs),
        scratch_shapes=[
            v((2 * rows, 2 * width), BF16), v((2 * rows, hidden), BF16), v((2 * rows, half), BF16),
            v((2 * rows, width), BF16), v((2, 2 * width, 2 * rows), BF16), v((4, 2 * quarter, 2 * rows), BF16),
            v((4, width, width), BF16), v((4, quarter, width), BF16),
            v((16, width), F32), v((16, width), BF16), v((8, width), F32), v((16, width), BF16),
            pltpu.SemaphoreType.DMA((24 + 9 * members,)),
        ],
        compiler_params=pltpu.CompilerParams(vmem_limit_bytes=(60 if last_row else 42) * MIB),
        cost_estimate=pl.CostEstimate(flops=8_000_000_000, bytes_accessed=24_000_000, transcendentals=0),
        name="weight_gradients",
    )(place, token, *in_hbm(early_row), *in_hbm(late_row), *in_hbm(before or ()))


def aligned_chunk(width, quarter, members):
    tall, short = width // members, quarter // members
    return (tall, short) if tall % 16 == 0 and short % 16 == 0 else (0, 0)


def ring_order(members):
    return list(range(0, members, 2)) + list(range(members - 1, 0, -2))


def ring_reduce(own, matrix, half, position, axis, pending):
    members = lax.axis_size(axis)
    order = ring_order(members)
    ahead = [(order[i], order[(i + 1) % members]) for i in range(members)]
    behind = [(b, a) for a, b in ahead]
    parts = len(own)
    tall, width = matrix.shape[1], half.shape[3]
    short = half.shape[2]
    steps = [1 - 2 * (part % 2) for part in range(parts)]

    def piece(array, index):
        cut = lambda start, size: lax.dynamic_slice_in_dim(array, start, size, 0)
        if isinstance(index, int):
            cut = lambda start, size: lax.slice_in_dim(array, start, start + size, axis=0)
        return jnp.concatenate([cut(index * tall, tall), cut(width + index * short, short)], 0).astype(F32)

    def chunk(part, number):
        index = (members - steps[part] * number) % members
        return own[part][index].astype(F32) if isinstance(own[part], (list, tuple)) else piece(own[part], index)

    def shift(part, value):
        return lax.ppermute(value, axis, ahead if part % 2 == 0 else behind)

    def reduce_step(number, current):
        moved = [shift(part, current[part]) for part in range(parts)]
        return [(moved[part].astype(F32) + chunk(part, number)).astype(BF16) for part in range(parts)]

    def place_chunks(number, current, matrix, half):
        for part in range(parts):
            index = lax.rem(position + jnp.uint32(members) + jnp.uint32(steps[part] % members) * (
                jnp.uint32(members + 1) - jnp.uint32(number)), jnp.uint32(members))
            wide = current[part].astype(F32)
            zero, block = jnp.uint32(0), jnp.uint32(part)
            matrix = lax.dynamic_update_slice(matrix, wide[None, :tall], (index, zero, jnp.uint32(part * width)))
            half = lax.dynamic_update_slice(half, wide[None, None, tall:], (block, index, zero, zero))
        return matrix, half

    def gather_step(number, carry):
        current, matrix, half = carry
        current = [shift(part, current[part]) for part in range(parts)]
        return (current, *place_chunks(number, current, matrix, half))

    current = [chunk(part, 0).astype(BF16) for part in range(parts)]
    extra = current[0]
    if members > 8:
        current = lax.fori_loop(1, members, reduce_step, current)
        carry = lax.fori_loop(1, members, gather_step, (current, *place_chunks(0, current, matrix, half)))
    else:
        for number in range(1, members):
            current = reduce_step(number, current)
        extra = current[0][tall + short :]
        current[0] = current[0][: tall + short]
        carry = (current, *place_chunks(0, current, matrix, half))
        for number in range(1, members):
            carry = gather_step(number, carry)
            if number in (1, 3):
                which = number // 2
                pending[which] = lax.optimization_barrier((pending[which], carry[0][0]))[0]
    return carry[1].reshape(tall * members, parts * width), carry[2].reshape(parts * short * members, width), extra, pending


def turn_rows(array, width, position, members):
    top = jnp.roll(array[:width], -position * (width // members), 0)
    return jnp.concatenate([top, jnp.roll(array[width:], -position * ((array.shape[0] - width) // members), 0)], 0)


def shards(
    patches, cotangent, mask_flags, segments, mask_token, norm_gains, norm_shifts, w_first, first_bias, down_half
):
    section = lax.axis_index("section")
    core = section & 1
    stage = section >> 1
    early = stage == 0
    swap = [(0, 1), (1, 0), (2, 3), (3, 2)]
    forth = [(0, 2), (1, 3)]
    back = [(2, 0), (3, 1)]
    row_count, rows, width = patches.shape
    count = row_count // 2
    members = lax.axis_size("dp")
    place_of = np.zeros(members, np.int32)
    for spot, member in enumerate(ring_order(members)):
        place_of[member] = spot
    position = jnp.asarray(place_of)[lax.axis_index("dp").astype(jnp.uint32)]

    first_own, half_own = w_first[0], down_half[0]
    hidden = first_own.shape[1]
    quarter = hidden // 8
    tall, short = width // members, quarter // members
    aligned = aligned_chunk(width, quarter, members)[0] > 0
    first_other = lax.ppermute(first_own, "section", swap)
    half_other = lax.ppermute(half_own, "section", swap)
    own_vecs = (norm_gains, norm_shifts, first_bias)
    vecs = own_vecs + tuple(lax.ppermute(array, "section", swap) for array in own_vecs)
    weights = (first_own, first_other, half_own, half_other)
    turns = position if aligned else 0 * position
    place = jnp.stack([core, stage, turns, jnp.int32(16 * (tall // 16)), jnp.int32(16 * (short // 16))]).astype(jnp.int32)
    token = mask_token[None]

    forwards, acts, packs = [], [], []
    sent = patches[0]
    for slot in range(count + 1):
        result = forward_call(slot, place, patches, sent, mask_flags, segments, token, vecs, weights)
        forwards.append(result)
        if slot < count:
            sent = lax.ppermute(result[2], "section", forth)
        acts.append(lax.ppermute(result[9], "section", swap))
        if slot == 0:
            weights = hold_call(place, lax.optimization_barrier((weights, result[2]))[0])

    def assemble(pairs):
        chosen = [jnp.where(early, a, b) for a, b in pairs]
        keep, send = jnp.stack(chosen[0::2]), jnp.stack(chosen[1::2])
        received = lax.ppermute(send, "section", swap)
        return jnp.where(
            core == 0, jnp.concatenate([keep, received], 0), jnp.concatenate([received, keep], 0)
        )

    backs = []
    returned = patches[0]
    grads = None
    for slot in range(count + 1):
        saved = [
            [forwards[which][i] for i in (3, 4, 5, 6, 7, 10)] for which in (max(slot - 1, 0), min(slot + 1, count))
        ]
        backs.append(backward_call(slot, place, cotangent, returned, mask_flags, vecs, weights, *saved))
        if slot < count:
            returned = lax.ppermute(backs[slot][2], "section", back)
            if slot == 0:
                returned, acts[:2] = lax.optimization_barrier((returned, acts[:2]))
        packs.append(lax.ppermute(backs[slot][5], "section", swap))
        if slot > 0:
            row = slot - 1
            chosen = [
                (backs[b][4], packs[b], forwards[f][8], acts[f], backs[b][3]) for f, b in ((row, row + 1), (row + 1, row))
            ]
            total = sum(backs[b][3][6:7] for b in range(1, slot + 1))
            if row == count - 1:
                cross = [(0, 3), (1, 2)]
                total = lax.ppermute(total, "section", forth) + lax.ppermute(total, "section", cross)
            grads = weight_call(place, total, *chosen, grads, row == count - 1, members)
            if row < count - 1:
                returned, grads, acts = lax.optimization_barrier((returned, grads, acts))

    blank, small = grads[:2], grads[2]
    if aligned:
        own = [grads[3 + part * members : 3 + (part + 1) * members] for part in range(4)]
    else:
        own = [turn_rows(array, width, position, members) for array in grads[3:]]
        small = lax.psum(small, "dp")

    pending = [
        [(forwards[row][i], forwards[row + 1][i]) for row in range(count) for i in (0, 1)],
        [(backs[row + 1][i], backs[row][i]) for row in range(count) for i in (0, 1)],
    ]
    grad_first, grad_half, extra, pending = ring_reduce(own, *blank, position.astype(jnp.uint32), "dp", pending)
    if aligned:
        small = extra[:8].astype(F32)
    token_grad = small[6]

    finals = assemble(pending[0])
    back_rows = assemble(pending[1]).astype(F32)
    back_rows = jnp.where((section == 0) & (mask_flags[..., None] == 1), 0.0, back_rows)
    return (
        finals[None],
        back_rows[None],
        token_grad,
        small[0:1],
        small[1:2],
        grad_first[None],
        small[2:6].reshape(1, hidden),
        grad_half[None],
    )


def solution(mesh):
    return jax.shard_map(
        shards,
        mesh=mesh,
        in_specs=(
            P("dp", None, None),
            P("dp", None, None),
            P("dp", None),
            P("dp", None),
            P(),
            P("section", None),
            P("section", None),
            P("section", None, None),
            P("section", None),
            P("section", None, None),
        ),
        out_specs=(
            P("section", "dp", None, None),
            P("section", "dp", None, None),
            P(),
            P("section", None),
            P("section", None),
            P("section", None, None),
            P("section", None),
            P("section", None, None),
        ),
        check_vma=False,
    )
```

```python
from functools import partial

import jax
import jax.numpy as jnp
import numpy as np
from jax import lax
from jax.experimental import pallas as pl
from jax.experimental.pallas import tpu as pltpu
from jax.sharding import PartitionSpec as P

HEADS = 12
EPSILON = 1e-06
NEGATIVE = -1000000000.0
GROUP = 256
TILE = 768
MIB = 1024 * 1024
VMEM_LIMIT = 49 * MIB
BF16 = jnp.bfloat16
F32 = jnp.float32
ANY = pl.BlockSpec(memory_space=pl.ANY)
SMEM = pl.BlockSpec(memory_space=pltpu.SMEM)
VMEM = pl.BlockSpec(memory_space=pltpu.VMEM)


def dot_nn(a, b):
    return jnp.dot(a, b, preferred_element_type=F32)


def dot_nt(a, b):
    return lax.dot_general(a, b, (((1,), (1,)), ((), ())), preferred_element_type=F32)


def dot_tn(a, b):
    return lax.dot_general(a, b, (((0,), (0,)), ((), ())), preferred_element_type=F32)


def fetch(choice, first, second, target, sem):
    @pl.when(choice)
    def _():
        pltpu.make_async_copy(first, target, sem).start()

    @pl.when(jnp.logical_not(choice))
    def _():
        pltpu.make_async_copy(second, target, sem).start()

    return pltpu.make_async_copy(first, target, sem)


def deliver(choice, source, first, second, sem):
    @pl.when(choice)
    def _():
        pltpu.make_async_copy(source, first, sem).start()

    @pl.when(jnp.logical_not(choice))
    def _():
        pltpu.make_async_copy(source, second, sem).start()

    return pltpu.make_async_copy(source, first, sem)


def start_copy(source, target, sem):
    copy = pltpu.make_async_copy(source, target, sem)
    copy.start()
    return copy


def settle(place, *copies):
    @pl.when(place[0] >= 0)
    def _():
        for copy in copies:
            copy.wait()


def norm_parts(x):
    centred = x - jnp.mean(x, -1, keepdims=True)
    scale = lax.rsqrt(jnp.mean(centred * centred, -1, keepdims=True) + EPSILON)
    return centred * scale, scale


def gelu_pair(hidden):
    base = 1.0 + 0.23164189 * jnp.abs(hidden)
    t = pl.reciprocal(base, approx=True)
    t = t * (2.0 - base * t)
    poly = ((((0.5307027145 * t - 0.7265760135) * t + 0.7107068705) * t - 0.142248368) * t + 0.127414796) * t
    fall = jnp.exp2(hidden * hidden * -0.7213475204444817)
    tail = poly * fall
    cdf = jnp.where(hidden >= 0, 1.0 - tail, tail)
    return hidden * cdf, cdf + hidden * fall * 0.3989422804014327


def columns(index, width):
    return pl.ds(pl.multiple_of(index * width, width), width)


def head_mask(rows, head):
    lane = lax.broadcasted_iota(jnp.int32, (rows, GROUP), 1)
    return (lane >= head * 64) & (lane < head * 64 + 64)


def load_down(core_even, half_own, half_other, w_down, sems):
    half = half_own.shape[0]
    low = fetch(core_even, half_own, half_other, w_down.at[pl.ds(0, half)], sems.at[2])
    high = fetch(core_even, half_other, half_own, w_down.at[pl.ds(half, half)], sems.at[3])
    return low, high


def vectors(core_even, refs):
    own, other = refs[:3], refs[3:]
    att = [jnp.where(core_even, a[...].astype(F32), b[...].astype(F32)) for a, b in zip(own, other)]
    mlp = [jnp.where(core_even, b[...].astype(F32), a[...].astype(F32)) for a, b in zip(own, other)]
    return att, mlp


def upright(row, width):
    return jnp.broadcast_to(row.astype(F32), (width, row.shape[1])).T[:, :1]


def in_hbm(arrays):
    return [pltpu.with_memory_space_constraint(array, pltpu.HBM) for array in arrays]


def pin_own(arrays):
    mine, theirs, act, act_theirs, small = arrays
    return [*in_hbm([mine]), theirs, *in_hbm([act, act_theirs]), small]


def row_number(place, slot, count, backward):
    late = place[1]
    number = slot - (1 - late) if backward else slot - late
    return place[0] * count + jnp.clip(number, 0, count - 1)


def forward_kernel(
    slot, count, held, place, patches, sent_row, flags, segments, token, *refs
):
    vecs, refs = refs[:6], refs[6:]
    if held:
        (w_att, w_up, w_down), refs = refs[:3], refs[3:]
    else:
        (first_own, first_other, half_own, half_other), refs = refs[:4], refs[4:]
    (keep_out, send_out, y_mlp_out, x_out, mid_out, qkv_out, soft_out, ctx_out, act_keep_out, act_send_out,
     slope_out, x, bias, normed, qkv, soft, ctx, mid, act, slope, y_mlp, sems) = refs[:22]
    if not held:
        w_att, w_up, w_down = refs[22:]
    core_even = place[0] == 0
    early = place[1] == 0
    rows, width = x.shape
    groups = width // GROUP
    row = row_number(place, slot, count, False)
    get_x = fetch(early, patches.at[row], sent_row, x, sems.at[4])
    if not held:
        get_att = fetch(core_even, first_own, first_other, w_att, sems.at[0])
    (att_gain, att_shift, att_bias), (mlp_gain, mlp_shift, mlp_bias) = vectors(core_even, vecs)
    seg = segments[pl.ds(row, 1)]
    bias[...] = jnp.where(upright(seg, 128) == seg.astype(F32), 0.0, NEGATIVE)
    settle(place, get_x)

    @pl.when(early)
    def _():
        flag = upright(flags[pl.ds(row, 1)], 128)
        x[...] = jnp.where(flag == 1.0, token[...].astype(F32), x[...].astype(F32)).astype(BF16)

    puts = [start_copy(x, x_out, sems.at[5])]
    hat, _ = norm_parts(x[...].astype(F32))
    normed[...] = (hat * att_gain + att_shift).astype(BF16)
    if not held:
        settle(place, get_att)
        get_up = fetch(core_even, first_other, first_own, w_up, sems.at[1])
        get_low, get_high = load_down(core_even, half_own, half_other, w_down, sems)
    projected = dot_nn(normed[...], w_att[:, : 3 * width])
    q_low = (projected[:, :width] + att_bias[:, :width]).astype(BF16)
    qkv[:, :width] = (q_low * 0.125).astype(BF16)
    qkv[:, width : 2 * width] = projected[:, width : 2 * width].astype(BF16)
    qkv[:, 2 * width :] = (projected[:, 2 * width :] + att_bias[:, width : 2 * width]).astype(BF16)
    puts.append(start_copy(qkv, qkv_out, sems.at[6]))
    heads = GROUP // 64
    for group in range(groups):
        cols = pl.ds(group * GROUP, GROUP)
        q = qkv[:, cols]
        k = qkv[:, pl.ds(width + group * GROUP, GROUP)]
        v = qkv[:, pl.ds(2 * width + group * GROUP, GROUP)]
        masks = [head_mask(rows, head) for head in range(heads)]
        scores = dot_nt(jnp.concatenate([jnp.where(mask, q, 0) for mask in masks], 0), k)
        total = jnp.zeros((rows, GROUP), F32)
        for head in range(heads):
            mine = scores[head * rows : (head + 1) * rows] + bias[...]
            raised = jnp.exp(mine - jnp.max(mine, -1, keepdims=True))
            weight = (raised * (1.0 / jnp.sum(raised, -1, keepdims=True))).astype(BF16)
            soft[group * heads + head] = weight
            total = total + dot_nn(weight, jnp.where(masks[head], v, 0))
        ctx[:, cols] = total.astype(BF16)
        span = pl.ds(group * heads, heads)
        puts.append(start_copy(soft.at[span], soft_out.at[span], sems.at[17 + group]))
    puts.append(start_copy(ctx, ctx_out, sems.at[8]))
    y = x[...].astype(F32) + dot_nn(ctx[...], w_att[:, 3 * width :]) + att_bias[:, 2 * width : 3 * width]
    low = y.astype(BF16)
    mid[...] = low
    puts.append(start_copy(mid, mid_out, sems.at[9]))
    puts.append(deliver(core_even, mid, keep_out, send_out, sems.at[10]))
    hat, _ = norm_parts(low.astype(F32))
    normed[...] = (hat * mlp_gain + mlp_shift).astype(BF16)
    if not held:
        settle(place, get_up)
    half = act.shape[1] // 2
    for side in range(2):
        cols = pl.ds(side * half, half)
        hidden = dot_nn(normed[...], w_up[:, cols]) + mlp_bias[:, side * half : (side + 1) * half]
        active, rate = gelu_pair(hidden)
        act[:, cols] = active.astype(BF16)
        slope[:, cols] = rate.astype(BF16)
        targets = (act_send_out, act_keep_out) if side else (act_keep_out, act_send_out)
        puts.append(deliver(core_even, act.at[:, cols], *targets, sems.at[11 + side]))
        puts.append(start_copy(slope.at[:, cols], slope_out.at[:, cols], sems.at[13 + side]))
    if not held:
        settle(place, get_low, get_high)
    y = mid[...].astype(F32) + dot_nn(act[...], w_down[...]) + att_bias[:, 3 * width :]
    y_mlp[...] = y.astype(BF16)
    puts.append(start_copy(y_mlp, y_mlp_out, sems.at[15]))
    puts.append(deliver(core_even, y_mlp, send_out, keep_out, sems.at[16]))
    for put in puts:
        put.wait()


def hold_kernel(place, first_own, first_other, half_own, half_other, w_att, w_up, w_down, sems):
    core_even = place[0] == 0
    copies = [
        fetch(core_even, first_own, first_other, w_att, sems.at[0]),
        fetch(core_even, first_other, first_own, w_up, sems.at[1]),
        *load_down(core_even, half_own, half_other, w_down, sems),
    ]
    for copy in copies:
        copy.wait()


def hold_call(place, weights):
    width, hidden = weights[0].shape
    v = pltpu.VMEM
    return pl.pallas_call(
        hold_kernel,
        out_shape=[v((width, hidden), BF16), v((width, hidden), BF16), v((hidden, width), BF16)],
        in_specs=[SMEM] + [ANY] * 4,
        out_specs=[VMEM] * 3,
        scratch_shapes=[pltpu.SemaphoreType.DMA((4,))],
        compiler_params=pltpu.CompilerParams(vmem_limit_bytes=VMEM_LIMIT),
        cost_estimate=pl.CostEstimate(flops=0, bytes_accessed=14_000_000, transcendentals=0),
        name="hold_weights",
    )(place, *weights)


def forward_call(slot, place, patches, sent_row, flags, segments, token, vecs, weights):
    rows, width = sent_row.shape
    held = len(weights) == 3
    if held:
        weights = [pltpu.with_memory_space_constraint(array, pltpu.VMEM) for array in weights]
    hidden = weights[0].shape[1]
    low = lambda *shape: jax.ShapeDtypeStruct(shape, BF16)
    row = low(rows, width)
    outs = [row, row, row, row, row, low(rows, 3 * width), low(HEADS, rows, rows), row]
    outs += [low(rows, hidden // 2), low(rows, hidden // 2), low(rows, hidden)]
    v = pltpu.VMEM
    return pl.pallas_call(
        partial(forward_kernel, slot, patches.shape[0] // 2, held),
        out_shape=outs,
        in_specs=[SMEM, ANY, ANY] + [VMEM] * 9 + ([VMEM] * 3 if held else [ANY] * 4),
        out_specs=[ANY] * len(outs),
        scratch_shapes=[
            v((rows, width), BF16), v((rows, rows), F32), v((rows, width), BF16),
            v((rows, 3 * width), BF16), v((HEADS, rows, rows), BF16), v((rows, width), BF16), v((rows, width), BF16),
            v((rows, hidden), BF16), v((rows, hidden), BF16), v((rows, width), BF16),
            pltpu.SemaphoreType.DMA((20,)),
        ]
        + ([] if held else [v((width, hidden), BF16), v((width, hidden), BF16), v((hidden, width), BF16)]),
        compiler_params=pltpu.CompilerParams(vmem_limit_bytes=VMEM_LIMIT if held else 60 * MIB),
        cost_estimate=pl.CostEstimate(flops=7_000_000_000, bytes_accessed=26_000_000, transcendentals=2_500_000),
        name="row_forward",
    )(place, patches, sent_row, flags, segments, token, *vecs, *weights)


def backward_kernel(slot, count, place, cotangent, back_row, flags, *refs):
    vecs = refs[:6]
    (w_att, w_up, w_down,
     x_a, mid_a, qkv_a, soft_a, ctx_a, slope_a, x_b, mid_b, qkv_b, soft_b, ctx_b, slope_b,
     keep_out, send_out, grad_x_out, small_out, pack_keep, pack_send,
     grad_y, x, mid, qkv, soft, ctx, slope, normed_att, normed_mlp, dqkv, dhid, gmid, gx,
     dctx_all, ds_all, soft_all, small_low, sems) = refs[6:]
    core_even = place[0] == 0
    early = place[1] == 0
    rows, width = x.shape
    groups = width // GROUP
    row = row_number(place, slot, count, True)
    busy = jnp.logical_and(early, slot >= 1) | jnp.logical_and(jnp.logical_not(early), slot < count)
    small_out[...] = jnp.zeros(small_out.shape, F32)

    @pl.when(busy)
    def _():
        get_g = fetch(early, back_row, cotangent.at[row], grad_y, sems.at[4])
        get_slope = fetch(early, slope_a, slope_b, slope, sems.at[5])
        (att_gain, att_shift, _), (mlp_gain, mlp_shift, _) = vectors(core_even, vecs)
        settle(place, get_g)

        def pack(source, start, to_even, sem):
            spot = (pl.ds(0, rows), pl.ds(start, source.shape[1]))
            if to_even:
                return deliver(core_even, source, pack_keep.at[spot], pack_send.at[spot], sem)
            return deliver(core_even, source, pack_send.at[spot], pack_keep.at[spot], sem)

        hidden = dhid.shape[1]
        last = 2 * width + hidden
        puts = [
            start_copy(grad_y, pack_keep.at[pl.ds(0, rows), pl.ds(last, width)], sems.at[11]),
            start_copy(grad_y, pack_send.at[pl.ds(0, rows), pl.ds(last, width)], sems.at[20]),
        ]
        small_out[5:6] = jnp.sum(grad_y[...].astype(F32), 0, keepdims=True)
        settle(place, get_slope)
        get_mid = fetch(early, mid_a, mid_b, mid, sems.at[6])
        get_soft = fetch(early, soft_a, soft_b, soft, sems.at[9])
        get_qkv = fetch(early, qkv_a, qkv_b, qkv, sems.at[8])
        get_ctx = fetch(early, ctx_a, ctx_b, ctx, sems.at[10])
        get_x = fetch(early, x_a, x_b, x, sems.at[7])
        half = hidden // 2
        for side in range(2):
            cols = pl.ds(side * half, half)
            low = (dot_nt(grad_y[...], w_down[cols, :]) * slope[:, cols].astype(F32)).astype(BF16)
            dhid[:, cols] = low
            sums = jnp.sum(low.astype(F32), 0, keepdims=True)
            for part in range(half // width):
                number = 10 + side * (half // width) + part
                small_out[number : number + 1] = sums[:, part * width : (part + 1) * width]
        puts.append(pack(dhid, 2 * width, False, sems.at[12]))
        settle(place, get_mid)
        dnorm = dot_nt(dhid[...], w_up[...])
        hat, scale = norm_parts(mid[...].astype(F32))
        normed_mlp[...] = (hat * mlp_gain + mlp_shift).astype(BF16)
        puts.append(pack(normed_mlp, 0, False, sems.at[13]))
        puts.append(pack(normed_mlp, width, False, sems.at[21]))
        small_out[8:9] = jnp.sum(dnorm * hat, 0, keepdims=True)
        small_out[9:10] = jnp.sum(dnorm, 0, keepdims=True)
        u = dnorm * mlp_gain
        grad = grad_y[...].astype(F32) + scale * (
            u - jnp.mean(u, -1, keepdims=True) - hat * jnp.mean(u * hat, -1, keepdims=True)
        )
        low = grad.astype(BF16)
        gmid[...] = low
        puts.append(pack(gmid, 2 * width + 3 * width, True, sems.at[14]))
        puts.append(deliver(core_even, gmid, send_out, keep_out, sems.at[15]))
        small_out[4:5] = jnp.sum(low.astype(F32), 0, keepdims=True)
        settle(place, get_qkv, get_soft, get_ctx)
        puts.append(pack(ctx, width, True, sems.at[22]))
        dctx_all[...] = dot_nt(gmid[...], w_att[:, 3 * width :]).astype(BF16)
        heads = GROUP // 64

        def group_step(group, carry):
            cols = columns(group, GROUP)
            k_cols = pl.ds(pl.multiple_of(width + group * GROUP, GROUP), GROUP)
            v_cols = pl.ds(pl.multiple_of(2 * width + group * GROUP, GROUP), GROUP)
            dctx = dctx_all[:, cols]
            q = qkv[:, cols]
            k = qkv[:, k_cols]
            v = qkv[:, v_cols]
            product = dctx.astype(F32) * ctx[:, cols].astype(F32)
            masks = [head_mask(rows, head) for head in range(heads)]
            mine = jnp.concatenate([jnp.where(mask, dctx, 0) for mask in masks], 0)
            dp = dot_nt(mine, v)
            dq = jnp.zeros((rows, GROUP), F32)
            for head in range(heads):
                span = pl.ds(head * rows, rows)
                weight = soft[group * heads + head]
                delta = jnp.sum(jnp.where(masks[head], product, 0.0), -1, keepdims=True)
                ds = (weight.astype(F32) * (dp[head * rows : (head + 1) * rows] - delta)).astype(BF16)
                ds_all[span] = ds
                soft_all[span] = weight
                dq = dq + dot_nn(ds, jnp.where(masks[head], k, 0))
            dk = dot_tn(ds_all[...], jnp.concatenate([jnp.where(mask, q, 0) for mask in masks], 0))
            dv = dot_tn(soft_all[...], mine)
            dq_low = (dq * 0.125).astype(BF16)
            dv_low = dv.astype(BF16)
            dqkv[:, cols] = dq_low
            dqkv[:, k_cols] = dk.astype(BF16)
            dqkv[:, v_cols] = dv_low
            small_out[2:3, cols] = jnp.sum(dq_low.astype(F32), 0, keepdims=True)
            small_out[3:4, cols] = jnp.sum(dv_low.astype(F32), 0, keepdims=True)
            return carry

        lax.fori_loop(0, groups, group_step, 0)
        puts.append(pack(dqkv, 2 * width, True, sems.at[16]))
        settle(place, get_x)
        dnorm = dot_nt(dqkv[...], w_att[:, : 3 * width])
        hat, scale = norm_parts(x[...].astype(F32))
        normed_att[...] = (hat * att_gain + att_shift).astype(BF16)
        puts.append(pack(normed_att, 0, True, sems.at[17]))
        small_out[0:1] = jnp.sum(dnorm * hat, 0, keepdims=True)
        small_out[1:2] = jnp.sum(dnorm, 0, keepdims=True)
        u = dnorm * att_gain
        grad = gmid[...].astype(F32) + scale * (
            u - jnp.mean(u, -1, keepdims=True) - hat * jnp.mean(u * hat, -1, keepdims=True)
        )
        gx[...] = grad.astype(BF16)
        puts.append(start_copy(gx, grad_x_out, sems.at[18]))
        puts.append(deliver(core_even, gx, keep_out, send_out, sems.at[19]))
        token = jnp.sum(jnp.where(upright(flags[pl.ds(row, 1)], 128) == 1.0, grad, 0.0), 0, keepdims=True)
        small_out[6:7] = token
        small_out[14:15] = token
        theirs = jnp.where(core_even, small_out[8:16], small_out[0:8])
        high = theirs.astype(BF16)
        small_low[...] = jnp.concatenate([high, (theirs - high.astype(F32)).astype(BF16)], 0)
        puts.append(start_copy(small_low, pack_send.at[pl.ds(rows, 16), pl.ds(0, width)], sems.at[23]))
        for put in puts:
            put.wait()


def backward_call(slot, place, cotangent, back_row, flags, vecs, weights, saved_early, saved_late):
    rows, width = back_row.shape
    hidden = weights[0].shape[1]
    low = lambda *shape: jax.ShapeDtypeStruct(shape, BF16)
    row = low(rows, width)
    pack = low(rows + 16, 3 * width + hidden)
    weights = [pltpu.with_memory_space_constraint(array, pltpu.VMEM) for array in weights]
    outs = [row, row, row, jax.ShapeDtypeStruct((16, width), F32), pack, pack]
    specs = [ANY] * len(outs)
    specs[3] = VMEM
    v = pltpu.VMEM
    return pl.pallas_call(
        partial(backward_kernel, slot, cotangent.shape[0] // 2),
        out_shape=outs,
        in_specs=[SMEM, ANY, ANY] + [VMEM] * 10 + [ANY] * 12,
        out_specs=specs,
        scratch_shapes=[
            v((rows, width), BF16), v((rows, width), BF16), v((rows, width), BF16),
            v((rows, 3 * width), BF16), v((HEADS, rows, rows), BF16), v((rows, width), BF16), v((rows, hidden), BF16),
            v((rows, width), BF16), v((rows, width), BF16), v((rows, 3 * width), BF16), v((rows, hidden), BF16),
            v((rows, width), BF16), v((rows, width), BF16), v((rows, width), BF16),
            v((GROUP // 64 * rows, rows), BF16), v((GROUP // 64 * rows, rows), BF16),
            v((16, width), BF16), pltpu.SemaphoreType.DMA((24,)),
        ],
        compiler_params=pltpu.CompilerParams(vmem_limit_bytes=VMEM_LIMIT),
        cost_estimate=pl.CostEstimate(flops=8_000_000_000, bytes_accessed=34_000_000, transcendentals=1_000),
        name="row_backward",
    )(place, cotangent, back_row, flags, *vecs, *weights, *in_hbm(saved_early), *in_hbm(saved_late))


def weight_kernel(first_row, last_row, tall_rows, short_rows, place, token, *refs):
    sources, refs = refs[:10], refs[10:]
    if not first_row:
        before, refs = refs[:3], refs[3:]
    made = len(refs) - 13
    outs, refs = refs[:made], refs[made:]
    (left, right, act, grad_y, turned, part_t, grad_first, grad_half, mine, theirs, summed, small_low, sems) = refs
    early = place[1] == 0
    rows = left.shape[0] // 2
    hidden = right.shape[1]
    width = grad_y.shape[1]
    quarter = grad_half.shape[1]
    tall = pl.ds(pl.multiple_of(place[2] * place[3], 16), width)
    short = pl.ds(pl.multiple_of(place[2] * place[4], 16), quarter)
    core_even = place[0] == 0
    get_mine = fetch(early, sources[4], sources[9], mine, sems.at[10])
    spot = (pl.ds(rows, 16), pl.ds(0, width))
    get_theirs = fetch(early, sources[1].at[spot], sources[6].at[spot], theirs, sems.at[11])
    if not first_row:
        old_small = start_copy(before[2], summed, sems.at[12])
    waits = []
    for index, (first, second) in enumerate(zip(sources[2:4], sources[7:9])):
        waits.append(fetch(early, first, second, act.at[pl.ds(index * rows, rows)], sems.at[index]))
    start = 0
    pieces = []
    for number, target in enumerate((left, right, grad_y)):
        span = pl.ds(start, target.shape[1])
        start += target.shape[1]
        pieces.append([(first.at[pl.ds(0, rows), span], second.at[pl.ds(0, rows), span], target.at[pl.ds(index * rows, rows)], sems.at[2 + 2 * number + index])
                       for index, (first, second) in enumerate(zip(sources[:2], sources[5:7]))])
    waits += [fetch(early, *piece) for piece in pieces[2]]
    if not first_row:
        old_half = start_copy(before[1], grad_half, sems.at[8])
    waits_left = [fetch(early, *piece) for piece in pieces[0]]
    waits_right = [fetch(early, *piece) for piece in pieces[1]]
    if not first_row:
        old_first = start_copy(before[0], grad_first, sems.at[9])
    puts = []
    settle(place, get_mine, get_theirs, *([] if first_row else [old_small]))
    ours = jnp.where(core_even, mine[0:8], mine[8:16]) + theirs[0:8].astype(F32) + theirs[8:16].astype(F32)
    summed[...] = ours if first_row else ours + summed[...]
    if last_row:
        lines = lax.broadcasted_iota(jnp.int32, summed.shape, 0)
        summed[...] = jnp.where((lines == 6) & jnp.logical_not(early), token[...], summed[...])
        small_low[...] = jnp.concatenate([summed[...], jnp.zeros(summed.shape, F32)], 0).astype(BF16)
        if tall_rows:
            for index in range(width // tall_rows):
                target = outs[3 + index].at[pl.ds(tall_rows + short_rows, 16)]
                puts.append(start_copy(small_low, target, sems.at[14 + index]))
    puts.append(start_copy(summed, outs[2], sems.at[13]))

    def total(target, index, value):
        if not first_row:
            value = value + target[index].astype(F32)
        target[index] = value.astype(BF16)

    settle(place, *waits, *([] if first_row else [old_half]))

    def half_step(part, carry):
        flipped = act[:, columns(part, quarter)].T
        part_t[part, pl.ds(0, quarter)] = flipped
        part_t[part, pl.ds(quarter, quarter)] = flipped
        return carry

    lax.fori_loop(0, 4, half_step, 0)
    value = dot_nn(jnp.concatenate([part_t[part, short] for part in range(4)], 0), grad_y[...])
    for part in range(4):
        total(grad_half, part, value[part * quarter : (part + 1) * quarter])
    chunks = width // tall_rows if tall_rows else 0

    def ship(source, part, start, sem):
        if not chunks:
            return [start_copy(source.at[part], outs[3 + part].at[pl.ds(start, source.shape[1])], sems.at[sem + part])]
        size = source.shape[1] // chunks
        return [
            start_copy(
                source.at[part, pl.ds(index * size, size)],
                outs[3 + part * chunks + index].at[pl.ds(start // chunks, size)],
                sems.at[sem + part * chunks + index],
            )
            for index in range(chunks)
        ]

    if last_row:
        for part in range(4):
            puts += ship(grad_half, part, width, 14 + chunks)
    if not last_row:
        puts.append(start_copy(grad_half, outs[1], sems.at[14]))
    settle(place, *waits_left)

    settle(place, *waits_right, *([] if first_row else [old_first]))

    def turn_step(side, carry):
        flipped = left[:, columns(side, width)].T
        turned[side, pl.ds(0, width)] = flipped
        turned[side, pl.ds(width, width)] = flipped
        return carry

    lax.fori_loop(0, 2, turn_step, 0)
    value = dot_nn(turned[0, tall], right[:, : 3 * width])
    for part in range(3):
        total(grad_first, part, value[:, part * width : (part + 1) * width])
    total(grad_first, 3, dot_nn(turned[1, tall], right[:, 3 * width :]))
    if last_row:
        for part in range(4):
            puts += ship(grad_first, part, 0, 14 + chunks + 4 * max(chunks, 1))
    if not last_row:
        puts.append(start_copy(grad_first, outs[0], sems.at[15]))
    for put in puts:
        put.wait()


def weight_call(place, token, early_row, late_row, before, last_row, members):
    rows, half = early_row[2].shape
    hidden = 2 * half
    width = (early_row[0].shape[1] - hidden) // 3
    quarter = half // 4
    low = lambda *shape: jax.ShapeDtypeStruct(shape, BF16)
    tall, short = aligned_chunk(width, quarter, members)
    sums = jax.ShapeDtypeStruct((8, width), F32)
    outs = [pltpu.HBM((4, width, width), BF16), pltpu.HBM((4, quarter, width), BF16), sums]
    if last_row:
        outs = [
            pltpu.HBM((members, width // members, hidden), F32),
            pltpu.HBM((4, members, quarter // members, width), F32),
            sums,
        ]
        outs += [low(tall + short + 16, width)] * members + [low(tall + short, width)] * (3 * members) if tall else [low(width + quarter, width)] * 4
    v = pltpu.VMEM
    return pl.pallas_call(
        partial(weight_kernel, before is None, last_row, tall, short),
        out_shape=outs,
        in_specs=[SMEM, VMEM] + [ANY] * (10 if before is None else 13),
        out_specs=[ANY] * len(outs),
        scratch_shapes=[
            v((2 * rows, 2 * width), BF16), v((2 * rows, hidden), BF16), v((2 * rows, half), BF16),
            v((2 * rows, width), BF16), v((2, 2 * width, 2 * rows), BF16), v((4, 2 * quarter, 2 * rows), BF16),
            v((4, width, width), BF16), v((4, quarter, width), BF16),
            v((16, width), F32), v((16, width), BF16), v((8, width), F32), v((16, width), BF16),
            pltpu.SemaphoreType.DMA((24 + 9 * members,)),
        ],
        compiler_params=pltpu.CompilerParams(vmem_limit_bytes=(60 if last_row else 34) * MIB),
        cost_estimate=pl.CostEstimate(flops=8_000_000_000, bytes_accessed=24_000_000, transcendentals=0),
        name="weight_gradients",
    )(place, token, *pin_own(early_row), *pin_own(late_row), *in_hbm(before or ()))


def aligned_chunk(width, quarter, members):
    tall, short = width // members, quarter // members
    return (tall, short) if tall % 16 == 0 and short % 16 == 0 else (0, 0)


def ring_order(members):
    return list(range(0, members, 2)) + list(range(members - 1, 0, -2))


def ring_reduce(own, matrix, half, position, axis, pending):
    members = lax.axis_size(axis)
    order = ring_order(members)
    ahead = [(order[i], order[(i + 1) % members]) for i in range(members)]
    behind = [(b, a) for a, b in ahead]
    parts = len(own)
    tall, width = matrix.shape[1], half.shape[3]
    short = half.shape[2]
    steps = [1 - 2 * (part % 2) for part in range(parts)]

    def piece(array, index):
        cut = lambda start, size: lax.dynamic_slice_in_dim(array, start, size, 0)
        if isinstance(index, int):
            cut = lambda start, size: lax.slice_in_dim(array, start, start + size, axis=0)
        return jnp.concatenate([cut(index * tall, tall), cut(width + index * short, short)], 0).astype(F32)

    def chunk(part, number):
        index = (members - steps[part] * number) % members
        return own[part][index].astype(F32) if isinstance(own[part], (list, tuple)) else piece(own[part], index)

    def shift(part, value):
        return lax.ppermute(value, axis, ahead if part % 2 == 0 else behind)

    def reduce_step(number, current):
        moved = [shift(part, current[part]) for part in range(parts)]
        return [(moved[part].astype(F32) + chunk(part, number)).astype(BF16) for part in range(parts)]

    def place_chunks(number, current, matrix, half):
        for part in range(parts):
            index = lax.rem(position + jnp.uint32(members) + jnp.uint32(steps[part] % members) * (
                jnp.uint32(members + 1) - jnp.uint32(number)), jnp.uint32(members))
            wide = current[part].astype(F32)
            zero, block = jnp.uint32(0), jnp.uint32(part)
            matrix = lax.dynamic_update_slice(matrix, wide[None, :tall], (index, zero, jnp.uint32(part * width)))
            half = lax.dynamic_update_slice(half, wide[None, None, tall:], (block, index, zero, zero))
        return matrix, half

    def gather_step(number, carry):
        current, matrix, half = carry
        current = [shift(part, current[part]) for part in range(parts)]
        return (current, *place_chunks(number, current, matrix, half))

    current = [chunk(part, 0).astype(BF16) for part in range(parts)]
    extra = current[0]
    if members > 8:
        current = lax.fori_loop(1, members, reduce_step, current)
        carry = lax.fori_loop(1, members, gather_step, (current, *place_chunks(0, current, matrix, half)))
    else:
        for number in range(1, members):
            current = reduce_step(number, current)
        extra = current[0][tall + short :]
        current[0] = current[0][: tall + short]
        carry = (current, *place_chunks(0, current, matrix, half))
        for number in range(1, members):
            carry = gather_step(number, carry)
            if number in (1, 3):
                which = number // 2
                pending[which] = lax.optimization_barrier((pending[which], carry[0][0]))[0]
    return carry[1].reshape(tall * members, parts * width), carry[2].reshape(parts * short * members, width), extra, pending


def turn_rows(array, width, position, members):
    top = jnp.roll(array[:width], -position * (width // members), 0)
    return jnp.concatenate([top, jnp.roll(array[width:], -position * ((array.shape[0] - width) // members), 0)], 0)


def shards(
    patches, cotangent, mask_flags, segments, mask_token, norm_gains, norm_shifts, w_first, first_bias, down_half
):
    section = lax.axis_index("section")
    core = section & 1
    stage = section >> 1
    early = stage == 0
    swap = [(0, 1), (1, 0), (2, 3), (3, 2)]
    forth = [(0, 2), (1, 3)]
    back = [(2, 0), (3, 1)]
    row_count, rows, width = patches.shape
    count = row_count // 2
    members = lax.axis_size("dp")
    place_of = np.zeros(members, np.int32)
    for spot, member in enumerate(ring_order(members)):
        place_of[member] = spot
    position = jnp.asarray(place_of)[lax.axis_index("dp").astype(jnp.uint32)]

    first_own, half_own = w_first[0], down_half[0]
    hidden = first_own.shape[1]
    quarter = hidden // 8
    tall, short = width // members, quarter // members
    aligned = aligned_chunk(width, quarter, members)[0] > 0
    first_other = lax.ppermute(first_own, "section", swap)
    half_other = lax.ppermute(half_own, "section", swap)
    own_vecs = (norm_gains, norm_shifts, first_bias)
    vecs = own_vecs + tuple(lax.ppermute(array, "section", swap) for array in own_vecs)
    weights = (first_own, first_other, half_own, half_other)
    turns = position if aligned else 0 * position
    place = jnp.stack([core, stage, turns, jnp.int32(16 * (tall // 16)), jnp.int32(16 * (short // 16))]).astype(jnp.int32)
    token = mask_token[None]

    forwards, acts, packs = [], [], []
    sent = patches[0]
    for slot in range(count + 1):
        result = forward_call(slot, place, patches, sent, mask_flags, segments, token, vecs, weights)
        forwards.append(result)
        if slot < count:
            sent = lax.ppermute(result[2], "section", forth)
        acts.append(lax.ppermute(result[9], "section", swap))
        if slot == 0:
            weights = hold_call(place, lax.optimization_barrier((weights, result[2]))[0])

    def assemble(pairs):
        chosen = [jnp.where(early, a, b) for a, b in pairs]
        keep, send = jnp.stack(chosen[0::2]), jnp.stack(chosen[1::2])
        received = lax.ppermute(send, "section", swap)
        return jnp.where(
            core == 0, jnp.concatenate([keep, received], 0), jnp.concatenate([received, keep], 0)
        )

    backs = []
    returned = patches[0]
    grads = None
    for slot in range(count + 1):
        saved = [
            [forwards[which][i] for i in (3, 4, 5, 6, 7, 10)] for which in (max(slot - 1, 0), min(slot + 1, count))
        ]
        backs.append(backward_call(slot, place, cotangent, returned, mask_flags, vecs, weights, *saved))
        if slot < count:
            returned = lax.ppermute(backs[slot][2], "section", back)
            if slot == 0:
                returned, acts[:2] = lax.optimization_barrier((returned, acts[:2]))
        packs.append(lax.ppermute(backs[slot][5], "section", swap))
        if slot > 0:
            row = slot - 1
            chosen = [
                (backs[b][4], packs[b], forwards[f][8], acts[f], backs[b][3]) for f, b in ((row, row + 1), (row + 1, row))
            ]
            total = sum(backs[b][3][6:7] for b in range(1, slot + 1))
            if row == count - 1:
                cross = [(0, 3), (1, 2)]
                total = lax.ppermute(total, "section", forth) + lax.ppermute(total, "section", cross)
            grads = weight_call(place, total, *chosen, grads, row == count - 1, members)
            if row < count - 1:
                returned, grads, acts = lax.optimization_barrier((returned, grads, acts))

    blank, small = grads[:2], grads[2]
    if aligned:
        own = [grads[3 + part * members : 3 + (part + 1) * members] for part in range(4)]
    else:
        own = [turn_rows(array, width, position, members) for array in grads[3:]]
        small = lax.psum(small, "dp")

    pending = [
        [(forwards[row][i], forwards[row + 1][i]) for row in range(count) for i in (0, 1)],
        [(backs[row + 1][i], backs[row][i]) for row in range(count) for i in (0, 1)],
    ]
    grad_first, grad_half, extra, pending = ring_reduce(own, *blank, position.astype(jnp.uint32), "dp", pending)
    if aligned:
        small = extra[:8].astype(F32)
    token_grad = small[6]

    finals = assemble(pending[0])
    back_rows = assemble(pending[1]).astype(F32)
    back_rows = jnp.where((section == 0) & (mask_flags[..., None] == 1), 0.0, back_rows)
    return (
        finals[None],
        back_rows[None],
        token_grad,
        small[0:1],
        small[1:2],
        grad_first[None],
        small[2:6].reshape(1, hidden),
        grad_half[None],
    )


def solution(mesh):
    return jax.shard_map(
        shards,
        mesh=mesh,
        in_specs=(
            P("dp", None, None),
            P("dp", None, None),
            P("dp", None),
            P("dp", None),
            P(),
            P("section", None),
            P("section", None),
            P("section", None, None),
            P("section", None),
            P("section", None, None),
        ),
        out_specs=(
            P("section", "dp", None, None),
            P("section", "dp", None, None),
            P(),
            P("section", None),
            P("section", None),
            P("section", None, None),
            P("section", None),
            P("section", None, None),
        ),
        check_vma=False,
    )
```

```python
from functools import partial

import jax
import jax.numpy as jnp
import numpy as np
from jax import lax
from jax.experimental import pallas as pl
from jax.experimental.pallas import tpu as pltpu
from jax.sharding import PartitionSpec as P

HEADS = 12
EPSILON = 1e-06
NEGATIVE = -1000000000.0
GROUP = 256
TILE = 768
MIB = 1024 * 1024
VMEM_LIMIT = 49 * MIB
BF16 = jnp.bfloat16
F32 = jnp.float32
ANY = pl.BlockSpec(memory_space=pl.ANY)
SMEM = pl.BlockSpec(memory_space=pltpu.SMEM)
VMEM = pl.BlockSpec(memory_space=pltpu.VMEM)


def dot_nn(a, b):
    return jnp.dot(a, b, preferred_element_type=F32)


def dot_nt(a, b):
    return lax.dot_general(a, b, (((1,), (1,)), ((), ())), preferred_element_type=F32)


def dot_tn(a, b):
    return lax.dot_general(a, b, (((0,), (0,)), ((), ())), preferred_element_type=F32)


def fetch(choice, first, second, target, sem):
    @pl.when(choice)
    def _():
        pltpu.make_async_copy(first, target, sem).start()

    @pl.when(jnp.logical_not(choice))
    def _():
        pltpu.make_async_copy(second, target, sem).start()

    return pltpu.make_async_copy(first, target, sem)


def deliver(choice, source, first, second, sem):
    @pl.when(choice)
    def _():
        pltpu.make_async_copy(source, first, sem).start()

    @pl.when(jnp.logical_not(choice))
    def _():
        pltpu.make_async_copy(source, second, sem).start()

    return pltpu.make_async_copy(source, first, sem)


def start_copy(source, target, sem):
    copy = pltpu.make_async_copy(source, target, sem)
    copy.start()
    return copy


def settle(place, *copies):
    @pl.when(place[0] >= 0)
    def _():
        for copy in copies:
            copy.wait()


def norm_parts(x):
    centred = x - jnp.mean(x, -1, keepdims=True)
    scale = lax.rsqrt(jnp.mean(centred * centred, -1, keepdims=True) + EPSILON)
    return centred * scale, scale


def gelu_pair(hidden):
    base = 1.0 + 0.23164189 * jnp.abs(hidden)
    t = pl.reciprocal(base, approx=True)
    t = t * (2.0 - base * t)
    poly = ((((0.5307027145 * t - 0.7265760135) * t + 0.7107068705) * t - 0.142248368) * t + 0.127414796) * t
    fall = jnp.exp2(hidden * hidden * -0.7213475204444817)
    tail = poly * fall
    cdf = jnp.where(hidden >= 0, 1.0 - tail, tail)
    return hidden * cdf, cdf + hidden * fall * 0.3989422804014327


def columns(index, width):
    return pl.ds(pl.multiple_of(index * width, width), width)


def head_mask(rows, head):
    lane = lax.broadcasted_iota(jnp.int32, (rows, GROUP), 1)
    return (lane >= head * 64) & (lane < head * 64 + 64)


def load_down(core_even, half_own, half_other, w_down, sems):
    half = half_own.shape[0]
    low = fetch(core_even, half_own, half_other, w_down.at[pl.ds(0, half)], sems.at[2])
    high = fetch(core_even, half_other, half_own, w_down.at[pl.ds(half, half)], sems.at[3])
    return low, high


def vectors(core_even, refs):
    own, other = refs[:3], refs[3:]
    att = [jnp.where(core_even, a[...].astype(F32), b[...].astype(F32)) for a, b in zip(own, other)]
    mlp = [jnp.where(core_even, b[...].astype(F32), a[...].astype(F32)) for a, b in zip(own, other)]
    return att, mlp


def upright(row, width):
    return jnp.broadcast_to(row.astype(F32), (width, row.shape[1])).T[:, :1]


def in_hbm(arrays):
    return [pltpu.with_memory_space_constraint(array, pltpu.HBM) for array in arrays]


def pin_own(arrays):
    mine, theirs, act, act_theirs, small = arrays
    return [*in_hbm([mine]), theirs, *in_hbm([act, act_theirs]), small]


def row_number(place, slot, count, backward):
    late = place[1]
    number = slot - (1 - late) if backward else slot - late
    return place[0] * count + jnp.clip(number, 0, count - 1)


def forward_kernel(
    slot, count, held, place, patches, sent_row, flags, segments, token, *refs
):
    vecs, refs = refs[:6], refs[6:]
    if held:
        (w_att, w_up, w_down), refs = refs[:3], refs[3:]
    else:
        (first_own, first_other, half_own, half_other), refs = refs[:4], refs[4:]
    (keep_out, send_out, y_mlp_out, x_out, mid_out, qkv_out, soft_out, ctx_out, act_keep_out, act_send_out,
     slope_out, x, bias, normed, qkv, soft, ctx, mid, act, slope, y_mlp, sems) = refs[:22]
    if not held:
        w_att, w_up, w_down = refs[22:]
    core_even = place[0] == 0
    early = place[1] == 0
    rows, width = x.shape
    groups = width // GROUP
    row = row_number(place, slot, count, False)
    get_x = fetch(early, patches.at[row], sent_row, x, sems.at[4])
    if not held:
        get_att = fetch(core_even, first_own, first_other, w_att, sems.at[0])
    (att_gain, att_shift, att_bias), (mlp_gain, mlp_shift, mlp_bias) = vectors(core_even, vecs)
    seg = segments[pl.ds(row, 1)]
    bias[...] = jnp.where(upright(seg, 128) == seg.astype(F32), 0.0, NEGATIVE)
    settle(place, get_x)

    @pl.when(early)
    def _():
        flag = upright(flags[pl.ds(row, 1)], 128)
        x[...] = jnp.where(flag == 1.0, token[...].astype(F32), x[...].astype(F32)).astype(BF16)

    puts = [start_copy(x, x_out, sems.at[5])]
    hat, _ = norm_parts(x[...].astype(F32))
    normed[...] = (hat * att_gain + att_shift).astype(BF16)
    if not held:
        settle(place, get_att)
        get_up = fetch(core_even, first_other, first_own, w_up, sems.at[1])
        get_low, get_high = load_down(core_even, half_own, half_other, w_down, sems)
    projected = dot_nn(normed[...], w_att[:, : 3 * width])
    q_low = (projected[:, :width] + att_bias[:, :width]).astype(BF16)
    qkv[:, :width] = (q_low * 0.125).astype(BF16)
    qkv[:, width : 2 * width] = projected[:, width : 2 * width].astype(BF16)
    qkv[:, 2 * width :] = (projected[:, 2 * width :] + att_bias[:, width : 2 * width]).astype(BF16)
    puts.append(start_copy(qkv, qkv_out, sems.at[6]))
    heads = GROUP // 64
    for group in range(groups):
        cols = pl.ds(group * GROUP, GROUP)
        q = qkv[:, cols]
        k = qkv[:, pl.ds(width + group * GROUP, GROUP)]
        v = qkv[:, pl.ds(2 * width + group * GROUP, GROUP)]
        masks = [head_mask(rows, head) for head in range(heads)]
        scores = dot_nt(jnp.concatenate([jnp.where(mask, q, 0) for mask in masks], 0), k)
        total = jnp.zeros((rows, GROUP), F32)
        for head in range(heads):
            mine = scores[head * rows : (head + 1) * rows] + bias[...]
            raised = jnp.exp(mine - jnp.max(mine, -1, keepdims=True))
            weight = (raised * (1.0 / jnp.sum(raised, -1, keepdims=True))).astype(BF16)
            soft[group * heads + head] = weight
            total = total + dot_nn(weight, jnp.where(masks[head], v, 0))
        ctx[:, cols] = total.astype(BF16)
        span = pl.ds(group * heads, heads)
        puts.append(start_copy(soft.at[span], soft_out.at[span], sems.at[17 + group]))
    puts.append(start_copy(ctx, ctx_out, sems.at[8]))
    y = x[...].astype(F32) + dot_nn(ctx[...], w_att[:, 3 * width :]) + att_bias[:, 2 * width : 3 * width]
    low = y.astype(BF16)
    mid[...] = low
    puts.append(start_copy(mid, mid_out, sems.at[9]))
    puts.append(deliver(core_even, mid, keep_out, send_out, sems.at[10]))
    hat, _ = norm_parts(low.astype(F32))
    normed[...] = (hat * mlp_gain + mlp_shift).astype(BF16)
    if not held:
        settle(place, get_up)
    half = act.shape[1] // 2
    for side in range(2):
        cols = pl.ds(side * half, half)
        hidden = dot_nn(normed[...], w_up[:, cols]) + mlp_bias[:, side * half : (side + 1) * half]
        active, rate = gelu_pair(hidden)
        act[:, cols] = active.astype(BF16)
        slope[:, cols] = rate.astype(BF16)
        targets = (act_send_out, act_keep_out) if side else (act_keep_out, act_send_out)
        puts.append(deliver(core_even, act.at[:, cols], *targets, sems.at[11 + side]))
        puts.append(start_copy(slope.at[:, cols], slope_out.at[:, cols], sems.at[13 + side]))
    if not held:
        settle(place, get_low, get_high)
    y = mid[...].astype(F32) + dot_nn(act[...], w_down[...]) + att_bias[:, 3 * width :]
    y_mlp[...] = y.astype(BF16)
    puts.append(start_copy(y_mlp, y_mlp_out, sems.at[15]))
    puts.append(deliver(core_even, y_mlp, send_out, keep_out, sems.at[16]))
    for put in puts:
        put.wait()


def hold_kernel(place, first_own, first_other, half_own, half_other, w_att, w_up, w_down, sems):
    core_even = place[0] == 0
    copies = [
        fetch(core_even, first_own, first_other, w_att, sems.at[0]),
        fetch(core_even, first_other, first_own, w_up, sems.at[1]),
        *load_down(core_even, half_own, half_other, w_down, sems),
    ]
    for copy in copies:
        copy.wait()


def hold_call(place, weights):
    width, hidden = weights[0].shape
    v = pltpu.VMEM
    return pl.pallas_call(
        hold_kernel,
        out_shape=[v((width, hidden), BF16), v((width, hidden), BF16), v((hidden, width), BF16)],
        in_specs=[SMEM] + [ANY] * 4,
        out_specs=[VMEM] * 3,
        scratch_shapes=[pltpu.SemaphoreType.DMA((4,))],
        compiler_params=pltpu.CompilerParams(vmem_limit_bytes=VMEM_LIMIT),
        cost_estimate=pl.CostEstimate(flops=0, bytes_accessed=14_000_000, transcendentals=0),
        name="hold_weights",
    )(place, *weights)


def forward_call(slot, place, patches, sent_row, flags, segments, token, vecs, weights):
    rows, width = sent_row.shape
    held = len(weights) == 3
    if held:
        weights = [pltpu.with_memory_space_constraint(array, pltpu.VMEM) for array in weights]
    hidden = weights[0].shape[1]
    low = lambda *shape: jax.ShapeDtypeStruct(shape, BF16)
    row = low(rows, width)
    outs = [row, row, row, row, row, low(rows, 3 * width), low(HEADS, rows, rows), row]
    outs += [low(rows, hidden // 2), low(rows, hidden // 2), low(rows, hidden)]
    v = pltpu.VMEM
    return pl.pallas_call(
        partial(forward_kernel, slot, patches.shape[0] // 2, held),
        out_shape=outs,
        in_specs=[SMEM, ANY, ANY] + [VMEM] * 9 + ([VMEM] * 3 if held else [ANY] * 4),
        out_specs=[ANY] * len(outs),
        scratch_shapes=[
            v((rows, width), BF16), v((rows, rows), F32), v((rows, width), BF16),
            v((rows, 3 * width), BF16), v((HEADS, rows, rows), BF16), v((rows, width), BF16), v((rows, width), BF16),
            v((rows, hidden), BF16), v((rows, hidden), BF16), v((rows, width), BF16),
            pltpu.SemaphoreType.DMA((20,)),
        ]
        + ([] if held else [v((width, hidden), BF16), v((width, hidden), BF16), v((hidden, width), BF16)]),
        compiler_params=pltpu.CompilerParams(vmem_limit_bytes=VMEM_LIMIT if held else 60 * MIB),
        cost_estimate=pl.CostEstimate(flops=7_000_000_000, bytes_accessed=26_000_000, transcendentals=2_500_000),
        name="row_forward",
    )(place, patches, sent_row, flags, segments, token, *vecs, *weights)


def backward_kernel(slot, count, place, cotangent, back_row, flags, *refs):
    vecs = refs[:6]
    (w_att, w_up, w_down,
     x_a, mid_a, qkv_a, soft_a, ctx_a, slope_a, x_b, mid_b, qkv_b, soft_b, ctx_b, slope_b,
     keep_out, send_out, grad_x_out, small_out, pack_keep, pack_send,
     grad_y, x, mid, qkv, soft, ctx, slope, normed_att, normed_mlp, dqkv, dhid, gmid, gx,
     dctx_all, ds_all, soft_all, small_low, sems) = refs[6:]
    core_even = place[0] == 0
    early = place[1] == 0
    rows, width = x.shape
    groups = width // GROUP
    row = row_number(place, slot, count, True)
    busy = jnp.logical_and(early, slot >= 1) | jnp.logical_and(jnp.logical_not(early), slot < count)
    small_out[...] = jnp.zeros(small_out.shape, F32)

    @pl.when(busy)
    def _():
        get_g = fetch(early, back_row, cotangent.at[row], grad_y, sems.at[4])
        get_slope = fetch(early, slope_a, slope_b, slope, sems.at[5])
        (att_gain, att_shift, _), (mlp_gain, mlp_shift, _) = vectors(core_even, vecs)
        settle(place, get_g)

        def pack(source, start, to_even, sem):
            spot = (pl.ds(0, rows), pl.ds(start, source.shape[1]))
            if to_even:
                return deliver(core_even, source, pack_keep.at[spot], pack_send.at[spot], sem)
            return deliver(core_even, source, pack_send.at[spot], pack_keep.at[spot], sem)

        hidden = dhid.shape[1]
        last = 2 * width + hidden
        puts = [
            start_copy(grad_y, pack_keep.at[pl.ds(0, rows), pl.ds(last, width)], sems.at[11]),
            start_copy(grad_y, pack_send.at[pl.ds(0, rows), pl.ds(last, width)], sems.at[20]),
        ]
        small_out[5:6] = jnp.sum(grad_y[...].astype(F32), 0, keepdims=True)
        settle(place, get_slope)
        get_mid = fetch(early, mid_a, mid_b, mid, sems.at[6])
        get_soft = fetch(early, soft_a, soft_b, soft, sems.at[9])
        get_qkv = fetch(early, qkv_a, qkv_b, qkv, sems.at[8])
        get_ctx = fetch(early, ctx_a, ctx_b, ctx, sems.at[10])
        get_x = fetch(early, x_a, x_b, x, sems.at[7])
        half = hidden // 2
        for side in range(2):
            cols = pl.ds(side * half, half)
            low = (dot_nt(grad_y[...], w_down[cols, :]) * slope[:, cols].astype(F32)).astype(BF16)
            dhid[:, cols] = low
            sums = jnp.sum(low.astype(F32), 0, keepdims=True)
            for part in range(half // width):
                number = 10 + side * (half // width) + part
                small_out[number : number + 1] = sums[:, part * width : (part + 1) * width]
        puts.append(pack(dhid, 2 * width, False, sems.at[12]))
        settle(place, get_mid)
        dnorm = dot_nt(dhid[...], w_up[...])
        hat, scale = norm_parts(mid[...].astype(F32))
        normed_mlp[...] = (hat * mlp_gain + mlp_shift).astype(BF16)
        puts.append(pack(normed_mlp, 0, False, sems.at[13]))
        puts.append(pack(normed_mlp, width, False, sems.at[21]))
        small_out[8:9] = jnp.sum(dnorm * hat, 0, keepdims=True)
        small_out[9:10] = jnp.sum(dnorm, 0, keepdims=True)
        u = dnorm * mlp_gain
        grad = grad_y[...].astype(F32) + scale * (
            u - jnp.mean(u, -1, keepdims=True) - hat * jnp.mean(u * hat, -1, keepdims=True)
        )
        low = grad.astype(BF16)
        gmid[...] = low
        puts.append(pack(gmid, 2 * width + 3 * width, True, sems.at[14]))
        puts.append(deliver(core_even, gmid, send_out, keep_out, sems.at[15]))
        small_out[4:5] = jnp.sum(low.astype(F32), 0, keepdims=True)
        settle(place, get_qkv, get_soft, get_ctx)
        puts.append(pack(ctx, width, True, sems.at[22]))
        dctx_all[...] = dot_nt(gmid[...], w_att[:, 3 * width :]).astype(BF16)
        heads = GROUP // 64

        def group_step(group, carry):
            cols = columns(group, GROUP)
            k_cols = pl.ds(pl.multiple_of(width + group * GROUP, GROUP), GROUP)
            v_cols = pl.ds(pl.multiple_of(2 * width + group * GROUP, GROUP), GROUP)
            dctx = dctx_all[:, cols]
            q = qkv[:, cols]
            k = qkv[:, k_cols]
            v = qkv[:, v_cols]
            product = dctx.astype(F32) * ctx[:, cols].astype(F32)
            masks = [head_mask(rows, head) for head in range(heads)]
            mine = jnp.concatenate([jnp.where(mask, dctx, 0) for mask in masks], 0)
            dp = dot_nt(mine, v)
            dq = jnp.zeros((rows, GROUP), F32)
            for head in range(heads):
                span = pl.ds(head * rows, rows)
                weight = soft[group * heads + head]
                delta = jnp.sum(jnp.where(masks[head], product, 0.0), -1, keepdims=True)
                ds = (weight.astype(F32) * (dp[head * rows : (head + 1) * rows] - delta)).astype(BF16)
                ds_all[span] = ds
                soft_all[span] = weight
                dq = dq + dot_nn(ds, jnp.where(masks[head], k, 0))
            dk = dot_tn(ds_all[...], jnp.concatenate([jnp.where(mask, q, 0) for mask in masks], 0))
            dv = dot_tn(soft_all[...], mine)
            dq_low = (dq * 0.125).astype(BF16)
            dv_low = dv.astype(BF16)
            dqkv[:, cols] = dq_low
            dqkv[:, k_cols] = dk.astype(BF16)
            dqkv[:, v_cols] = dv_low
            small_out[2:3, cols] = jnp.sum(dq_low.astype(F32), 0, keepdims=True)
            small_out[3:4, cols] = jnp.sum(dv_low.astype(F32), 0, keepdims=True)
            return carry

        lax.fori_loop(0, groups, group_step, 0)
        puts.append(pack(dqkv, 2 * width, True, sems.at[16]))
        settle(place, get_x)
        dnorm = dot_nt(dqkv[...], w_att[:, : 3 * width])
        hat, scale = norm_parts(x[...].astype(F32))
        normed_att[...] = (hat * att_gain + att_shift).astype(BF16)
        puts.append(pack(normed_att, 0, True, sems.at[17]))
        small_out[0:1] = jnp.sum(dnorm * hat, 0, keepdims=True)
        small_out[1:2] = jnp.sum(dnorm, 0, keepdims=True)
        u = dnorm * att_gain
        grad = gmid[...].astype(F32) + scale * (
            u - jnp.mean(u, -1, keepdims=True) - hat * jnp.mean(u * hat, -1, keepdims=True)
        )
        gx[...] = grad.astype(BF16)
        puts.append(start_copy(gx, grad_x_out, sems.at[18]))
        puts.append(deliver(core_even, gx, keep_out, send_out, sems.at[19]))
        token = jnp.sum(jnp.where(upright(flags[pl.ds(row, 1)], 128) == 1.0, grad, 0.0), 0, keepdims=True)
        small_out[6:7] = token
        small_out[14:15] = token
        theirs = jnp.where(core_even, small_out[8:16], small_out[0:8])
        high = theirs.astype(BF16)
        small_low[...] = jnp.concatenate([high, (theirs - high.astype(F32)).astype(BF16)], 0)
        puts.append(start_copy(small_low, pack_send.at[pl.ds(rows, 16), pl.ds(0, width)], sems.at[23]))
        for put in puts:
            put.wait()


def backward_call(slot, place, cotangent, back_row, flags, vecs, weights, saved_early, saved_late):
    rows, width = back_row.shape
    hidden = weights[0].shape[1]
    low = lambda *shape: jax.ShapeDtypeStruct(shape, BF16)
    row = low(rows, width)
    pack = low(rows + 16, 3 * width + hidden)
    weights = [pltpu.with_memory_space_constraint(array, pltpu.VMEM) for array in weights]
    outs = [row, row, row, jax.ShapeDtypeStruct((16, width), F32), pack, pack]
    specs = [ANY] * len(outs)
    specs[3] = VMEM
    v = pltpu.VMEM
    return pl.pallas_call(
        partial(backward_kernel, slot, cotangent.shape[0] // 2),
        out_shape=outs,
        in_specs=[SMEM, ANY, ANY] + [VMEM] * 10 + [ANY] * 12,
        out_specs=specs,
        scratch_shapes=[
            v((rows, width), BF16), v((rows, width), BF16), v((rows, width), BF16),
            v((rows, 3 * width), BF16), v((HEADS, rows, rows), BF16), v((rows, width), BF16), v((rows, hidden), BF16),
            v((rows, width), BF16), v((rows, width), BF16), v((rows, 3 * width), BF16), v((rows, hidden), BF16),
            v((rows, width), BF16), v((rows, width), BF16), v((rows, width), BF16),
            v((GROUP // 64 * rows, rows), BF16), v((GROUP // 64 * rows, rows), BF16),
            v((16, width), BF16), pltpu.SemaphoreType.DMA((24,)),
        ],
        compiler_params=pltpu.CompilerParams(vmem_limit_bytes=VMEM_LIMIT),
        cost_estimate=pl.CostEstimate(flops=8_000_000_000, bytes_accessed=34_000_000, transcendentals=1_000),
        name="row_backward",
    )(place, cotangent, back_row, flags, *vecs, *weights, *in_hbm(saved_early), *in_hbm(saved_late))


def weight_kernel(first_row, last_row, tall_rows, short_rows, place, token, *refs):
    sources, refs = refs[:10], refs[10:]
    if not first_row:
        before, refs = refs[:3], refs[3:]
    made = len(refs) - 13
    outs, refs = refs[:made], refs[made:]
    (left, right, act, grad_y, turned, part_t, grad_first, grad_half, mine, theirs, summed, small_low, sems) = refs
    early = place[1] == 0
    rows = left.shape[0] // 2
    hidden = right.shape[1]
    width = grad_y.shape[1]
    quarter = grad_half.shape[1]
    tall = pl.ds(pl.multiple_of(place[2] * place[3], 16), width)
    short = pl.ds(pl.multiple_of(place[2] * place[4], 16), quarter)
    core_even = place[0] == 0
    get_mine = fetch(early, sources[4], sources[9], mine, sems.at[10])
    spot = (pl.ds(rows, 16), pl.ds(0, width))
    get_theirs = fetch(early, sources[1].at[spot], sources[6].at[spot], theirs, sems.at[11])
    if not first_row:
        old_small = start_copy(before[2], summed, sems.at[12])
    waits = []
    for index, (first, second) in enumerate(zip(sources[2:4], sources[7:9])):
        waits.append(fetch(early, first, second, act.at[pl.ds(index * rows, rows)], sems.at[index]))
    start = 0
    pieces = []
    for number, target in enumerate((left, right, grad_y)):
        span = pl.ds(start, target.shape[1])
        start += target.shape[1]
        pieces.append([(first.at[pl.ds(0, rows), span], second.at[pl.ds(0, rows), span], target.at[pl.ds(index * rows, rows)], sems.at[2 + 2 * number + index])
                       for index, (first, second) in enumerate(zip(sources[:2], sources[5:7]))])
    waits += [fetch(early, *piece) for piece in pieces[2]]
    if not first_row:
        old_half = start_copy(before[1], grad_half, sems.at[8])
    waits_left = [fetch(early, *piece) for piece in pieces[0]]
    waits_right = [fetch(early, *piece) for piece in pieces[1]]
    if not first_row:
        old_first = start_copy(before[0], grad_first, sems.at[9])
    puts = []
    settle(place, get_mine, get_theirs, *([] if first_row else [old_small]))
    ours = jnp.where(core_even, mine[0:8], mine[8:16]) + theirs[0:8].astype(F32) + theirs[8:16].astype(F32)
    summed[...] = ours if first_row else ours + summed[...]
    if last_row:
        lines = lax.broadcasted_iota(jnp.int32, summed.shape, 0)
        summed[...] = jnp.where((lines == 6) & jnp.logical_not(early), token[...], summed[...])
        small_low[...] = jnp.concatenate([summed[...], jnp.zeros(summed.shape, F32)], 0).astype(BF16)
        if tall_rows:
            for index in range(width // tall_rows):
                target = outs[3 + index].at[pl.ds(tall_rows + short_rows, 16)]
                puts.append(start_copy(small_low, target, sems.at[14 + index]))
    puts.append(start_copy(summed, outs[2], sems.at[13]))

    def total(target, index, value):
        if not first_row:
            value = value + target[index].astype(F32)
        target[index] = value.astype(BF16)

    settle(place, *waits, *([] if first_row else [old_half]))

    def half_step(part, carry):
        flipped = act[:, columns(part, quarter)].T
        part_t[part, pl.ds(0, quarter)] = flipped
        part_t[part, pl.ds(quarter, quarter)] = flipped
        return carry

    lax.fori_loop(0, 4, half_step, 0)
    value = dot_nn(jnp.concatenate([part_t[part, short] for part in range(4)], 0), grad_y[...])
    for part in range(4):
        total(grad_half, part, value[part * quarter : (part + 1) * quarter])
    chunks = width // tall_rows if tall_rows else 0

    def ship(source, part, start, sem):
        if not chunks:
            return [start_copy(source.at[part], outs[3 + part].at[pl.ds(start, source.shape[1])], sems.at[sem + part])]
        size = source.shape[1] // chunks
        return [
            start_copy(
                source.at[part, pl.ds(index * size, size)],
                outs[3 + part * chunks + index].at[pl.ds(start // chunks, size)],
                sems.at[sem + part * chunks + index],
            )
            for index in range(chunks)
        ]

    if last_row:
        for part in range(4):
            puts += ship(grad_half, part, width, 14 + chunks)
    if not last_row:
        puts.append(start_copy(grad_half, outs[1], sems.at[14]))
    settle(place, *waits_left)

    settle(place, *waits_right, *([] if first_row else [old_first]))

    def turn_step(side, carry):
        flipped = left[:, columns(side, width)].T
        turned[side, pl.ds(0, width)] = flipped
        turned[side, pl.ds(width, width)] = flipped
        return carry

    lax.fori_loop(0, 2, turn_step, 0)
    value = dot_nn(turned[0, tall], right[:, : 3 * width])
    for part in range(3):
        total(grad_first, part, value[:, part * width : (part + 1) * width])
    total(grad_first, 3, dot_nn(turned[1, tall], right[:, 3 * width :]))
    if last_row:
        for part in range(4):
            puts += ship(grad_first, part, 0, 14 + chunks + 4 * max(chunks, 1))
    if not last_row:
        puts.append(start_copy(grad_first, outs[0], sems.at[15]))
    for put in puts:
        put.wait()


def weight_call(place, token, early_row, late_row, before, last_row, members):
    rows, half = early_row[2].shape
    hidden = 2 * half
    width = (early_row[0].shape[1] - hidden) // 3
    quarter = half // 4
    low = lambda *shape: jax.ShapeDtypeStruct(shape, BF16)
    tall, short = aligned_chunk(width, quarter, members)
    sums = jax.ShapeDtypeStruct((8, width), F32)
    outs = [pltpu.HBM((4, width, width), BF16), pltpu.HBM((4, quarter, width), BF16), sums]
    if last_row:
        outs = [
            pltpu.HBM((members, width // members, hidden), F32),
            pltpu.HBM((4, members, quarter // members, width), F32),
            sums,
        ]
        outs += [low(tall + short + 16, width)] * members + [low(tall + short, width)] * (3 * members) if tall else [low(width + quarter, width)] * 4
    v = pltpu.VMEM
    return pl.pallas_call(
        partial(weight_kernel, before is None, last_row, tall, short),
        out_shape=outs,
        in_specs=[SMEM, VMEM] + [ANY] * (10 if before is None else 13),
        out_specs=[ANY] * len(outs),
        scratch_shapes=[
            v((2 * rows, 2 * width), BF16), v((2 * rows, hidden), BF16), v((2 * rows, half), BF16),
            v((2 * rows, width), BF16), v((2, 2 * width, 2 * rows), BF16), v((4, 2 * quarter, 2 * rows), BF16),
            v((4, width, width), BF16), v((4, quarter, width), BF16),
            v((16, width), F32), v((16, width), BF16), v((8, width), F32), v((16, width), BF16),
            pltpu.SemaphoreType.DMA((24 + 9 * members,)),
        ],
        compiler_params=pltpu.CompilerParams(vmem_limit_bytes=(60 if last_row else 34) * MIB),
        cost_estimate=pl.CostEstimate(flops=8_000_000_000, bytes_accessed=24_000_000, transcendentals=0),
        name="weight_gradients",
    )(place, token, *pin_own(early_row), *pin_own(late_row), *in_hbm(before or ()))


def aligned_chunk(width, quarter, members):
    tall, short = width // members, quarter // members
    return (tall, short) if tall % 16 == 0 and short % 16 == 0 else (0, 0)


def ring_order(members):
    return list(range(0, members, 2)) + list(range(members - 1, 0, -2))


def ring_reduce(own, matrix, half, position, axis, pending):
    members = lax.axis_size(axis)
    order = ring_order(members)
    ahead = [(order[i], order[(i + 1) % members]) for i in range(members)]
    behind = [(b, a) for a, b in ahead]
    parts = len(own)
    tall, width = matrix.shape[1], half.shape[3]
    short = half.shape[2]
    steps = [1 - 2 * (part % 2) for part in range(parts)]

    def piece(array, index):
        cut = lambda start, size: lax.dynamic_slice_in_dim(array, start, size, 0)
        if isinstance(index, int):
            cut = lambda start, size: lax.slice_in_dim(array, start, start + size, axis=0)
        return jnp.concatenate([cut(index * tall, tall), cut(width + index * short, short)], 0).astype(F32)

    def chunk(part, number):
        index = (members - steps[part] * number) % members
        return own[part][index].astype(F32) if isinstance(own[part], (list, tuple)) else piece(own[part], index)

    def shift(part, value):
        return lax.ppermute(value, axis, ahead if part % 2 == 0 else behind)

    def reduce_step(number, current):
        moved = [shift(part, current[part]) for part in range(parts)]
        return [(moved[part].astype(F32) + chunk(part, number)).astype(BF16) for part in range(parts)]

    def place_chunks(number, current, matrix, half):
        for part in range(parts):
            index = lax.rem(position + jnp.uint32(members) + jnp.uint32(steps[part] % members) * (
                jnp.uint32(members + 1) - jnp.uint32(number)), jnp.uint32(members))
            wide = current[part].astype(F32)
            zero, block = jnp.uint32(0), jnp.uint32(part)
            matrix = lax.dynamic_update_slice(matrix, wide[None, :tall], (index, zero, jnp.uint32(part * width)))
            half = lax.dynamic_update_slice(half, wide[None, None, tall:], (block, index, zero, zero))
        return matrix, half

    def gather_step(number, carry):
        current, matrix, half = carry
        current = [shift(part, current[part]) for part in range(parts)]
        return (current, *place_chunks(number, current, matrix, half))

    current = [chunk(part, 0).astype(BF16) for part in range(parts)]
    extra = current[0]
    if members > 8:
        current = lax.fori_loop(1, members, reduce_step, current)
        carry = lax.fori_loop(1, members, gather_step, (current, *place_chunks(0, current, matrix, half)))
    else:
        for number in range(1, members):
            current = reduce_step(number, current)
            if number in (3, 5):
                which = number // 2 - 1
                pending[which] = lax.optimization_barrier((pending[which], current[0]))[0]
        extra = current[0][tall + short :]
        current[0] = current[0][: tall + short]
        carry = (current, *place_chunks(0, current, matrix, half))
        for number in range(1, members):
            carry = gather_step(number, carry)
    return carry[1].reshape(tall * members, parts * width), carry[2].reshape(parts * short * members, width), extra, pending


def turn_rows(array, width, position, members):
    top = jnp.roll(array[:width], -position * (width // members), 0)
    return jnp.concatenate([top, jnp.roll(array[width:], -position * ((array.shape[0] - width) // members), 0)], 0)


def shards(
    patches, cotangent, mask_flags, segments, mask_token, norm_gains, norm_shifts, w_first, first_bias, down_half
):
    section = lax.axis_index("section")
    core = section & 1
    stage = section >> 1
    early = stage == 0
    swap = [(0, 1), (1, 0), (2, 3), (3, 2)]
    forth = [(0, 2), (1, 3)]
    back = [(2, 0), (3, 1)]
    row_count, rows, width = patches.shape
    count = row_count // 2
    members = lax.axis_size("dp")
    place_of = np.zeros(members, np.int32)
    for spot, member in enumerate(ring_order(members)):
        place_of[member] = spot
    position = jnp.asarray(place_of)[lax.axis_index("dp").astype(jnp.uint32)]

    first_own, half_own = w_first[0], down_half[0]
    hidden = first_own.shape[1]
    quarter = hidden // 8
    tall, short = width // members, quarter // members
    aligned = aligned_chunk(width, quarter, members)[0] > 0
    first_other = lax.ppermute(first_own, "section", swap)
    half_other = lax.ppermute(half_own, "section", swap)
    own_vecs = (norm_gains, norm_shifts, first_bias)
    vecs = own_vecs + tuple(lax.ppermute(array, "section", swap) for array in own_vecs)
    weights = (first_own, first_other, half_own, half_other)
    turns = position if aligned else 0 * position
    place = jnp.stack([core, stage, turns, jnp.int32(16 * (tall // 16)), jnp.int32(16 * (short // 16))]).astype(jnp.int32)
    token = mask_token[None]

    forwards, acts, packs = [], [], []
    sent = patches[0]
    for slot in range(count + 1):
        result = forward_call(slot, place, patches, sent, mask_flags, segments, token, vecs, weights)
        forwards.append(result)
        if slot < count:
            sent = lax.ppermute(result[2], "section", forth)
        acts.append(lax.ppermute(result[9], "section", swap))
        if slot == 0:
            weights = hold_call(place, lax.optimization_barrier((weights, result[2]))[0])

    def assemble(pairs):
        chosen = [jnp.where(early, a, b) for a, b in pairs]
        keep, send = jnp.stack(chosen[0::2]), jnp.stack(chosen[1::2])
        received = lax.ppermute(send, "section", swap)
        return jnp.where(
            core == 0, jnp.concatenate([keep, received], 0), jnp.concatenate([received, keep], 0)
        )

    backs = []
    returned = patches[0]
    grads = None
    for slot in range(count + 1):
        saved = [
            [forwards[which][i] for i in (3, 4, 5, 6, 7, 10)] for which in (max(slot - 1, 0), min(slot + 1, count))
        ]
        backs.append(backward_call(slot, place, cotangent, returned, mask_flags, vecs, weights, *saved))
        if slot < count:
            returned = lax.ppermute(backs[slot][2], "section", back)
            if slot == 0:
                returned, acts[:2] = lax.optimization_barrier((returned, acts[:2]))
        packs.append(lax.ppermute(backs[slot][5], "section", swap))
        if slot > 0:
            row = slot - 1
            chosen = [
                (backs[b][4], packs[b], forwards[f][8], acts[f], backs[b][3]) for f, b in ((row, row + 1), (row + 1, row))
            ]
            total = sum(backs[b][3][6:7] for b in range(1, slot + 1))
            if row == count - 1:
                cross = [(0, 3), (1, 2)]
                total = lax.ppermute(total, "section", forth) + lax.ppermute(total, "section", cross)
            grads = weight_call(place, total, *chosen, grads, row == count - 1, members)
            if row < count - 1:
                returned, grads, acts = lax.optimization_barrier((returned, grads, acts))

    blank, small = grads[:2], grads[2]
    if aligned:
        own = [grads[3 + part * members : 3 + (part + 1) * members] for part in range(4)]
    else:
        own = [turn_rows(array, width, position, members) for array in grads[3:]]
        small = lax.psum(small, "dp")

    pending = [
        [(forwards[row][i], forwards[row + 1][i]) for row in range(count) for i in (0, 1)],
        [(backs[row + 1][i], backs[row][i]) for row in range(count) for i in (0, 1)],
    ]
    grad_first, grad_half, extra, pending = ring_reduce(own, *blank, position.astype(jnp.uint32), "dp", pending)
    if aligned:
        small = extra[:8].astype(F32)
    token_grad = small[6]

    finals = assemble(pending[0])
    back_rows = assemble(pending[1]).astype(F32)
    back_rows = jnp.where((section == 0) & (mask_flags[..., None] == 1), 0.0, back_rows)
    return (
        finals[None],
        back_rows[None],
        token_grad,
        small[0:1],
        small[1:2],
        grad_first[None],
        small[2:6].reshape(1, hidden),
        grad_half[None],
    )


def solution(mesh):
    return jax.shard_map(
        shards,
        mesh=mesh,
        in_specs=(
            P("dp", None, None),
            P("dp", None, None),
            P("dp", None),
            P("dp", None),
            P(),
            P("section", None),
            P("section", None),
            P("section", None, None),
            P("section", None),
            P("section", None, None),
        ),
        out_specs=(
            P("section", "dp", None, None),
            P("section", "dp", None, None),
            P(),
            P("section", None),
            P("section", None),
            P("section", None, None),
            P("section", None),
            P("section", None, None),
        ),
        check_vma=False,
    )
```
